32 devices in a mesh: box: 4 (over y, x), samp: 8 (over z, core).
Axes of the slice: x: 2, y: 2, z: 4, core: 2. Of those that a mesh axis runs over, the one named last changes fastest.
Arguments:
- density: bfloat16 [512, 2, 128], P(('box', 'samp')), may hold values from -6 to 6
- radiate: bfloat16 [512, 128, 1024], P(('box', 'samp')), may hold values from -0.5 to 0.5
- receive: bfloat16 [512, 128, 1024], P(('box', 'samp')), may hold values from -0.1875 to 0.1875
- near_tiles: bfloat16 [7168, 2, 128, 128], P(('box', 'samp')), may hold values from -0.109375 to 0.109375
- near_src: int32 [512, 27], P(('box', 'samp')), may hold values from 0 to 512, as said below
- near_tile: int32 [512, 27], P(('box', 'samp')), may hold values from 0 to 7168, as said below
- send_box: int32 [32, 32, 4], P(('box', 'samp')), may hold values from 0 to 16, as said below
- distant_pattern_slot: int32 [512, 189], P(('box', 'samp')), may hold values from 0 to 128, as said below
- far_type: int32 [512, 189], P(('box', 'samp')), may hold values from 0 to 315
- trans_lo: bfloat16 [316, 2, 512], replicated, may hold values from -0.4375 to 0.4375
- interp_matrix: bfloat16 [512, 2048], replicated, may hold values from -0.25 to 0.25
- shifts: float32 [8, 2, 2048], replicated, may hold values from -2 to 2
- par_far: int32 [64, 189], P('box'), may hold values from 0 to 64, as said below
- par_type: int32 [64, 189], P('box'), may hold values from 0 to 315
- trans_hi: bfloat16 [316, 2, 2048], replicated, may hold values from -0.4375 to 0.4375
Outputs:
- field: float32 [512, 2, 128], P(('box', 'samp'))
The draws below stay inside these ranges and needn't reach their ends.
Inputs may be any that keep to these rules, and one draw needn't show every extreme that they name: `send_box`: entries equal to 16 are empty and come last in a slot row. A sender fills slots for a receiver only if it lies within 8 device numbers of it, or is 16, 8 or 4 device numbers away cyclically; for every other pair all slots are empty. One device sends 4 patterns to another in every draw, and some device receives 4 from every device that fills slots for it. `distant_pattern_slot`: the value 32 * 4 marks an empty entry; empty entries come last in a row; every other entry names a non-empty slot that its sender fills for the box's device; at least 94 entries of a row are non-empty. `near_src`: the value 512 marks an empty entry; empty entries come last in a row; a source box lies on the box's own device or on the device of index one lower or one higher. `near_tile`: empty where near_src is; every other entry names a tile of the box's own device, and the non-empty entries of one device's boxes name each of its 224 tiles once. `par_far`: the value 64 marks an empty entry; empty entries come last in a row; at least 94 entries of a row are non-empty.
All inputs are finite; a program needn't handle non-finite values.
Results may differ from the reference program's by a relative error of at most 0.0065.
Values may be sent and summed in bfloat16 or wider, within the bound.
No kernel may reach another device: no remote copies, remote signals or barrier semaphores. Data moves between devices by JAX's collectives and lax.ppermute only.
A program may use at most 128 MiB of HBM per device.

```python
import jax
import jax.numpy as jnp
from jax import lax

BOX_DEV = 16
PANELS = 128
Q_LO = 512
Q_HI = 2048
NEAR = 27
FAR = 189
TYPES = 316
SLOTS = 4
REACH = 8
NDEV = 32
NBOX = 512
NPAR = 64
TILE_DEV = 224


def jump_table():
    return jnp.array([NDEV // 2, NDEV // 4, NDEV - NDEV // 4, NDEV // 8, NDEV - NDEV // 8], jnp.int32)


def linked_pairs():
    emitter_values = jnp.arange(NDEV)[:, None]
    destination = jnp.arange(NDEV)[None, :]
    apart = (emitter_values - destination) % NDEV
    nearby = jnp.abs(emitter_values - destination) <= REACH
    jumps = jump_table()
    across = jnp.any(apart[:, :, None] == jumps[None, None, :], 2)
    return nearby | across


def slot_counts(key):
    base = jax.random.fold_in(key, 7001)
    tally_per_kind = jax.random.randint(jax.random.fold_in(base, 1), (NDEV, NDEV), 1, SLOTS + 1)
    target = jax.random.randint(jax.random.fold_in(base, 3), (), 0, NDEV)
    emitter_values = jnp.arange(NDEV)[:, None]
    destination = jnp.arange(NDEV)[None, :]
    linked = linked_pairs()
    filled = ((emitter_values - destination) % NDEV == NDEV // 2) | (destination == target)
    return jnp.where(linked, jnp.where(filled, SLOTS, tally_per_kind), 0)


def draw_send_box(key, part):
    tally_per_kind = slot_counts(key)
    chosen = jax.random.randint(jax.random.fold_in(key, 7101), (NDEV, NDEV, SLOTS), 0, BOX_DEV)
    position = jnp.arange(SLOTS)[None, None, :]
    return jnp.where(position < tally_per_kind[:, :, None], chosen, BOX_DEV).astype(jnp.int32)


def draw_distant_pattern_slot(key, part):
    tally_per_kind = slot_counts(key)
    receiver = (jnp.arange(NBOX) // BOX_DEV)[:, None]
    half_reach = REACH // 2
    step_one = jax.random.randint(jax.random.fold_in(key, 7204), (NBOX, FAR), -half_reach, half_reach + 1)
    step_two = jax.random.randint(jax.random.fold_in(key, 7205), (NBOX, FAR), -half_reach, half_reach + 1)
    local_sender = jnp.clip(receiver + step_one + step_two, 0, NDEV - 1)
    jump_index = jax.random.randint(jax.random.fold_in(key, 7206), (NBOX, FAR), 0, 5)
    far_sender = (receiver + jump_table()[jump_index]) % NDEV
    crossing = jax.random.randint(jax.random.fold_in(key, 7207), (NBOX, FAR), 0, 4) == 0
    sender = jnp.where(crossing, far_sender, local_sender)
    limits = tally_per_kind[sender, receiver]
    within = jax.random.randint(jax.random.fold_in(key, 7202), (NBOX, FAR), 0, limits)
    live_count = jax.random.randint(jax.random.fold_in(key, 7203), (NBOX, 1), FAR // 2, FAR + 1)
    column = jnp.arange(FAR)[None, :]
    return jnp.where(column < live_count, sender * SLOTS + within, NDEV * SLOTS).astype(jnp.int32)


def permuted(subkey):
    return jax.random.permutation(subkey, TILE_DEV)


def near_layout(key):
    base = jax.random.fold_in(key, 7301)
    half_count = (NEAR + 1) // 2
    spread = jax.random.randint(jax.random.fold_in(base, 1), (NDEV, BOX_DEV // 2), -(NEAR // 2), NEAR // 2 + 1)
    fullest = jax.random.randint(jax.random.fold_in(base, 2), (), 0, NDEV)
    spread = spread.at[fullest, 0].set(NEAR // 2)
    tally_per_kind = jnp.stack([half_count + spread, half_count - spread], 2).reshape(NDEV, BOX_DEV)
    starts = jnp.cumsum(tally_per_kind, 1) - tally_per_kind
    orders = jax.vmap(permuted)(jax.random.split(jax.random.fold_in(base, 3), NDEV))
    column = jnp.arange(NEAR)
    position = starts[:, :, None] + column[None, None, :]
    live = column[None, None, :] < tally_per_kind[:, :, None]
    safe_position = jnp.minimum(position, TILE_DEV - 1).reshape(NDEV, BOX_DEV * NEAR)
    picked = jnp.take_along_axis(orders, safe_position, 1).reshape(NDEV, BOX_DEV, NEAR)
    owner = jnp.arange(NDEV)[:, None, None]
    tiles = jnp.where(live, owner * TILE_DEV + picked, NDEV * TILE_DEV)
    step_side = jax.random.randint(jax.random.fold_in(base, 4), (NDEV, BOX_DEV, NEAR), -1, 2)
    neighbour = jnp.clip(owner + step_side, 0, NDEV - 1)
    local_box = jax.random.randint(jax.random.fold_in(base, 5), (NDEV, BOX_DEV, NEAR), 0, BOX_DEV)
    sources = jnp.where(live, neighbour * BOX_DEV + local_box, NBOX)
    return (sources.reshape(NBOX, NEAR).astype(jnp.int32), tiles.reshape(NBOX, NEAR).astype(jnp.int32))


def draw_near_src(key, part):
    return near_layout(key)[0]


def draw_near_tile(key, part):
    return near_layout(key)[1]


def draw_par_far(key, part):
    chosen = jax.random.randint(jax.random.fold_in(key, 7401), (NPAR, FAR), 0, NPAR)
    live_count = jax.random.randint(jax.random.fold_in(key, 7402), (NPAR, 1), FAR // 2, FAR + 1)
    column = jnp.arange(FAR)[None, :]
    return jnp.where(column < live_count, chosen, NPAR).astype(jnp.int32)


def plant(values, own_key, least, largest):
    extent = values.shape
    index_at = [jax.random.randint(jax.random.fold_in(own_key, axis), (), 0, extent[axis]) for axis in range(len(extent))]
    values = values.at[tuple(index_at)].set(least)
    longest = extent.index(max(extent))
    index_at[longest] = (index_at[longest] + 1) % extent[longest]
    return values.at[tuple(index_at)].set(largest)


def block_levels(rng, shape, pieces, least, high):
    level = 1.0
    for dim, blocks in pieces:
        steps = jax.random.uniform(jax.random.fold_in(jax.random.fold_in(rng, 6), dim), (blocks,), jnp.float32, least / len(pieces), high / len(pieces))
        level = level * jnp.repeat(jnp.exp(steps), shape[dim] // blocks).reshape((-1,) + (1,) * (len(shape) - 1 - dim))
    return level


def noise(stream_key, shape, scale, bound, pieces=(), held_as=jnp.bfloat16):
    drawn = scale * jax.random.normal(stream_key, shape, jnp.float32)
    if pieces:
        drawn = drawn * block_levels(stream_key, shape, pieces, -0.22, 0.18)
    return jnp.clip(drawn, -bound, bound).astype(held_as)


def setup_inputs(seed: int = 0) -> dict:
    arg_keys = jax.random.split(jax.random.key(seed), 16)
    density = noise(arg_keys[0], (NBOX, 2, PANELS), 1.0, 6.0, ((0, 32),))
    radiate = noise(arg_keys[1], (NBOX, PANELS, 2 * Q_LO), PANELS ** -0.5, 0.5, ((0, 32),))
    receive = noise(arg_keys[2], (NBOX, PANELS, 2 * Q_LO), (2 * Q_LO) ** -0.5, 0.1875, ((0, 32),))
    near_tiles = noise(arg_keys[3], (NBOX * ((NEAR + 1) // 2), 2, PANELS, PANELS), (PANELS * NEAR) ** -0.5, 0.109375, ((0, 32),))
    near_src = draw_near_src(jax.random.fold_in(arg_keys[15], 71), 0)
    near_tile = draw_near_tile(jax.random.fold_in(arg_keys[15], 71), 0)
    send_box = draw_send_box(jax.random.fold_in(arg_keys[15], 71), 0)
    distant_pattern_slot = draw_distant_pattern_slot(jax.random.fold_in(arg_keys[15], 71), 0)
    far_type = plant(jax.random.randint(arg_keys[8], (NBOX, FAR), 0, TYPES), jax.random.fold_in(arg_keys[8], 1), 0, TYPES - 1).astype(jnp.int32)
    trans_lo = noise(arg_keys[9], (TYPES, 2, Q_LO), FAR ** -0.5, 0.4375)
    interp_matrix = noise(arg_keys[10], (Q_LO, Q_HI), Q_LO ** -0.5, 0.25)
    shifts = noise(arg_keys[11], (8, 2, Q_HI), 8 ** -0.5, 2.0, (), jnp.float32)
    par_far = draw_par_far(jax.random.fold_in(arg_keys[15], 71), 0)
    par_type = plant(jax.random.randint(arg_keys[13], (NPAR, FAR), 0, TYPES), jax.random.fold_in(arg_keys[13], 1), 0, TYPES - 1).astype(jnp.int32)
    trans_hi = noise(arg_keys[14], (TYPES, 2, Q_HI), FAR ** -0.5, 0.4375)
    return {"density": density, "radiate": radiate, "receive": receive, "near_tiles": near_tiles, "near_src": near_src, "near_tile": near_tile, "send_box": send_box, "distant_pattern_slot": distant_pattern_slot, "far_type": far_type, "trans_lo": trans_lo, "interp_matrix": interp_matrix, "shifts": shifts, "par_far": par_far, "par_type": par_type, "trans_hi": trans_hi}


def radiated(density, radiate):
    half_width = radiate.shape[-1] // 2
    matvec_result = jnp.einsum("lmq,lqj->lmj", density.astype(jnp.float32), radiate.astype(jnp.float32))
    real_part = matvec_result[:, 0, :half_width] - matvec_result[:, 1, half_width:]
    imag_part = matvec_result[:, 0, half_width:] + matvec_result[:, 1, :half_width]
    return jnp.stack([real_part, imag_part], 1)


def translated(pattern_in, operator_in):
    emitter_values = pattern_in.astype(jnp.float32)
    factor = operator_in.astype(jnp.float32)
    real_part = jnp.sum(factor[..., 0, :] * emitter_values[..., 0, :] - factor[..., 1, :] * emitter_values[..., 1, :], -2)
    imag_part = jnp.sum(factor[..., 0, :] * emitter_values[..., 1, :] + factor[..., 1, :] * emitter_values[..., 0, :], -2)
    return jnp.stack([real_part, imag_part], -2)


def shifted_sum(interpolated, shifts):
    width = interpolated.shape[-1]
    grouped = interpolated.reshape(-1, 8, 2, width)
    real_part = jnp.sum(grouped[:, :, 0] * shifts[:, 0] - grouped[:, :, 1] * shifts[:, 1], 1)
    imag_part = jnp.sum(grouped[:, :, 0] * shifts[:, 1] + grouped[:, :, 1] * shifts[:, 0], 1)
    return jnp.stack([real_part, imag_part], 1)


def spread_down(incoming_hi, shifts):
    parent = incoming_hi[:, None]
    real_part = shifts[None, :, 0] * parent[:, :, 0] + shifts[None, :, 1] * parent[:, :, 1]
    imag_part = shifts[None, :, 0] * parent[:, :, 1] - shifts[None, :, 1] * parent[:, :, 0]
    stacked = jnp.stack([real_part, imag_part], 2)
    return stacked.reshape(-1, 2, incoming_hi.shape[-1]).astype(jnp.bfloat16)


def received_field(receive, incoming):
    real_in = incoming[:, 0]
    imag_in = incoming[:, 1]
    blending_operator = jnp.stack([jnp.concatenate([real_in, -imag_in], -1), jnp.concatenate([imag_in, real_in], -1)], 1)
    return jnp.einsum("mws,mis->miw", receive.astype(jnp.float32), blending_operator.astype(jnp.float32))


def reference(density, radiate, receive, near_tiles, near_src, near_tile, send_box, distant_pattern_slot, far_type, trans_lo, interp_matrix, shifts, par_far, par_type, trans_hi):
    pattern_lo = radiated(density, radiate).astype(jnp.bfloat16)
    receiver = (jnp.arange(NBOX, dtype=jnp.int32) // BOX_DEV)[:, None]
    live = distant_pattern_slot < NDEV * SLOTS
    sender = jnp.minimum(distant_pattern_slot // SLOTS, NDEV - 1)
    within = distant_pattern_slot % SLOTS
    chosen = send_box[sender, receiver, within]
    far_source = jnp.where(live, sender * BOX_DEV + chosen, NBOX).astype(jnp.int32)
    padded_lo = jnp.concatenate([pattern_lo, jnp.zeros((1, 2, Q_LO), jnp.bfloat16)], 0)

    def far_box(entries):
        rows, kinds = entries
        return translated(padded_lo[rows], trans_lo[kinds])

    incoming_lo = lax.map(far_box, (far_source, far_type))
    interpolated = jnp.einsum("gcq,qh->gch", pattern_lo.astype(jnp.float32), interp_matrix.astype(jnp.float32))
    pattern_hi = shifted_sum(interpolated, shifts).astype(jnp.bfloat16)
    padded_hi = jnp.concatenate([pattern_hi, jnp.zeros((1, 2, Q_HI), jnp.bfloat16)], 0)

    def far_parent(entries):
        rows, kinds = entries
        return translated(padded_hi[rows], trans_hi[kinds])

    incoming_hi = lax.map(far_parent, (par_far, par_type))
    down = spread_down(incoming_hi, shifts)
    from_parent = jnp.einsum("gch,qh->gcq", down.astype(jnp.float32), interp_matrix.astype(jnp.float32))
    incoming = (incoming_lo + from_parent).astype(jnp.bfloat16)
    far_field = received_field(receive, incoming)
    density_pad = jnp.concatenate([density, jnp.zeros((1, 2, PANELS), jnp.bfloat16)], 0)
    tiles_pad = jnp.concatenate([near_tiles, jnp.zeros((1, 2, PANELS, PANELS), jnp.bfloat16)], 0)

    def near_box(entries):
        sources, tiles = entries
        values = density_pad[sources].astype(jnp.float32)
        blocks = tiles_pad[tiles].astype(jnp.float32)
        matvec_result = jnp.einsum("naij,nbj->abi", blocks, values)
        return jnp.stack([matvec_result[0, 0] - matvec_result[1, 1], matvec_result[0, 1] + matvec_result[1, 0]], 0)

    close_range_field = lax.map(near_box, (near_src, near_tile))
    return 0.5 * density.astype(jnp.float32) + close_range_field + far_field
```

```python
import functools

import jax
import jax.numpy as jnp
from jax import lax
from jax.experimental import pallas as pl
from jax.experimental.pallas import tpu as pltpu
from jax.sharding import PartitionSpec as P

F32 = jnp.float32
BF16 = jnp.bfloat16
LANE = 128
VMEM_SPEC = pl.BlockSpec(memory_space=pltpu.VMEM)
SMEM_SPEC = pl.BlockSpec(memory_space=pltpu.SMEM)
ANY_SPEC = pl.BlockSpec(memory_space=pl.ANY)
MIB = 1 << 20


def iota(shape, dim):
    return lax.broadcasted_iota(jnp.int32, shape, dim)


def dot_nn(lhs, rhs):
    return lax.dot_general(lhs, rhs, (((1,), (0,)), ((), ())), preferred_element_type=F32)


def dot_nt(lhs, rhs):
    return lax.dot_general(lhs, rhs, (((1,), (1,)), ((), ())), preferred_element_type=F32)


def shifted(value, axis, steps):
    count = lax.axis_size(axis)
    first, last = (max(0, -steps), min(count, count - steps))
    return lax.ppermute(value, axis, [(source, source + steps) for source in range(first, last)])


def radiate_kernel(
    dens_ref, radiate_ref, send_ref, interp_ref, shift_ref, out_ref, rad, summed, table, parent, sems
):
    boxes = rad.shape[0]
    width = rad.shape[2] // 2
    per_step = 4
    steps = boxes // per_step
    copies = []
    for step in range(steps):
        part = pl.ds(step * per_step, per_step)
        copies.append(pltpu.make_async_copy(radiate_ref.at[part], rad.at[part], sems.at[step]))
        copies[-1].start()
    dens = dens_ref[...].astype(F32)
    owner = (iota(dens.shape, 0) // 2) % per_step
    blocks = jnp.concatenate([jnp.where(owner == b, dens, 0.0) for b in range(per_step)], 1)
    for step in range(steps):
        copies[step].wait()
        rows = slice(step * 2 * per_step, (step + 1) * 2 * per_step)
        weights = rad[step * per_step : (step + 1) * per_step].reshape(per_step * LANE, 2 * width)
        summed[rows] = dot_nn(blocks[rows].astype(BF16), weights).reshape(
            2 * per_step, 2 * width // LANE, LANE
        )
    chunks = width // LANE
    re_chunks, im_chunks = [], []
    for r in range(chunks):
        first_lo = summed[pl.ds(0, boxes, stride=2), r, :]
        first_hi = summed[pl.ds(0, boxes, stride=2), chunks + r, :]
        second_lo = summed[pl.ds(1, boxes, stride=2), r, :]
        second_hi = summed[pl.ds(1, boxes, stride=2), chunks + r, :]
        re_chunks.append((first_lo - second_hi).astype(BF16))
        im_chunks.append((first_hi + second_lo).astype(BF16))
    re_part = jnp.concatenate(re_chunks, 1)
    im_part = jnp.concatenate(im_chunks, 1)
    for r in range(chunks):
        table[pl.ds(r, boxes, stride=8), :] = re_chunks[r].astype(F32)
        table[pl.ds(chunks + r, boxes, stride=8), :] = im_chunks[r].astype(F32)
    table[pl.ds(boxes * 8, 8), :] = jnp.zeros((8, LANE), F32)
    wide = dot_nn(jnp.concatenate([re_part, im_part], 0), interp_ref[...])
    hi_chunks = wide.shape[1] // LANE
    parents = boxes // 8
    for r in range(hi_chunks):
        cols = slice(r * LANE, (r + 1) * LANE)
        s_re = shift_ref[pl.ds(2 * r, 8, stride=2 * hi_chunks), :]
        s_im = shift_ref[pl.ds(2 * r + 1, 8, stride=2 * hi_chunks), :]
        for p in range(parents):
            w_re = wide[p * 8 : (p + 1) * 8, cols]
            w_im = wide[boxes + p * 8 : boxes + (p + 1) * 8, cols]
            row = p * 2 * hi_chunks + r
            parent[row : row + 1] = jnp.sum(w_re * s_re - w_im * s_im, 0, keepdims=True)
            row += hi_chunks
            parent[row : row + 1] = jnp.sum(w_re * s_im + w_im * s_re, 0, keepdims=True)
    slots, devices = send_ref.shape
    hi_rows = parents * 2 * hi_chunks
    parent_block = parent[...].astype(BF16)

    def fill(d, carry):
        for k in range(slots // 2):
            pair = [
                table[pl.ds(pl.multiple_of(send_ref[2 * k + h, d] * 8, 8), 8), :] for h in range(2)
            ]
            out_ref[d, 16 * k : 16 * (k + 1)] = jnp.concatenate(pair, 0).astype(BF16)
        out_ref[d, 8 * slots : 8 * slots + hi_rows] = parent_block
        return carry

    lax.fori_loop(0, devices, fill, 0)


def middle_kernel(
    types,
    box_total,
    lower_ref,
    dens_ref,
    upper_ref,
    near_src_ref,
    near_tile_ref,
    tiles_ref,
    slot_ref,
    type_ref,
    op_lo_ref,
    par_far_ref,
    par_type_ref,
    op_hi_ref,
    near_ref,
    d_lo_ref,
    d_hi_ref,
    tiles,
    dens3,
    acc,
    window,
    code,
    index,
    wide_op,
    wide_hi,
    op_lo,
    sems,
):
    boxes, near = near_src_ref.shape
    tile_count = tiles.shape[0]
    per_box = tile_count // boxes
    copies = []
    for step in range(boxes):
        part = pl.ds(step * per_box, per_box)
        copies.append(pltpu.make_async_copy(tiles_ref.at[part], tiles.at[part], sems.at[step]))
        copies[-1].start()
    position = lax.axis_index("box") * lax.axis_size("samp") + lax.axis_index("samp")

    def locate(g, carry):
        for n in range(near):
            source = near_src_ref[g, n]
            live = source < box_total
            tile = jnp.where(live, near_tile_ref[g, n] - position * tile_count, tile_count)
            code[tile] = g * 64 + source - (position - 1) * boxes
        return carry

    lax.fori_loop(0, boxes, locate, 0)

    for k, ref in enumerate((lower_ref, dens_ref, upper_ref)):
        dens3[pl.ds(2 * boxes * k, 2 * boxes), :] = ref[...].astype(F32)
    first = dens3[pl.ds(0, 3 * boxes, stride=2), :]
    second = dens3[pl.ds(1, 3 * boxes, stride=2), :]
    window[...] = jnp.concatenate(
        [
            jnp.concatenate([first, -second], 1),
            jnp.concatenate([second, first], 1),
            jnp.zeros((LANE - 6 * boxes, 2 * LANE), F32),
        ],
        0,
    ).astype(BF16)
    acc[...] = jnp.zeros(acc.shape, F32)

    faces = index.shape[1]
    index[...] = jnp.full(index.shape, -1, jnp.int32)
    far = slot_ref.shape[1]
    rows = slot_ref.shape[0]
    parents = boxes // 8
    index[0:rows, 0:far] = slot_ref[...]
    index[rows : 2 * rows, 0:far] = type_ref[...]
    prow = par_far_ref.shape[0]
    index[2 * rows : 2 * rows + prow, 0:far] = par_far_ref[...]
    index[2 * rows + prow : 2 * rows + 2 * prow, 0:far] = par_type_ref[...]

    type_pad = op_lo.shape[0]
    chunks = op_lo.shape[1] // (2 * LANE)
    wide_op[0 : types * 2 * chunks] = op_lo_ref[...].astype(F32)
    wide_op[types * 2 * chunks : type_pad * 2 * chunks] = jnp.zeros(
        ((type_pad - types) * 2 * chunks, LANE), F32
    )
    for c in range(2):
        for r in range(chunks):
            col = (c * chunks + r) * LANE
            op_lo[:, col : col + LANE] = wide_op[
                pl.ds(2 * r + c, type_pad, stride=2 * chunks), :
            ].astype(BF16)

    def counts(source_row, type_row, sources):
        source = index[pl.ds(source_row, 1), :]
        kind = index[pl.ds(type_row, 1), :]
        by_source = jnp.where(iota((sources, faces), 0) == source, 1.0, 0.0).astype(BF16)
        by_type = jnp.where(iota((type_pad, faces), 0) == kind, 1.0, 0.0).astype(BF16)
        return dot_nt(by_source, by_type).astype(BF16)

    lane = iota((8, LANE), 1)
    lane = jnp.where(lane < 3 * boxes, lane, jnp.where(lane < 6 * boxes, lane - 3 * boxes, -1))
    slot_total = d_lo_ref.shape[1]

    def step_box(g, carry):
        part = pl.ds(g * per_box, per_box)
        d_lo_ref[g] = dot_nn(counts(g, rows + g, slot_total), op_lo[...]).astype(d_lo_ref.dtype)
        pltpu.make_async_copy(tiles_ref.at[part], tiles.at[part], sems.at[g]).wait()
        both = tiles[part]
        lhs = jnp.concatenate(
            [both[:, 0].reshape(per_box * LANE, LANE), both[:, 1].reshape(per_box * LANE, LANE)], 1
        )
        product = dot_nt(lhs, window[...]).reshape(per_box, LANE // 8, 8, LANE)
        for j in range(per_box):
            entry = code[g * per_box + j]
            chosen = lane == (entry & 63)
            owner = entry >> 6
            acc[owner] = acc[owner] + jnp.where(chosen[None], product[j], 0.0)
        return carry

    lax.fori_loop(0, boxes, step_box, 0)

    start = 2 * rows + lax.axis_index("samp") * parents
    sources = d_hi_ref.shape[0] // parents
    count_hi = jnp.concatenate(
        [counts(start + p, start + prow + p, sources) for p in range(parents)], 0
    )
    hi_chunks = op_hi_ref.shape[0] // (2 * types)
    group = 4 * 2 * hi_chunks

    def widen(i, carry):
        part = pl.ds(pl.multiple_of(i * group, group), group)
        wide_hi[part] = op_hi_ref[part].astype(F32)
        return carry

    lax.fori_loop(0, types // 4, widen, 0, unroll=2)
    wide_hi[types * 2 * hi_chunks : type_pad * 2 * hi_chunks] = jnp.zeros(
        ((type_pad - types) * 2 * hi_chunks, LANE), F32
    )
    for c in range(2):
        for r in range(0, hi_chunks, 2):
            rhs = jnp.concatenate(
                [
                    wide_hi[pl.ds(2 * (r + q) + c, type_pad, stride=2 * hi_chunks), :].astype(BF16)
                    for q in range(2)
                ],
                1,
            )
            col = (c * hi_chunks + r) * LANE
            d_hi_ref[:, col : col + 2 * LANE] = dot_nn(count_hi, rhs).astype(d_hi_ref.dtype)

    for g in range(boxes):
        flipped = acc[g].reshape(LANE, LANE).T
        row = 2 * g
        near_ref[row : row + 1] = (
            jnp.sum(flipped[0 : 3 * boxes], 0, keepdims=True)
            + 0.5 * dens3[pl.ds(2 * boxes + row, 1), :]
        )
        near_ref[row + 1 : row + 2] = (
            jnp.sum(flipped[3 * boxes : 6 * boxes], 0, keepdims=True)
            + 0.5 * dens3[pl.ds(2 * boxes + row + 1, 1), :]
        )


def last_kernel(
    arrived_ref,
    d_lo_ref,
    d_hi_ref,
    shift_ref,
    interp_ref,
    receive_ref,
    near_ref,
    out_ref,
    receive,
    slots,
    parents,
    down,
    incoming,
    blend,
    sems,
):
    boxes = receive.shape[0]
    per_step = 4
    steps = boxes // per_step
    copies = []
    for step in range(steps):
        part = pl.ds(step * per_step, per_step)
        copies.append(pltpu.make_async_copy(receive_ref.at[part], receive.at[part], sems.at[step]))
        copies[-1].start()
    devices, lines, _ = arrived_ref.shape
    own_parents = boxes // 8
    sources = d_hi_ref.shape[0] // own_parents
    hi_chunks = d_hi_ref.shape[1] // (2 * LANE)
    slot_total = d_lo_ref.shape[1]
    chunks = d_lo_ref.shape[2] // (2 * LANE)
    lo_lines = slot_total // devices * 2 * chunks
    hi_lines = lines - lo_lines
    parents[...] = arrived_ref[:, lo_lines:, :].astype(F32).reshape(devices * hi_lines, LANE)
    slots[...] = arrived_ref[:, :lo_lines, :].astype(F32).reshape(devices * lo_lines, LANE)
    for r in range(hi_chunks):
        first = parents[pl.ds(r, sources, stride=2 * hi_chunks), :]
        second = parents[pl.ds(hi_chunks + r, sources, stride=2 * hi_chunks), :]
        s_re = shift_ref[pl.ds(2 * r, 8, stride=2 * hi_chunks), :]
        s_im = shift_ref[pl.ds(2 * r + 1, 8, stride=2 * hi_chunks), :]
        re_rows, im_rows = [], []
        for p in range(own_parents):
            rows = slice(p * sources, (p + 1) * sources)
            o_re = d_hi_ref[rows, r * LANE : (r + 1) * LANE].astype(F32)
            o_im = d_hi_ref[rows, (hi_chunks + r) * LANE : (hi_chunks + r + 1) * LANE].astype(F32)
            t_re = jnp.sum(o_re * first - o_im * second, 0, keepdims=True)
            t_im = jnp.sum(o_re * second + o_im * first, 0, keepdims=True)
            re_rows.append(s_re * t_re + s_im * t_im)
            im_rows.append(s_re * t_im - s_im * t_re)
        cols = slice(r * LANE, (r + 1) * LANE)
        down[:, cols] = jnp.concatenate(re_rows + im_rows, 0).astype(BF16)
    for r in range(chunks):
        first = slots[pl.ds(r, slot_total, stride=2 * chunks), :]
        second = slots[pl.ds(chunks + r, slot_total, stride=2 * chunks), :]
        for g in range(boxes):
            o_re = d_lo_ref[g, :, r * LANE : (r + 1) * LANE].astype(F32)
            o_im = d_lo_ref[g, :, (chunks + r) * LANE : (chunks + r + 1) * LANE].astype(F32)
            cols = slice(r * LANE, (r + 1) * LANE)
            incoming[g : g + 1, cols] = jnp.sum(o_re * first - o_im * second, 0, keepdims=True)
            incoming[boxes + g : boxes + g + 1, cols] = jnp.sum(
                o_re * second + o_im * first, 0, keepdims=True
            )
    total = incoming[...] + dot_nt(down[...], interp_ref[...])
    total = total.astype(BF16).astype(F32)
    for r in range(chunks):
        re_part = total[:boxes, r * LANE : (r + 1) * LANE]
        im_part = total[boxes:, r * LANE : (r + 1) * LANE]
        blend[pl.ds(0, boxes, stride=2), r, :] = re_part
        blend[pl.ds(1, boxes, stride=2), r, :] = im_part
        blend[pl.ds(0, boxes, stride=2), chunks + r, :] = -im_part
        blend[pl.ds(1, boxes, stride=2), chunks + r, :] = re_part
    owner = (iota((2 * per_step, LANE), 0) // 2) % per_step
    for step in range(steps):
        rows = slice(step * 2 * per_step, (step + 1) * 2 * per_step)
        lhs = jnp.concatenate([blend[rows, r, :] for r in range(2 * chunks)], 1).astype(BF16)
        copies[step].wait()
        weights = receive[step * per_step : (step + 1) * per_step]
        product = dot_nt(lhs, weights.reshape(per_step * LANE, 2 * chunks * LANE))
        total = near_ref[rows]
        for b in range(per_step):
            total = total + jnp.where(owner == b, product[:, b * LANE : (b + 1) * LANE], 0.0)
        out_ref[rows] = total


def tiled_rows(array):
    count, parts, width = array.shape
    cut = array.reshape(count, parts, width // LANE, LANE)
    return cut.transpose(0, 2, 1, 3).reshape(-1, LANE)


def on_device(
    density,
    radiate,
    receive,
    near_tiles,
    near_src,
    near_tile,
    send_box,
    distant_pattern_slot,
    far_type,
    trans_lo,
    interp_matrix,
    shifts,
    par_far,
    par_type,
    trans_hi,
):
    boxes, _, panels = density.shape
    devices = lax.axis_size("box") * lax.axis_size("samp")
    slots = send_box.shape[2]
    types, _, width_lo = trans_lo.shape
    width_hi = trans_hi.shape[2]
    parents = boxes // 8
    slot_total = devices * slots
    par_total = devices * parents
    type_pad = -(-types // 8) * 8
    lines = slots * 2 * width_lo // LANE + parents * 2 * width_hi // LANE
    held = F32 if slot_total <= 128 else BF16
    rows = density.reshape(boxes * 2, panels)
    lower = shifted(rows, ("box", "samp"), 1)
    upper = shifted(rows, ("box", "samp"), -1)
    shift_rows = tiled_rows(shifts)
    outgoing = pl.pallas_call(
        radiate_kernel,
        out_shape=jax.ShapeDtypeStruct((devices, lines, LANE), BF16),
        in_specs=[VMEM_SPEC, ANY_SPEC, SMEM_SPEC, VMEM_SPEC, VMEM_SPEC],
        out_specs=VMEM_SPEC,
        scratch_shapes=[
            pltpu.VMEM(radiate.shape, BF16),
            pltpu.VMEM((2 * boxes, 2 * width_lo // LANE, LANE), F32),
            pltpu.VMEM((boxes * 8 + 8, LANE), F32),
            pltpu.VMEM((parents * 2 * width_hi // LANE, LANE), F32),
            pltpu.SemaphoreType.DMA((boxes // 4,)),
        ],
        compiler_params=pltpu.CompilerParams(vmem_limit_bytes=12 * MIB),
        cost_estimate=pl.CostEstimate(flops=10**9, bytes_accessed=8 * MIB, transcendentals=0),
    )(rows, radiate, send_box[0].T, interp_matrix, shift_rows)
    arrived = lax.all_to_all(outgoing, ("box", "samp"), split_axis=0, concat_axis=0, tiled=True)
    tile_count = near_tiles.shape[0]
    near, d_lo, d_hi = pl.pallas_call(
        functools.partial(middle_kernel, types, boxes * devices),
        out_shape=(
            pltpu.VMEM((2 * boxes, panels), F32),
            pltpu.VMEM((boxes, slot_total, 2 * width_lo), held),
            pltpu.VMEM((parents * par_total, 2 * width_hi), held),
        ),
        in_specs=[VMEM_SPEC] * 3
        + [SMEM_SPEC] * 2
        + [ANY_SPEC]
        + [VMEM_SPEC] * 6,
        out_specs=(VMEM_SPEC,) * 3,
        scratch_shapes=[
            pltpu.VMEM(near_tiles.shape, BF16),
            pltpu.VMEM((6 * boxes, panels), F32),
            pltpu.VMEM((boxes, panels // 8, 8, LANE), F32),
            pltpu.VMEM((LANE, 2 * LANE), BF16),
            pltpu.SMEM((tile_count + 8,), jnp.int32),
            pltpu.VMEM((2 * boxes + 2 * par_far.shape[0], 2 * LANE), jnp.int32),
            pltpu.VMEM((type_pad * 2 * width_lo // LANE, LANE), F32),
            pltpu.VMEM((type_pad * 2 * width_hi // LANE, LANE), F32),
            pltpu.VMEM((type_pad, 2 * width_lo), BF16),
            pltpu.SemaphoreType.DMA((boxes,)),
        ],
        compiler_params=pltpu.CompilerParams(vmem_limit_bytes=30 * MIB),
        cost_estimate=pl.CostEstimate(flops=10**10, bytes_accessed=20 * MIB, transcendentals=0),
    )(
        lower,
        rows,
        upper,
        near_src,
        near_tile,
        near_tiles,
        distant_pattern_slot,
        far_type,
        tiled_rows(trans_lo),
        par_far,
        par_type,
        tiled_rows(trans_hi),
    )
    lo_lines = slots * 2 * width_lo // LANE
    field = pl.pallas_call(
        last_kernel,
        out_shape=jax.ShapeDtypeStruct((2 * boxes, panels), F32),
        in_specs=[VMEM_SPEC] * 5 + [ANY_SPEC] + [VMEM_SPEC],
        out_specs=VMEM_SPEC,
        scratch_shapes=[
            pltpu.VMEM(receive.shape, BF16),
            pltpu.VMEM((devices * lo_lines, LANE), F32),
            pltpu.VMEM((devices * (lines - lo_lines), LANE), F32),
            pltpu.VMEM((2 * boxes, width_hi), BF16),
            pltpu.VMEM((2 * boxes, width_lo), F32),
            pltpu.VMEM((2 * boxes, 2 * width_lo // LANE, LANE), F32),
            pltpu.SemaphoreType.DMA((boxes // 4,)),
        ],
        compiler_params=pltpu.CompilerParams(vmem_limit_bytes=20 * MIB),
        cost_estimate=pl.CostEstimate(flops=10**9, bytes_accessed=8 * MIB, transcendentals=0),
    )(arrived, d_lo, d_hi, shift_rows, interp_matrix, receive, near)
    return field.reshape(boxes, 2, panels)


def solution(mesh):
    both = ("box", "samp")
    return jax.shard_map(
        on_device,
        mesh=mesh,
        in_specs=(
            P(both, None, None),
            P(both, None, None),
            P(both, None, None),
            P(both, None, None, None),
            P(both, None),
            P(both, None),
            P(both, None, None),
            P(both, None),
            P(both, None),
            P(),
            P(),
            P(),
            P("box", None),
            P("box", None),
            P(),
        ),
        out_specs=P(both, None, None),
        check_vma=False,
    )
```

```python
import functools

import jax
import jax.numpy as jnp
from jax import lax
from jax.experimental import pallas as pl
from jax.experimental.pallas import tpu as pltpu
from jax.sharding import PartitionSpec as P

F32 = jnp.float32
BF16 = jnp.bfloat16
LANE = 128
VMEM_SPEC = pl.BlockSpec(memory_space=pltpu.VMEM)
SMEM_SPEC = pl.BlockSpec(memory_space=pltpu.SMEM)
ANY_SPEC = pl.BlockSpec(memory_space=pl.ANY)
HBM_SPEC = pl.BlockSpec(memory_space=pltpu.HBM)
MIB = 1 << 20


def iota(shape, dim):
    return lax.broadcasted_iota(jnp.int32, shape, dim)


def dot_nn(lhs, rhs):
    return lax.dot_general(lhs, rhs, (((1,), (0,)), ((), ())), preferred_element_type=F32)


def dot_nt(lhs, rhs):
    return lax.dot_general(lhs, rhs, (((1,), (1,)), ((), ())), preferred_element_type=F32)


def shifted(value, axis, steps):
    count = lax.axis_size(axis)
    first, last = (max(0, -steps), min(count, count - steps))
    return lax.ppermute(value, axis, [(source, source + steps) for source in range(first, last)])


def fetch(pairs, sems, first=0):
    copies = []
    for k, (source, target) in enumerate(pairs):
        copies.append(pltpu.make_async_copy(source, target, sems.at[first + k]))
        copies[-1].start()
    return copies


def radiate_kernel(
    dens_hbm,
    radiate_ref,
    send_hbm,
    interp_hbm,
    shift_hbm,
    out_ref,
    rad,
    dens_ref,
    send_ref,
    interp_ref,
    shift_ref,
    summed,
    table,
    parent,
    sems,
    extra,
):
    boxes = rad.shape[0]
    width = rad.shape[2] // 2
    per_step = 4
    steps = boxes // per_step
    others = fetch(
        [(dens_hbm, dens_ref), (send_hbm, send_ref), (shift_hbm, shift_ref)], extra
    )
    copies = []
    for step in range(steps):
        part = pl.ds(step * per_step, per_step)
        copies.append(pltpu.make_async_copy(radiate_ref.at[part], rad.at[part], sems.at[step]))
        copies[-1].start()
    others += fetch([(interp_hbm, interp_ref)], extra, 3)
    others[0].wait()
    dens = dens_ref[...].astype(F32)
    owner = (iota(dens.shape, 0) // 2) % per_step
    blocks = jnp.concatenate([jnp.where(owner == b, dens, 0.0) for b in range(per_step)], 1)
    for step in range(steps):
        copies[step].wait()
        rows = slice(step * 2 * per_step, (step + 1) * 2 * per_step)
        weights = rad[step * per_step : (step + 1) * per_step].reshape(per_step * LANE, 2 * width)
        summed[rows] = dot_nn(blocks[rows].astype(BF16), weights).reshape(
            2 * per_step, 2 * width // LANE, LANE
        )
    chunks = width // LANE
    re_chunks, im_chunks = [], []
    for r in range(chunks):
        first_lo = summed[pl.ds(0, boxes, stride=2), r, :]
        first_hi = summed[pl.ds(0, boxes, stride=2), chunks + r, :]
        second_lo = summed[pl.ds(1, boxes, stride=2), r, :]
        second_hi = summed[pl.ds(1, boxes, stride=2), chunks + r, :]
        re_chunks.append((first_lo - second_hi).astype(BF16))
        im_chunks.append((first_hi + second_lo).astype(BF16))
    re_part = jnp.concatenate(re_chunks, 1)
    im_part = jnp.concatenate(im_chunks, 1)
    for r in range(chunks):
        table[pl.ds(r, boxes, stride=8), :] = re_chunks[r].astype(F32)
        table[pl.ds(chunks + r, boxes, stride=8), :] = im_chunks[r].astype(F32)
    table[pl.ds(boxes * 8, 8), :] = jnp.zeros((8, LANE), F32)
    for copy in others[1:]:
        copy.wait()
    wide = dot_nn(jnp.concatenate([re_part, im_part], 0), interp_ref[...])
    hi_chunks = wide.shape[1] // LANE
    parents = boxes // 8
    for r in range(hi_chunks):
        cols = slice(r * LANE, (r + 1) * LANE)
        s_re = shift_ref[pl.ds(2 * r, 8, stride=2 * hi_chunks), :]
        s_im = shift_ref[pl.ds(2 * r + 1, 8, stride=2 * hi_chunks), :]
        for p in range(parents):
            w_re = wide[p * 8 : (p + 1) * 8, cols]
            w_im = wide[boxes + p * 8 : boxes + (p + 1) * 8, cols]
            row = p * 2 * hi_chunks + r
            parent[row : row + 1] = jnp.sum(w_re * s_re - w_im * s_im, 0, keepdims=True)
            row += hi_chunks
            parent[row : row + 1] = jnp.sum(w_re * s_im + w_im * s_re, 0, keepdims=True)
    slots, devices = send_ref.shape
    hi_rows = parents * 2 * hi_chunks
    parent_block = parent[...].astype(BF16)

    def fill(d, carry):
        for k in range(slots // 2):
            pair = [
                table[pl.ds(pl.multiple_of(send_ref[2 * k + h, d] * 8, 8), 8), :] for h in range(2)
            ]
            out_ref[d, 16 * k : 16 * (k + 1)] = jnp.concatenate(pair, 0).astype(BF16)
        out_ref[d, 8 * slots : 8 * slots + hi_rows] = parent_block
        return carry

    lax.fori_loop(0, devices, fill, 0)


def middle_kernel(
    types,
    box_total,
    lower_hbm,
    dens_hbm,
    upper_hbm,
    near_src_hbm,
    near_tile_hbm,
    tiles_hbm,
    slot_hbm,
    type_hbm,
    op_lo_hbm,
    par_far_hbm,
    par_type_hbm,
    op_hi_hbm,
    near_ref,
    d_lo_ref,
    d_hi_ref,
    tiles,
    halo,
    near_src_ref,
    near_tile_ref,
    slot_ref,
    type_ref,
    op_lo_ref,
    par_far_ref,
    par_type_ref,
    op_hi,
    dens3,
    left,
    right,
    acc,
    code,
    index,
    wide_op,
    op_lo,
    sems,
    extra,
):
    boxes, near = near_src_ref.shape
    tile_count = tiles.shape[0]
    steps = sems.shape[0]
    per_step = tile_count // steps
    others = fetch(
        [
            (near_src_hbm, near_src_ref),
            (near_tile_hbm, near_tile_ref),
            (op_lo_hbm, op_lo_ref),
            (slot_hbm, slot_ref),
            (type_hbm, type_ref),
            (lower_hbm, halo.at[0]),
            (dens_hbm, halo.at[1]),
            (upper_hbm, halo.at[2]),
            (par_far_hbm, par_far_ref),
            (par_type_hbm, par_type_ref),
            (op_hi_hbm, op_hi),
        ],
        extra,
    )

    def tile_copy(step):
        part = pl.ds(step * per_step, per_step)
        return pltpu.make_async_copy(tiles_hbm.at[part], tiles.at[part], sems.at[step])

    for step in range(steps):
        tile_copy(step).start()
    position = lax.axis_index("box") * lax.axis_size("samp") + lax.axis_index("samp")
    d_hi_ref[...] = jnp.zeros(d_hi_ref.shape, F32)
    acc[...] = jnp.zeros(acc.shape, F32)
    index[...] = jnp.full(index.shape, -1, jnp.int32)
    left[...] = jnp.zeros(left.shape, F32)
    right[...] = jnp.zeros(right.shape, F32)
    type_pad = op_lo.shape[0]
    chunks = op_lo.shape[1] // (2 * LANE)
    wide_op[types * 2 * chunks : type_pad * 2 * chunks] = jnp.zeros(
        ((type_pad - types) * 2 * chunks, LANE), F32
    )
    others[0].wait()
    others[1].wait()

    def locate(g, carry):
        for n in range(near):
            source = near_src_ref[g, n]
            live = source < box_total
            tile = jnp.where(live, near_tile_ref[g, n] - position * tile_count, tile_count)
            code[tile] = g * 64 + source - (position - 1) * boxes
        return carry

    lax.fori_loop(0, boxes, locate, 0)

    for copy in others[2:]:
        copy.wait()
    wide_op[0 : types * 2 * chunks] = op_lo_ref[...].astype(F32)
    for c in range(2):
        for r in range(chunks):
            col = (c * chunks + r) * LANE
            op_lo[:, col : col + LANE] = wide_op[
                pl.ds(2 * r + c, type_pad, stride=2 * chunks), :
            ].astype(BF16)
    far = slot_ref.shape[1]
    index[0:boxes, 0:far] = slot_ref[...]
    index[boxes : 2 * boxes, 0:far] = type_ref[...]
    for k in range(3):
        dens3[pl.ds(2 * boxes * k, 2 * boxes), :] = halo[k].astype(F32)
    first = dens3[pl.ds(0, 3 * boxes, stride=2), :]
    second = dens3[pl.ds(1, 3 * boxes, stride=2), :]
    left[pl.ds(0, 3 * boxes, stride=8), :] = first
    left[pl.ds(1, 3 * boxes, stride=8), :] = second
    right[pl.ds(0, 3 * boxes, stride=8), :] = -second
    right[pl.ds(1, 3 * boxes, stride=8), :] = first

    slot_total = d_lo_ref.shape[1]
    per_boxes = boxes // steps
    faces = index.shape[1]
    parents = boxes // 8
    par_rows = d_hi_ref.shape[0] // parents
    hi_lines = op_hi.shape[0] // types
    empty = par_rows // hi_lines - 1
    own = lax.axis_index("samp") * parents
    far_step = -(-far // steps)

    def counts(g):
        source = index[pl.ds(g, 1), :]
        kind = index[pl.ds(boxes + g, 1), :]
        by_source = jnp.where(iota((slot_total, faces), 0) == source, 1.0, 0.0).astype(BF16)
        by_type = jnp.where(iota((type_pad, faces), 0) == kind, 1.0, 0.0).astype(BF16)
        return dot_nt(by_source, by_type).astype(BF16)

    def step_boxes(step, carry):
        start = step * per_boxes
        tally = jnp.concatenate([counts(start + k) for k in range(per_boxes)], 0)
        summed = dot_nn(tally, op_lo[...]).astype(d_lo_ref.dtype)
        d_lo_ref[pl.ds(start, per_boxes)] = summed.reshape(
            per_boxes, slot_total, 2 * chunks * LANE
        )
        tile_copy(step).wait()
        for pair in range(per_step // 2):
            tile = step * per_step + 2 * pair
            both = tiles[pl.ds(tile, 2)]
            weights = jnp.concatenate(
                [both[:, 0].reshape(2 * LANE, LANE), both[:, 1].reshape(2 * LANE, LANE)], 1
            )
            owners, lefts, rights = [], [], []
            for h in range(2):
                entry = code[tile + h]
                row = pl.ds(pl.multiple_of((entry & 63) * 8, 8), 8)
                owners.append(entry >> 6)
                lefts.append(left[row])
                rights.append(right[row])
            lhs = jnp.concatenate([jnp.concatenate(lefts, 0), jnp.concatenate(rights, 0)], 1)
            product = dot_nt(lhs.astype(BF16), weights)
            for h in range(2):
                acc[owners[h]] = (
                    acc[owners[h]] + product[8 * h : 8 * (h + 1), h * LANE : (h + 1) * LANE]
                )
        for e in range(far_step):
            f = step * far_step + e
            inside = f < far
            f = jnp.minimum(f, far - 1)
            for p in range(parents):
                source = jnp.where(inside, par_far_ref[own + p, f], empty)
                kind = par_type_ref[own + p, f]
                at = pl.ds(pl.multiple_of(p * par_rows + source * hi_lines, hi_lines), hi_lines)
                term = op_hi[pl.ds(pl.multiple_of(kind * hi_lines, hi_lines), hi_lines)]
                d_hi_ref[at] = d_hi_ref[at] + term.astype(F32)
        return carry

    lax.fori_loop(0, steps, step_boxes, 0)
    for g in range(boxes):
        row = 2 * g
        near_ref[row : row + 2] = acc[g, 0:2] + 0.5 * dens3[pl.ds(2 * boxes + row, 2), :]


def last_kernel(
    arrived_ref,
    d_lo_ref,
    d_hi_ref,
    shift_hbm,
    interp_hbm,
    receive_ref,
    near_ref,
    out_ref,
    receive,
    shift_ref,
    interp_ref,
    slots,
    upward,
    down,
    incoming,
    blend,
    sems,
    extra,
):
    boxes = receive.shape[0]
    per_step = 4
    steps = boxes // per_step
    others = fetch([(shift_hbm, shift_ref), (interp_hbm, interp_ref)], extra)
    copies = []
    for step in range(steps):
        part = pl.ds(step * per_step, per_step)
        copies.append(pltpu.make_async_copy(receive_ref.at[part], receive.at[part], sems.at[step]))
        copies[-1].start()
    devices, lines, _ = arrived_ref.shape
    own_parents = boxes // 8
    slot_total = d_lo_ref.shape[1]
    chunks = d_lo_ref.shape[2] // (2 * LANE)
    lo_lines = slot_total // devices * 2 * chunks
    hi_lines = (lines - lo_lines) // own_parents
    hi_chunks = hi_lines // 2
    par_rows = d_hi_ref.shape[0] // own_parents
    slots[...] = arrived_ref[:, :lo_lines, :].astype(F32).reshape(devices * lo_lines, LANE)

    def gather(device, sums):
        for q in range(own_parents):
            line = lo_lines + q * hi_lines
            first = arrived_ref[device, line : line + hi_chunks].astype(F32)
            second = arrived_ref[device, line + hi_chunks : line + hi_lines].astype(F32)
            new = []
            for p in range(own_parents):
                row = p * par_rows + (device * own_parents + q) * hi_lines
                o_re = d_hi_ref[pl.ds(row, hi_chunks, stride=2), :]
                o_im = d_hi_ref[pl.ds(row + 1, hi_chunks, stride=2), :]
                new.append(sums[2 * p] + (o_re * first - o_im * second))
                new.append(sums[2 * p + 1] + (o_re * second + o_im * first))
            sums = tuple(new)
        return sums

    zero = jnp.zeros((hi_chunks, LANE), F32)
    sums = lax.fori_loop(0, devices, gather, (zero,) * (2 * own_parents), unroll=4)
    for k in range(2 * own_parents):
        upward[k * hi_chunks : (k + 1) * hi_chunks] = sums[k]
    others[0].wait()
    for r in range(hi_chunks):
        s_re = shift_ref[pl.ds(2 * r, 8, stride=2 * hi_chunks), :]
        s_im = shift_ref[pl.ds(2 * r + 1, 8, stride=2 * hi_chunks), :]
        re_rows, im_rows = [], []
        for p in range(own_parents):
            row = 2 * p * hi_chunks + r
            t_re = upward[row : row + 1]
            t_im = upward[row + hi_chunks : row + hi_chunks + 1]
            re_rows.append(s_re * t_re + s_im * t_im)
            im_rows.append(s_re * t_im - s_im * t_re)
        cols = slice(r * LANE, (r + 1) * LANE)
        down[:, cols] = jnp.concatenate(re_rows + im_rows, 0).astype(BF16)
    for r in range(chunks):
        first = slots[pl.ds(r, slot_total, stride=2 * chunks), :]
        second = slots[pl.ds(chunks + r, slot_total, stride=2 * chunks), :]
        for g in range(boxes):
            o_re = d_lo_ref[g, :, r * LANE : (r + 1) * LANE].astype(F32)
            o_im = d_lo_ref[g, :, (chunks + r) * LANE : (chunks + r + 1) * LANE].astype(F32)
            cols = slice(r * LANE, (r + 1) * LANE)
            incoming[g : g + 1, cols] = jnp.sum(o_re * first - o_im * second, 0, keepdims=True)
            incoming[boxes + g : boxes + g + 1, cols] = jnp.sum(
                o_re * second + o_im * first, 0, keepdims=True
            )
    others[1].wait()
    total = incoming[...] + dot_nt(down[...], interp_ref[...])
    total = total.astype(BF16).astype(F32)
    for r in range(chunks):
        re_part = total[:boxes, r * LANE : (r + 1) * LANE]
        im_part = total[boxes:, r * LANE : (r + 1) * LANE]
        blend[pl.ds(0, boxes, stride=2), r, :] = re_part
        blend[pl.ds(1, boxes, stride=2), r, :] = im_part
        blend[pl.ds(0, boxes, stride=2), chunks + r, :] = -im_part
        blend[pl.ds(1, boxes, stride=2), chunks + r, :] = re_part
    owner = (iota((2 * per_step, LANE), 0) // 2) % per_step
    for step in range(steps):
        rows = slice(step * 2 * per_step, (step + 1) * 2 * per_step)
        lhs = jnp.concatenate([blend[rows, r, :] for r in range(2 * chunks)], 1).astype(BF16)
        copies[step].wait()
        weights = receive[step * per_step : (step + 1) * per_step]
        product = dot_nt(lhs, weights.reshape(per_step * LANE, 2 * chunks * LANE))
        total = near_ref[rows]
        for b in range(per_step):
            total = total + jnp.where(owner == b, product[:, b * LANE : (b + 1) * LANE], 0.0)
        out_ref[rows] = total


def in_hbm(array):
    return pltpu.with_memory_space_constraint(array, pltpu.HBM)


def in_vmem(array):
    return pltpu.with_memory_space_constraint(array, pltpu.VMEM)


def tiled_rows(array):
    count, parts, width = array.shape
    cut = array.reshape(count, parts, width // LANE, LANE)
    return cut.transpose(0, 2, 1, 3).reshape(-1, LANE)


def on_device(
    density,
    radiate,
    receive,
    near_tiles,
    near_src,
    near_tile,
    send_box,
    distant_pattern_slot,
    far_type,
    trans_lo,
    interp_matrix,
    shifts,
    par_far,
    par_type,
    trans_hi,
):
    boxes, _, panels = density.shape
    devices = lax.axis_size("box") * lax.axis_size("samp")
    slots = send_box.shape[2]
    types, _, width_lo = trans_lo.shape
    width_hi = trans_hi.shape[2]
    parents = boxes // 8
    slot_total = devices * slots
    par_total = devices * parents
    type_pad = -(-types // 8) * 8
    lines = slots * 2 * width_lo // LANE + parents * 2 * width_hi // LANE
    held = F32 if slot_total <= 128 else BF16
    rows = density.reshape(boxes * 2, panels)
    lower = shifted(rows, ("box", "samp"), 1)
    upper = shifted(rows, ("box", "samp"), -1)
    shift_rows = tiled_rows(shifts)
    mid = rows
    send = send_box[0].T
    outgoing = pl.pallas_call(
        radiate_kernel,
        out_shape=jax.ShapeDtypeStruct((devices, lines, LANE), BF16),
        in_specs=[HBM_SPEC] * 5,
        out_specs=VMEM_SPEC,
        scratch_shapes=[
            pltpu.VMEM(radiate.shape, BF16),
            pltpu.VMEM(rows.shape, BF16),
            pltpu.SMEM(send.shape, jnp.int32),
            pltpu.VMEM(interp_matrix.shape, BF16),
            pltpu.VMEM(shift_rows.shape, F32),
            pltpu.VMEM((2 * boxes, 2 * width_lo // LANE, LANE), F32),
            pltpu.VMEM((boxes * 8 + 8, LANE), F32),
            pltpu.VMEM((parents * 2 * width_hi // LANE, LANE), F32),
            pltpu.SemaphoreType.DMA((boxes // 4,)),
            pltpu.SemaphoreType.DMA((4,)),
        ],
        compiler_params=pltpu.CompilerParams(vmem_limit_bytes=12 * MIB),
        cost_estimate=pl.CostEstimate(flops=10**9, bytes_accessed=8 * MIB, transcendentals=0),
    )(*(in_hbm(x) for x in (rows, radiate, send, interp_matrix, shift_rows)))
    outgoing, lower, upper = lax.optimization_barrier((outgoing, lower, upper))
    arrived = lax.all_to_all(outgoing, ("box", "samp"), split_axis=0, concat_axis=0, tiled=True)
    tile_count = near_tiles.shape[0]
    far = far_type.shape
    par_shape = par_far.shape
    op_hi_rows = tiled_rows(trans_hi)
    op_lo_rows = tiled_rows(trans_lo)
    hi_lines = 2 * width_hi // LANE
    near, d_lo, d_hi = pl.pallas_call(
        functools.partial(middle_kernel, types, boxes * devices),
        out_shape=(
            pltpu.VMEM((2 * boxes, panels), F32),
            pltpu.VMEM((boxes, slot_total, 2 * width_lo), held),
            pltpu.VMEM((parents * (par_total + 1) * hi_lines, LANE), F32),
        ),
        in_specs=[ANY_SPEC, HBM_SPEC, ANY_SPEC] + [HBM_SPEC] * 9,
        out_specs=(VMEM_SPEC,) * 3,
        scratch_shapes=[
            pltpu.VMEM(near_tiles.shape, BF16),
            pltpu.VMEM((3, 2 * boxes, panels), BF16),
            pltpu.SMEM(near_src.shape, jnp.int32),
            pltpu.SMEM(near_src.shape, jnp.int32),
            pltpu.VMEM(far, jnp.int32),
            pltpu.VMEM(far, jnp.int32),
            pltpu.VMEM(op_lo_rows.shape, BF16),
            pltpu.SMEM(par_shape, jnp.int32),
            pltpu.SMEM(par_shape, jnp.int32),
            pltpu.VMEM(op_hi_rows.shape, BF16),
            pltpu.VMEM((6 * boxes, panels), F32),
            pltpu.VMEM((3 * boxes * 8, LANE), F32),
            pltpu.VMEM((3 * boxes * 8, LANE), F32),
            pltpu.VMEM((boxes, 8, LANE), F32),
            pltpu.SMEM((tile_count + 8,), jnp.int32),
            pltpu.VMEM((2 * boxes, 2 * LANE), jnp.int32),
            pltpu.VMEM((type_pad * 2 * width_lo // LANE, LANE), F32),
            pltpu.VMEM((type_pad, 2 * width_lo), BF16),
            pltpu.SemaphoreType.DMA((4,)),
            pltpu.SemaphoreType.DMA((11,)),
        ],
        compiler_params=pltpu.CompilerParams(vmem_limit_bytes=28 * MIB),
        cost_estimate=pl.CostEstimate(flops=10**10, bytes_accessed=20 * MIB, transcendentals=0),
    )(
        lower,
        mid,
        upper,
        near_src,
        near_tile,
        near_tiles,
        distant_pattern_slot,
        far_type,
        op_lo_rows,
        par_far,
        par_type,
        op_hi_rows,
    )
    lo_lines = slots * 2 * width_lo // LANE
    field = pl.pallas_call(
        last_kernel,
        out_shape=jax.ShapeDtypeStruct((2 * boxes, panels), F32),
        in_specs=[VMEM_SPEC] * 3 + [HBM_SPEC] * 3 + [VMEM_SPEC],
        out_specs=VMEM_SPEC,
        scratch_shapes=[
            pltpu.VMEM(receive.shape, BF16),
            pltpu.VMEM(shift_rows.shape, F32),
            pltpu.VMEM(interp_matrix.shape, BF16),
            pltpu.VMEM((devices * lo_lines, LANE), F32),
            pltpu.VMEM((parents * hi_lines, LANE), F32),
            pltpu.VMEM((2 * boxes, width_hi), BF16),
            pltpu.VMEM((2 * boxes, width_lo), F32),
            pltpu.VMEM((2 * boxes, 2 * width_lo // LANE, LANE), F32),
            pltpu.SemaphoreType.DMA((boxes // 4,)),
            pltpu.SemaphoreType.DMA((2,)),
        ],
        compiler_params=pltpu.CompilerParams(vmem_limit_bytes=12 * MIB),
        cost_estimate=pl.CostEstimate(flops=10**9, bytes_accessed=8 * MIB, transcendentals=0),
    )(arrived, in_vmem(d_lo), in_vmem(d_hi), shift_rows, interp_matrix, receive, near)
    return field.reshape(boxes, 2, panels)


def solution(mesh):
    both = ("box", "samp")
    return jax.shard_map(
        on_device,
        mesh=mesh,
        in_specs=(
            P(both, None, None),
            P(both, None, None),
            P(both, None, None),
            P(both, None, None, None),
            P(both, None),
            P(both, None),
            P(both, None, None),
            P(both, None),
            P(both, None),
            P(),
            P(),
            P(),
            P("box", None),
            P("box", None),
            P(),
        ),
        out_specs=P(both, None, None),
        check_vma=False,
    )
```

```python
import functools

import jax
import jax.numpy as jnp
from jax import lax
from jax.experimental import pallas as pl
from jax.experimental.pallas import tpu as pltpu
from jax.sharding import PartitionSpec as P

F32 = jnp.float32
BF16 = jnp.bfloat16
LANE = 128
VMEM_SPEC = pl.BlockSpec(memory_space=pltpu.VMEM)
SMEM_SPEC = pl.BlockSpec(memory_space=pltpu.SMEM)
ANY_SPEC = pl.BlockSpec(memory_space=pl.ANY)
HBM_SPEC = pl.BlockSpec(memory_space=pltpu.HBM)
MIB = 1 << 20


def iota(shape, dim):
    return lax.broadcasted_iota(jnp.int32, shape, dim)


def dot_nn(lhs, rhs):
    return lax.dot_general(lhs, rhs, (((1,), (0,)), ((), ())), preferred_element_type=F32)


def dot_nt(lhs, rhs):
    return lax.dot_general(lhs, rhs, (((1,), (1,)), ((), ())), preferred_element_type=F32)


def shifted(value, axis, steps):
    count = lax.axis_size(axis)
    first, last = (max(0, -steps), min(count, count - steps))
    return lax.ppermute(value, axis, [(source, source + steps) for source in range(first, last)])


def fetch(pairs, sems, first=0):
    copies = []
    for k, (source, target) in enumerate(pairs):
        copies.append(pltpu.make_async_copy(source, target, sems.at[first + k]))
        copies[-1].start()
    return copies


def radiate_kernel(
    group,
    dens_hbm,
    radiate_ref,
    send_hbm,
    interp_hbm,
    shift_hbm,
    out_ref,
    rad,
    dens_ref,
    send_ref,
    interp_ref,
    shift_ref,
    summed,
    table,
    parent,
    sems,
    extra,
):
    boxes = rad.shape[0]
    width = rad.shape[2] // 2
    per_step = 4
    steps = boxes // per_step
    others = fetch(
        [(dens_hbm, dens_ref), (send_hbm, send_ref), (shift_hbm, shift_ref)], extra
    )
    copies = []
    for step in range(steps):
        part = pl.ds(step * per_step, per_step)
        copies.append(pltpu.make_async_copy(radiate_ref.at[part], rad.at[part], sems.at[step]))
        copies[-1].start()
    others += fetch([(interp_hbm, interp_ref)], extra, 3)
    others[0].wait()
    dens = dens_ref[...].astype(F32)
    owner = (iota(dens.shape, 0) // 2) % per_step
    blocks = jnp.concatenate([jnp.where(owner == b, dens, 0.0) for b in range(per_step)], 1)
    for step in range(steps):
        copies[step].wait()
        rows = slice(step * 2 * per_step, (step + 1) * 2 * per_step)
        weights = rad[step * per_step : (step + 1) * per_step].reshape(per_step * LANE, 2 * width)
        summed[rows] = dot_nn(blocks[rows].astype(BF16), weights).reshape(
            2 * per_step, 2 * width // LANE, LANE
        )
    chunks = width // LANE
    re_chunks, im_chunks = [], []
    for r in range(chunks):
        first_lo = summed[pl.ds(0, boxes, stride=2), r, :]
        first_hi = summed[pl.ds(0, boxes, stride=2), chunks + r, :]
        second_lo = summed[pl.ds(1, boxes, stride=2), r, :]
        second_hi = summed[pl.ds(1, boxes, stride=2), chunks + r, :]
        re_chunks.append((first_lo - second_hi).astype(BF16))
        im_chunks.append((first_hi + second_lo).astype(BF16))
    re_part = jnp.concatenate(re_chunks, 1)
    im_part = jnp.concatenate(im_chunks, 1)
    for r in range(chunks):
        table[pl.ds(r, boxes, stride=8), :] = re_chunks[r].astype(F32)
        table[pl.ds(chunks + r, boxes, stride=8), :] = im_chunks[r].astype(F32)
    table[pl.ds(boxes * 8, 8), :] = jnp.zeros((8, LANE), F32)
    for copy in others[1:]:
        copy.wait()
    wide = dot_nn(jnp.concatenate([re_part, im_part], 0), interp_ref[...])
    hi_chunks = wide.shape[1] // LANE
    parents = boxes // 8
    share = hi_chunks // group
    for r in range(hi_chunks):
        cols = slice(r * LANE, (r + 1) * LANE)
        s_re = shift_ref[pl.ds(2 * r, 8, stride=2 * hi_chunks), :]
        s_im = shift_ref[pl.ds(2 * r + 1, 8, stride=2 * hi_chunks), :]
        for p in range(parents):
            w_re = wide[p * 8 : (p + 1) * 8, cols]
            w_im = wide[boxes + p * 8 : boxes + (p + 1) * 8, cols]
            row = ((r // share) * parents + p) * 2 * share + r % share
            parent[row : row + 1] = jnp.sum(w_re * s_re - w_im * s_im, 0, keepdims=True)
            row += share
            parent[row : row + 1] = jnp.sum(w_re * s_im + w_im * s_re, 0, keepdims=True)
    slots, devices = send_ref.shape
    hi_rows = parents * 2 * share

    def fill(d, carry):
        for k in range(slots // 2):
            pair = [
                table[pl.ds(pl.multiple_of(send_ref[2 * k + h, d] * 8, 8), 8), :] for h in range(2)
            ]
            out_ref[d, 16 * k : 16 * (k + 1)] = jnp.concatenate(pair, 0).astype(BF16)
        member = pl.multiple_of(lax.rem(d, group) * hi_rows, 8)
        out_ref[d, 8 * slots : 8 * slots + hi_rows] = parent[pl.ds(member, hi_rows)].astype(BF16)
        return carry

    lax.fori_loop(0, devices, fill, 0)


def tally(index, source_row, type_row, sources, types):
    source = index[pl.ds(source_row, 1), :]
    kind = index[pl.ds(type_row, 1), :]
    faces = index.shape[1]
    by_source = jnp.where(iota((sources, faces), 0) == source, 1.0, 0.0).astype(BF16)
    by_type = jnp.where(iota((types, faces), 0) == kind, 1.0, 0.0).astype(BF16)
    return dot_nt(by_source, by_type).astype(BF16)


def parent_operator_kernel(
    types,
    group,
    par_far_hbm,
    par_type_hbm,
    op_hbm,
    d_ref,
    par_far_ref,
    par_type_ref,
    op_ref,
    index,
    wide,
    op,
    extra,
):
    others = fetch(
        [(par_far_hbm, par_far_ref), (par_type_hbm, par_type_ref), (op_hbm, op_ref)], extra
    )
    rows, far = par_far_ref.shape
    lines = op_ref.shape[0] // types
    share = lines // (2 * group)
    type_pad = op.shape[0]
    samp = lax.axis_index("samp")
    member = lax.rem(samp, group)
    first_parent = (samp - member) * (d_ref.shape[0] // group)
    place = member * (2 * share)
    base = place // 16 * 16
    index[...] = jnp.full(index.shape, -1, jnp.int32)
    wide[types * 16 : type_pad * 16] = jnp.zeros(((type_pad - types) * 16, LANE), F32)
    others[0].wait()
    others[1].wait()
    index[0:rows, 0:far] = par_far_ref[...]
    index[rows : 2 * rows, 0:far] = par_type_ref[...]
    others[2].wait()

    def widen(t, carry):
        source = pl.ds(pl.multiple_of(t * lines + base, 16), 16)
        wide[pl.ds(pl.multiple_of(t * 16, 16), 16)] = op_ref[source].astype(F32)
        return carry

    lax.fori_loop(0, types, widen, 0, unroll=4)
    for c in range(2):
        for k in range(share):
            col = (c * share + k) * LANE
            start = place - base + 2 * k + c
            op[:, col : col + LANE] = wide[pl.ds(start, type_pad, stride=16), :].astype(BF16)
    parents, sources, _ = d_ref.shape
    per_step = 4

    def step_parents(step, carry):
        start = step * per_step
        counts = jnp.concatenate(
            [
                tally(
                    index,
                    first_parent + start + k,
                    rows + first_parent + start + k,
                    sources,
                    type_pad,
                )
                for k in range(per_step)
            ],
            0,
        )
        d_ref[pl.ds(start, per_step)] = dot_nn(counts, op[...]).reshape(
            per_step, sources, 2 * share * LANE
        )
        return carry

    lax.fori_loop(0, parents // per_step, step_parents, 0)


def parent_kernel(lo_lines, arrived_ref, d_ref, out_ref, wide):
    parents, sources, width = d_ref.shape
    share = width // (2 * LANE)
    rows = out_ref.shape[1]
    wide[...] = arrived_ref[:, lo_lines:, :].astype(F32).reshape(wide.shape)
    for k in range(share):
        first = wide[pl.ds(k, sources, stride=2 * share), :]
        second = wide[pl.ds(share + k, sources, stride=2 * share), :]
        for p in range(parents):
            o_re = d_ref[p, :, k * LANE : (k + 1) * LANE]
            o_im = d_ref[p, :, (share + k) * LANE : (share + k + 1) * LANE]
            row = p * 2 * share + k
            to, row = row // rows, row % rows
            out_ref[to, row : row + 1] = jnp.sum(o_re * first - o_im * second, 0, keepdims=True)
            row += share
            out_ref[to, row : row + 1] = jnp.sum(o_re * second + o_im * first, 0, keepdims=True)


def middle_kernel(
    types,
    box_total,
    lower_hbm,
    dens_hbm,
    upper_hbm,
    near_src_hbm,
    near_tile_hbm,
    tiles_hbm,
    slot_hbm,
    type_hbm,
    op_lo_hbm,
    arrived_ref,
    near_ref,
    incoming_ref,
    tiles,
    halo,
    near_src_ref,
    near_tile_ref,
    slot_ref,
    type_ref,
    op_lo_ref,
    dens3,
    left,
    right,
    acc,
    code,
    index,
    wide_op,
    op_lo,
    summed,
    slots,
    sems,
    extra,
):
    boxes, near = near_src_ref.shape
    tile_count = tiles.shape[0]
    steps = sems.shape[0]
    per_step = tile_count // steps
    others = fetch(
        [
            (near_src_hbm, near_src_ref),
            (near_tile_hbm, near_tile_ref),
            (op_lo_hbm, op_lo_ref),
            (slot_hbm, slot_ref),
            (type_hbm, type_ref),
            (lower_hbm, halo.at[0]),
            (dens_hbm, halo.at[1]),
            (upper_hbm, halo.at[2]),
        ],
        extra,
    )

    def tile_copy(step):
        part = pl.ds(step * per_step, per_step)
        return pltpu.make_async_copy(tiles_hbm.at[part], tiles.at[part], sems.at[step])

    for step in range(steps):
        tile_copy(step).start()
    position = lax.axis_index("box") * lax.axis_size("samp") + lax.axis_index("samp")
    acc[...] = jnp.zeros(acc.shape, F32)
    index[...] = jnp.full(index.shape, -1, jnp.int32)
    left[...] = jnp.zeros(left.shape, F32)
    right[...] = jnp.zeros(right.shape, F32)
    type_pad = op_lo.shape[0]
    chunks = op_lo.shape[1] // (2 * LANE)
    wide_op[types * 2 * chunks : type_pad * 2 * chunks] = jnp.zeros(
        ((type_pad - types) * 2 * chunks, LANE), F32
    )
    others[0].wait()
    others[1].wait()

    def locate(g, carry):
        for n in range(near):
            source = near_src_ref[g, n]
            live = source < box_total
            tile = jnp.where(live, near_tile_ref[g, n] - position * tile_count, tile_count)
            code[tile] = g * 64 + source - (position - 1) * boxes
        return carry

    lax.fori_loop(0, boxes, locate, 0)

    for copy in others[2:]:
        copy.wait()
    wide_op[0 : types * 2 * chunks] = op_lo_ref[...].astype(F32)
    for c in range(2):
        for r in range(chunks):
            col = (c * chunks + r) * LANE
            op_lo[:, col : col + LANE] = wide_op[
                pl.ds(2 * r + c, type_pad, stride=2 * chunks), :
            ].astype(BF16)
    far = slot_ref.shape[1]
    index[0:boxes, 0:far] = slot_ref[...]
    index[boxes : 2 * boxes, 0:far] = type_ref[...]
    for k in range(3):
        dens3[pl.ds(2 * boxes * k, 2 * boxes), :] = halo[k].astype(F32)
    first = dens3[pl.ds(0, 3 * boxes, stride=2), :]
    second = dens3[pl.ds(1, 3 * boxes, stride=2), :]
    left[pl.ds(0, 3 * boxes, stride=8), :] = first
    left[pl.ds(1, 3 * boxes, stride=8), :] = second
    right[pl.ds(0, 3 * boxes, stride=8), :] = -second
    right[pl.ds(1, 3 * boxes, stride=8), :] = first

    lo_lines = slots.shape[0] // arrived_ref.shape[0]
    slots[...] = arrived_ref[:, :lo_lines, :].astype(F32).reshape(slots.shape)
    slot_total = slots.shape[0] // (2 * chunks)
    per_boxes = boxes // steps

    def step_boxes(step, carry):
        start = step * per_boxes
        counts = jnp.concatenate(
            [
                tally(index, start + k, boxes + start + k, slot_total, type_pad)
                for k in range(per_boxes)
            ],
            0,
        )
        summed[...] = dot_nn(counts, op_lo[...])
        tile_copy(step).wait()
        for pair in range(per_step // 2):
            tile = step * per_step + 2 * pair
            both = tiles[pl.ds(tile, 2)]
            weights = jnp.concatenate(
                [both[:, 0].reshape(2 * LANE, LANE), both[:, 1].reshape(2 * LANE, LANE)], 1
            )
            owners, lefts, rights = [], [], []
            for h in range(2):
                entry = code[tile + h]
                row = pl.ds(pl.multiple_of((entry & 63) * 8, 8), 8)
                owners.append(entry >> 6)
                lefts.append(left[row])
                rights.append(right[row])
            lhs = jnp.concatenate([jnp.concatenate(lefts, 0), jnp.concatenate(rights, 0)], 1)
            product = dot_nt(lhs.astype(BF16), weights)
            for h in range(2):
                acc[owners[h]] = (
                    acc[owners[h]] + product[8 * h : 8 * (h + 1), h * LANE : (h + 1) * LANE]
                )
        for r in range(chunks):
            cols = slice(r * LANE, (r + 1) * LANE)
            first = slots[pl.ds(r, slot_total, stride=2 * chunks), :]
            second = slots[pl.ds(chunks + r, slot_total, stride=2 * chunks), :]
            for k in range(per_boxes):
                part = slice(k * slot_total, (k + 1) * slot_total)
                o_re = summed[part, cols]
                o_im = summed[part, (chunks + r) * LANE : (chunks + r + 1) * LANE]
                incoming_ref[start + k, r : r + 1] = jnp.sum(
                    o_re * first - o_im * second, 0, keepdims=True
                )
                incoming_ref[boxes + start + k, r : r + 1] = jnp.sum(
                    o_re * second + o_im * first, 0, keepdims=True
                )
        return carry

    lax.fori_loop(0, steps, step_boxes, 0)
    for g in range(boxes):
        row = 2 * g
        near_ref[row : row + 2] = acc[g, 0:2] + 0.5 * dens3[pl.ds(2 * boxes + row, 2), :]


def last_kernel(
    parent_ref,
    incoming_ref,
    shift_hbm,
    interp_hbm,
    receive_ref,
    near_ref,
    out_ref,
    receive,
    shift_ref,
    interp_ref,
    down,
    blend,
    sems,
    extra,
):
    boxes = receive.shape[0]
    per_step = 4
    steps = boxes // per_step
    others = fetch([(shift_hbm, shift_ref), (interp_hbm, interp_ref)], extra)
    copies = []
    for step in range(steps):
        part = pl.ds(step * per_step, per_step)
        copies.append(pltpu.make_async_copy(receive_ref.at[part], receive.at[part], sems.at[step]))
        copies[-1].start()
    own_parents = boxes // 8
    hi_chunks = down.shape[1] // LANE
    chunks = incoming_ref.shape[1]
    share = hi_chunks // parent_ref.shape[0]
    others[0].wait()
    for r in range(hi_chunks):
        s_re = shift_ref[pl.ds(2 * r, 8, stride=2 * hi_chunks), :]
        s_im = shift_ref[pl.ds(2 * r + 1, 8, stride=2 * hi_chunks), :]
        re_rows, im_rows = [], []
        for p in range(own_parents):
            row = p * 2 * share + r % share
            t_re = parent_ref[r // share, row : row + 1]
            t_im = parent_ref[r // share, row + share : row + share + 1]
            re_rows.append(s_re * t_re + s_im * t_im)
            im_rows.append(s_re * t_im - s_im * t_re)
        cols = slice(r * LANE, (r + 1) * LANE)
        down[:, cols] = jnp.concatenate(re_rows + im_rows, 0).astype(BF16)
    others[1].wait()
    total = jnp.concatenate([incoming_ref[:, r, :] for r in range(chunks)], 1)
    total = total + dot_nt(down[...], interp_ref[...])
    total = total.astype(BF16).astype(F32)
    for r in range(chunks):
        re_part = total[:boxes, r * LANE : (r + 1) * LANE]
        im_part = total[boxes:, r * LANE : (r + 1) * LANE]
        blend[pl.ds(0, boxes, stride=2), r, :] = re_part
        blend[pl.ds(1, boxes, stride=2), r, :] = im_part
        blend[pl.ds(0, boxes, stride=2), chunks + r, :] = -im_part
        blend[pl.ds(1, boxes, stride=2), chunks + r, :] = re_part
    owner = (iota((2 * per_step, LANE), 0) // 2) % per_step
    for step in range(steps):
        rows = slice(step * 2 * per_step, (step + 1) * 2 * per_step)
        lhs = jnp.concatenate([blend[rows, r, :] for r in range(2 * chunks)], 1).astype(BF16)
        copies[step].wait()
        weights = receive[step * per_step : (step + 1) * per_step]
        product = dot_nt(lhs, weights.reshape(per_step * LANE, 2 * chunks * LANE))
        total = near_ref[rows]
        for b in range(per_step):
            total = total + jnp.where(owner == b, product[:, b * LANE : (b + 1) * LANE], 0.0)
        out_ref[rows] = total


def in_hbm(array):
    return pltpu.with_memory_space_constraint(array, pltpu.HBM)


def in_vmem(array):
    return pltpu.with_memory_space_constraint(array, pltpu.VMEM)


def tiled_rows(array):
    count, parts, width = array.shape
    cut = array.reshape(count, parts, width // LANE, LANE)
    return cut.transpose(0, 2, 1, 3).reshape(-1, LANE)


def on_device(
    density,
    radiate,
    receive,
    near_tiles,
    near_src,
    near_tile,
    send_box,
    distant_pattern_slot,
    far_type,
    trans_lo,
    interp_matrix,
    shifts,
    par_far,
    par_type,
    trans_hi,
):
    boxes, _, panels = density.shape
    devices = lax.axis_size("box") * lax.axis_size("samp")
    slots = send_box.shape[2]
    types, _, width_lo = trans_lo.shape
    width_hi = trans_hi.shape[2]
    parents = boxes // 8
    slot_total = devices * slots
    par_total = devices * parents
    type_pad = -(-types // 8) * 8
    samp_count = lax.axis_size("samp")
    group = min(samp_count, 8)
    share = width_hi // LANE // group
    lo_lines = slots * 2 * width_lo // LANE
    hi_lines = parents * 2 * share
    lines = lo_lines + hi_lines
    members = None
    if group < samp_count:
        members = [list(range(k, k + group)) for k in range(0, samp_count, group)]
    rows = density.reshape(boxes * 2, panels)
    shift_rows = tiled_rows(shifts)
    send = send_box[0].T
    outgoing = pl.pallas_call(
        functools.partial(radiate_kernel, group),
        out_shape=jax.ShapeDtypeStruct((devices, lines, LANE), BF16),
        in_specs=[HBM_SPEC] * 5,
        out_specs=VMEM_SPEC,
        scratch_shapes=[
            pltpu.VMEM(radiate.shape, BF16),
            pltpu.VMEM(rows.shape, BF16),
            pltpu.SMEM(send.shape, jnp.int32),
            pltpu.VMEM(interp_matrix.shape, BF16),
            pltpu.VMEM(shift_rows.shape, F32),
            pltpu.VMEM((2 * boxes, 2 * width_lo // LANE, LANE), F32),
            pltpu.VMEM((boxes * 8 + 8, LANE), F32),
            pltpu.VMEM((parents * 2 * width_hi // LANE, LANE), F32),
            pltpu.SemaphoreType.DMA((boxes // 4,)),
            pltpu.SemaphoreType.DMA((4,)),
        ],
        compiler_params=pltpu.CompilerParams(vmem_limit_bytes=12 * MIB),
        cost_estimate=pl.CostEstimate(flops=10**9, bytes_accessed=8 * MIB, transcendentals=0),
    )(*(in_hbm(x) for x in (rows, radiate, send, interp_matrix, shift_rows)))
    outgoing, near_rows = lax.optimization_barrier((outgoing, rows))
    arrived = lax.all_to_all(outgoing, ("box", "samp"), split_axis=0, concat_axis=0, tiled=True)
    lower = shifted(near_rows, ("box", "samp"), 1)
    upper = shifted(near_rows, ("box", "samp"), -1)
    tile_count = near_tiles.shape[0]
    far = far_type.shape
    op_hi_rows = tiled_rows(trans_hi)
    op_lo_rows = tiled_rows(trans_lo)
    d_hi = pl.pallas_call(
        functools.partial(parent_operator_kernel, types, group),
        out_shape=pltpu.VMEM((parents * group, par_total, 2 * share * LANE), F32),
        in_specs=[HBM_SPEC] * 3,
        out_specs=VMEM_SPEC,
        scratch_shapes=[
            pltpu.VMEM(par_far.shape, jnp.int32),
            pltpu.VMEM(par_far.shape, jnp.int32),
            pltpu.VMEM(op_hi_rows.shape, BF16),
            pltpu.VMEM((2 * par_far.shape[0], 2 * LANE), jnp.int32),
            pltpu.VMEM((type_pad * 16, LANE), F32),
            pltpu.VMEM((type_pad, 2 * share * LANE), BF16),
            pltpu.SemaphoreType.DMA((3,)),
        ],
        compiler_params=pltpu.CompilerParams(vmem_limit_bytes=12 * MIB),
        cost_estimate=pl.CostEstimate(flops=10**9, bytes_accessed=8 * MIB, transcendentals=0),
    )(*(in_hbm(x) for x in (par_far, par_type, op_hi_rows)))
    above = pl.pallas_call(
        functools.partial(parent_kernel, lo_lines),
        out_shape=jax.ShapeDtypeStruct((group, hi_lines, LANE), F32),
        in_specs=[VMEM_SPEC] * 2,
        out_specs=VMEM_SPEC,
        scratch_shapes=[pltpu.VMEM((devices * hi_lines, LANE), F32)],
        compiler_params=pltpu.CompilerParams(vmem_limit_bytes=4 * MIB),
        cost_estimate=pl.CostEstimate(flops=10**8, bytes_accessed=MIB, transcendentals=0),
    )(arrived, in_vmem(d_hi))
    above, lower, upper = lax.optimization_barrier((above, lower, upper))
    own_above = lax.all_to_all(
        above, "samp", split_axis=0, concat_axis=0, axis_index_groups=members, tiled=True
    )
    steps = 4
    near, incoming = pl.pallas_call(
        functools.partial(middle_kernel, types, boxes * devices),
        out_shape=(
            jax.ShapeDtypeStruct((2 * boxes, panels), F32),
            jax.ShapeDtypeStruct((2 * boxes, width_lo // LANE, LANE), F32),
        ),
        in_specs=[ANY_SPEC, HBM_SPEC, ANY_SPEC] + [HBM_SPEC] * 6 + [VMEM_SPEC],
        out_specs=(VMEM_SPEC,) * 2,
        scratch_shapes=[
            pltpu.VMEM(near_tiles.shape, BF16),
            pltpu.VMEM((3, 2 * boxes, panels), BF16),
            pltpu.SMEM(near_src.shape, jnp.int32),
            pltpu.SMEM(near_src.shape, jnp.int32),
            pltpu.VMEM(far, jnp.int32),
            pltpu.VMEM(far, jnp.int32),
            pltpu.VMEM(op_lo_rows.shape, BF16),
            pltpu.VMEM((6 * boxes, panels), F32),
            pltpu.VMEM((3 * boxes * 8, LANE), F32),
            pltpu.VMEM((3 * boxes * 8, LANE), F32),
            pltpu.VMEM((boxes, 8, LANE), F32),
            pltpu.SMEM((tile_count + 8,), jnp.int32),
            pltpu.VMEM((2 * boxes, 2 * LANE), jnp.int32),
            pltpu.VMEM((type_pad * 2 * width_lo // LANE, LANE), F32),
            pltpu.VMEM((type_pad, 2 * width_lo), BF16),
            pltpu.VMEM((boxes // steps * slot_total, 2 * width_lo), F32),
            pltpu.VMEM((devices * lo_lines, LANE), F32),
            pltpu.SemaphoreType.DMA((steps,)),
            pltpu.SemaphoreType.DMA((8,)),
        ],
        compiler_params=pltpu.CompilerParams(vmem_limit_bytes=(24 if slot_total <= 128 else 40) * MIB),
        cost_estimate=pl.CostEstimate(flops=10**10, bytes_accessed=20 * MIB, transcendentals=0),
    )(
        lower,
        in_hbm(rows),
        upper,
        *(
            in_hbm(x)
            for x in (
                near_src,
                near_tile,
                near_tiles,
                distant_pattern_slot,
                far_type,
                op_lo_rows,
            )
        ),
        arrived,
    )
    field = pl.pallas_call(
        last_kernel,
        out_shape=jax.ShapeDtypeStruct((2 * boxes, panels), F32),
        in_specs=[VMEM_SPEC] * 2 + [HBM_SPEC] * 3 + [VMEM_SPEC],
        out_specs=VMEM_SPEC,
        scratch_shapes=[
            pltpu.VMEM(receive.shape, BF16),
            pltpu.VMEM(shift_rows.shape, F32),
            pltpu.VMEM(interp_matrix.shape, BF16),
            pltpu.VMEM((2 * boxes, width_hi), BF16),
            pltpu.VMEM((2 * boxes, 2 * width_lo // LANE, LANE), F32),
            pltpu.SemaphoreType.DMA((boxes // 4,)),
            pltpu.SemaphoreType.DMA((2,)),
        ],
        compiler_params=pltpu.CompilerParams(vmem_limit_bytes=12 * MIB),
        cost_estimate=pl.CostEstimate(flops=10**9, bytes_accessed=8 * MIB, transcendentals=0),
    )(own_above, incoming, shift_rows, interp_matrix, receive, near)
    return field.reshape(boxes, 2, panels)


def solution(mesh):
    both = ("box", "samp")
    return jax.shard_map(
        on_device,
        mesh=mesh,
        in_specs=(
            P(both, None, None),
            P(both, None, None),
            P(both, None, None),
            P(both, None, None, None),
            P(both, None),
            P(both, None),
            P(both, None, None),
            P(both, None),
            P(both, None),
            P(),
            P(),
            P(),
            P("box", None),
            P("box", None),
            P(),
        ),
        out_specs=P(both, None, None),
        check_vma=False,
    )
```

```python
import functools

import jax
import jax.numpy as jnp
from jax import lax
from jax.experimental import pallas as pl
from jax.experimental.pallas import tpu as pltpu
from jax.sharding import PartitionSpec as P

F32 = jnp.float32
BF16 = jnp.bfloat16
LANE = 128
VMEM_SPEC = pl.BlockSpec(memory_space=pltpu.VMEM)
SMEM_SPEC = pl.BlockSpec(memory_space=pltpu.SMEM)
ANY_SPEC = pl.BlockSpec(memory_space=pl.ANY)
HBM_SPEC = pl.BlockSpec(memory_space=pltpu.HBM)
MIB = 1 << 20


def iota(shape, dim):
    return lax.broadcasted_iota(jnp.int32, shape, dim)


def dot_nn(lhs, rhs):
    return lax.dot_general(lhs, rhs, (((1,), (0,)), ((), ())), preferred_element_type=F32)


def dot_nt(lhs, rhs):
    return lax.dot_general(lhs, rhs, (((1,), (1,)), ((), ())), preferred_element_type=F32)


def exchanged(value, axes, first):
    count = lax.axis_size(axes)
    pairs = []
    for low in range(first, count - 1, 2):
        pairs += [(low, low + 1), (low + 1, low)]
    return lax.ppermute(value, axes, pairs)


def fetch(pairs, sems, first=0):
    copies = []
    for k, (source, target) in enumerate(pairs):
        copies.append(pltpu.make_async_copy(source, target, sems.at[first + k]))
        copies[-1].start()
    return copies


def radiate_kernel(
    group,
    dens_hbm,
    radiate_ref,
    send_hbm,
    interp_hbm,
    shift_hbm,
    out_ref,
    rad,
    dens_ref,
    send_ref,
    interp_ref,
    shift_ref,
    summed,
    table,
    parent,
    sems,
    extra,
):
    boxes = rad.shape[0]
    width = rad.shape[2] // 2
    per_step = 4
    steps = boxes // per_step
    others = fetch(
        [(dens_hbm, dens_ref), (send_hbm, send_ref), (shift_hbm, shift_ref)], extra
    )
    copies = []
    for step in range(steps):
        part = pl.ds(step * per_step, per_step)
        copies.append(pltpu.make_async_copy(radiate_ref.at[part], rad.at[part], sems.at[step]))
        copies[-1].start()
    others += fetch([(interp_hbm, interp_ref)], extra, 3)
    others[0].wait()
    dens = dens_ref[...].astype(F32)
    owner = (iota(dens.shape, 0) // 2) % per_step
    blocks = jnp.concatenate([jnp.where(owner == b, dens, 0.0) for b in range(per_step)], 1)
    for step in range(steps):
        copies[step].wait()
        rows = slice(step * 2 * per_step, (step + 1) * 2 * per_step)
        weights = rad[step * per_step : (step + 1) * per_step].reshape(per_step * LANE, 2 * width)
        summed[rows] = dot_nn(blocks[rows].astype(BF16), weights).reshape(
            2 * per_step, 2 * width // LANE, LANE
        )
    chunks = width // LANE
    re_chunks, im_chunks = [], []
    for r in range(chunks):
        first_lo = summed[pl.ds(0, boxes, stride=2), r, :]
        first_hi = summed[pl.ds(0, boxes, stride=2), chunks + r, :]
        second_lo = summed[pl.ds(1, boxes, stride=2), r, :]
        second_hi = summed[pl.ds(1, boxes, stride=2), chunks + r, :]
        re_chunks.append((first_lo - second_hi).astype(BF16))
        im_chunks.append((first_hi + second_lo).astype(BF16))
    re_part = jnp.concatenate(re_chunks, 1)
    im_part = jnp.concatenate(im_chunks, 1)
    for r in range(chunks):
        table[pl.ds(r, boxes, stride=8), :] = re_chunks[r].astype(F32)
        table[pl.ds(chunks + r, boxes, stride=8), :] = im_chunks[r].astype(F32)
    table[pl.ds(boxes * 8, 8), :] = jnp.zeros((8, LANE), F32)
    for copy in others[1:]:
        copy.wait()
    wide = dot_nn(jnp.concatenate([re_part, im_part], 0), interp_ref[...])
    hi_chunks = wide.shape[1] // LANE
    parents = boxes // 8
    share = hi_chunks // group
    for r in range(hi_chunks):
        cols = slice(r * LANE, (r + 1) * LANE)
        s_re = shift_ref[pl.ds(2 * r, 8, stride=2 * hi_chunks), :]
        s_im = shift_ref[pl.ds(2 * r + 1, 8, stride=2 * hi_chunks), :]
        for p in range(parents):
            w_re = wide[p * 8 : (p + 1) * 8, cols]
            w_im = wide[boxes + p * 8 : boxes + (p + 1) * 8, cols]
            row = ((r // share) * parents + p) * 2 * share + r % share
            parent[row : row + 1] = jnp.sum(w_re * s_re - w_im * s_im, 0, keepdims=True)
            row += share
            parent[row : row + 1] = jnp.sum(w_re * s_im + w_im * s_re, 0, keepdims=True)
    slots, devices = send_ref.shape
    hi_rows = parents * 2 * share

    def fill(d, carry):
        for k in range(slots // 2):
            pair = [
                table[pl.ds(pl.multiple_of(send_ref[2 * k + h, d] * 8, 8), 8), :] for h in range(2)
            ]
            out_ref[d, 16 * k : 16 * (k + 1)] = jnp.concatenate(pair, 0).astype(BF16)
        member = pl.multiple_of(lax.rem(d, group) * hi_rows, 8)
        out_ref[d, 8 * slots : 8 * slots + hi_rows] = parent[pl.ds(member, hi_rows)].astype(BF16)
        return carry

    lax.fori_loop(0, devices, fill, 0)


def tally(index, source_row, type_row, sources, types):
    source = index[pl.ds(source_row, 1), :]
    kind = index[pl.ds(type_row, 1), :]
    faces = index.shape[1]
    by_source = jnp.where(iota((sources, faces), 0) == source, 1.0, 0.0).astype(BF16)
    by_type = jnp.where(iota((types, faces), 0) == kind, 1.0, 0.0).astype(BF16)
    return dot_nt(by_source, by_type).astype(BF16)


def index_kernel(
    types,
    group,
    box_total,
    near_src_hbm,
    near_tile_hbm,
    slot_hbm,
    type_hbm,
    par_far_hbm,
    par_type_hbm,
    op_lo_hbm,
    op_hi_hbm,
    code_ref,
    counts_ref,
    op_lo,
    d_ref,
    near_src_ref,
    near_tile_ref,
    slot_ref,
    type_ref,
    par_far_ref,
    par_type_ref,
    op_lo_ref,
    op_hi_ref,
    index,
    wide_lo,
    wide_hi,
    op_hi,
    counts_hi,
    extra,
):
    others = fetch(
        [
            (near_src_hbm, near_src_ref),
            (near_tile_hbm, near_tile_ref),
            (slot_hbm, slot_ref),
            (type_hbm, type_ref),
            (par_far_hbm, par_far_ref),
            (par_type_hbm, par_type_ref),
            (op_lo_hbm, op_lo_ref),
            (op_hi_hbm, op_hi_ref),
        ],
        extra,
    )
    boxes, near = near_src_ref.shape
    rows, far = par_far_ref.shape
    parents, sources, _ = d_ref.shape
    slot_total = counts_ref.shape[0] // boxes
    type_pad = op_hi.shape[0]
    chunks = op_lo.shape[1] // (2 * LANE)
    lines = op_hi_ref.shape[0] // types
    share = lines // (2 * group)
    tile_count = code_ref.shape[0] - 8
    samp = lax.axis_index("samp")
    position = lax.axis_index("box") * lax.axis_size("samp") + samp
    member = lax.rem(samp, group)
    first_parent = 2 * boxes + (samp - member) * (parents // group)
    place = member * (2 * share)
    base = place // 16 * 16
    index[...] = jnp.full(index.shape, -1, jnp.int32)
    tail = (type_pad - types) * 2 * chunks
    wide_lo[types * 2 * chunks : type_pad * 2 * chunks] = jnp.zeros((tail, LANE), F32)
    wide_hi[types * 16 : type_pad * 16] = jnp.zeros(((type_pad - types) * 16, LANE), F32)
    for copy in others[:6]:
        copy.wait()

    def locate(g, carry):
        for n in range(near):
            source = near_src_ref[g, n]
            live = source < box_total
            tile = jnp.where(live, near_tile_ref[g, n] - position * tile_count, tile_count)
            code_ref[tile] = g * 64 + source - (position - 1) * boxes
        return carry

    lax.fori_loop(0, boxes, locate, 0)
    index[0:boxes, 0:far] = slot_ref[...]
    index[boxes : 2 * boxes, 0:far] = type_ref[...]
    index[2 * boxes : 2 * boxes + rows, 0:far] = par_far_ref[...]
    index[2 * boxes + rows : 2 * boxes + 2 * rows, 0:far] = par_type_ref[...]
    batch = 4

    def step_boxes(step, carry):
        for k in range(batch):
            g = step * batch + k
            at = pl.ds(pl.multiple_of(g * slot_total, slot_total), slot_total)
            counts_ref[at] = tally(index, g, boxes + g, slot_total, type_pad)
        return carry

    lax.fori_loop(0, boxes // batch, step_boxes, 0)

    def step_parents(step, carry):
        for k in range(batch):
            p = step * batch + k
            at = pl.ds(pl.multiple_of(p * sources, sources), sources)
            row = first_parent + p
            counts_hi[at] = tally(index, row, rows + row, sources, type_pad)
        return carry

    lax.fori_loop(0, parents // batch, step_parents, 0)
    others[6].wait()
    wide_lo[0 : types * 2 * chunks] = op_lo_ref[...].astype(F32)
    for c in range(2):
        for r in range(chunks):
            col = (c * chunks + r) * LANE
            op_lo[:, col : col + LANE] = wide_lo[
                pl.ds(2 * r + c, type_pad, stride=2 * chunks), :
            ].astype(BF16)
    others[7].wait()

    def widen(t, carry):
        source = pl.ds(pl.multiple_of(t * lines + base, 16), 16)
        wide_hi[pl.ds(pl.multiple_of(t * 16, 16), 16)] = op_hi_ref[source].astype(F32)
        return carry

    lax.fori_loop(0, types, widen, 0, unroll=4)
    for c in range(2):
        for k in range(share):
            col = (c * share + k) * LANE
            start = place - base + 2 * k + c
            op_hi[:, col : col + LANE] = wide_hi[pl.ds(start, type_pad, stride=16), :].astype(BF16)

    def sum_parents(step, carry):
        at = pl.ds(pl.multiple_of(step * batch * sources, batch * sources), batch * sources)
        d_ref[pl.ds(step * batch, batch)] = dot_nn(counts_hi[at], op_hi[...]).reshape(
            batch, sources, 2 * share * LANE
        )
        return carry

    lax.fori_loop(0, parents // batch, sum_parents, 0)


def parent_kernel(lo_lines, arrived_ref, d_ref, out_ref, wide):
    parents, sources, width = d_ref.shape
    share = width // (2 * LANE)
    rows = out_ref.shape[1]
    wide[...] = arrived_ref[:, lo_lines:, :].astype(F32).reshape(wide.shape)
    for k in range(share):
        first = wide[pl.ds(k, sources, stride=2 * share), :]
        second = wide[pl.ds(share + k, sources, stride=2 * share), :]
        for p in range(parents):
            o_re = d_ref[p, :, k * LANE : (k + 1) * LANE]
            o_im = d_ref[p, :, (share + k) * LANE : (share + k + 1) * LANE]
            row = p * 2 * share + k
            to, row = row // rows, row % rows
            out_ref[to, row : row + 1] = jnp.sum(o_re * first - o_im * second, 0, keepdims=True)
            row += share
            out_ref[to, row : row + 1] = jnp.sum(o_re * second + o_im * first, 0, keepdims=True)


def middle_kernel(
    even_ref,
    dens_hbm,
    odd_ref,
    tiles_hbm,
    code_hbm,
    counts_ref,
    op_lo,
    arrived_ref,
    near_ref,
    incoming_ref,
    tiles,
    halo,
    dens3,
    left,
    right,
    acc,
    code,
    summed,
    slots,
    sems,
    extra,
):
    boxes = near_ref.shape[0] // 2
    tile_count = tiles.shape[0]
    steps = sems.shape[0]
    per_step = tile_count // steps
    odd = lax.rem(lax.axis_index("samp"), 2)
    others = fetch(
        [
            (code_hbm, code),
            (even_ref, halo.at[2 - 2 * odd]),
            (dens_hbm, halo.at[1]),
            (odd_ref, halo.at[2 * odd]),
        ],
        extra,
    )

    def tile_copy(step):
        part = pl.ds(step * per_step, per_step)
        return pltpu.make_async_copy(tiles_hbm.at[part], tiles.at[part], sems.at[step])

    for step in range(steps):
        tile_copy(step).start()
    acc[...] = jnp.zeros(acc.shape, F32)
    left[...] = jnp.zeros(left.shape, F32)
    right[...] = jnp.zeros(right.shape, F32)
    lo_lines = slots.shape[0] // arrived_ref.shape[0]
    slots[...] = arrived_ref[:, :lo_lines, :].astype(F32).reshape(slots.shape)
    for copy in others:
        copy.wait()
    for k in range(3):
        dens3[pl.ds(2 * boxes * k, 2 * boxes), :] = halo[k].astype(F32)
    first = dens3[pl.ds(0, 3 * boxes, stride=2), :]
    second = dens3[pl.ds(1, 3 * boxes, stride=2), :]
    left[pl.ds(0, 3 * boxes, stride=8), :] = first
    left[pl.ds(1, 3 * boxes, stride=8), :] = second
    right[pl.ds(0, 3 * boxes, stride=8), :] = -second
    right[pl.ds(1, 3 * boxes, stride=8), :] = first

    chunks = op_lo.shape[1] // (2 * LANE)
    slot_total = slots.shape[0] // (2 * chunks)
    per_boxes = boxes // steps

    def step_boxes(step, carry):
        start = step * per_boxes
        height = per_boxes * slot_total
        at = pl.ds(pl.multiple_of(start * slot_total, height), height)
        summed[...] = dot_nn(counts_ref[at], op_lo[...])
        tile_copy(step).wait()
        for pair in range(per_step // 2):
            tile = step * per_step + 2 * pair
            both = tiles[pl.ds(tile, 2)]
            weights = jnp.concatenate(
                [both[:, 0].reshape(2 * LANE, LANE), both[:, 1].reshape(2 * LANE, LANE)], 1
            )
            owners, lefts, rights = [], [], []
            for h in range(2):
                entry = code[tile + h]
                row = pl.ds(pl.multiple_of((entry & 63) * 8, 8), 8)
                owners.append(entry >> 6)
                lefts.append(left[row])
                rights.append(right[row])
            lhs = jnp.concatenate([jnp.concatenate(lefts, 0), jnp.concatenate(rights, 0)], 1)
            product = dot_nt(lhs.astype(BF16), weights)
            for h in range(2):
                acc[owners[h]] = (
                    acc[owners[h]] + product[8 * h : 8 * (h + 1), h * LANE : (h + 1) * LANE]
                )
        for r in range(chunks):
            cols = slice(r * LANE, (r + 1) * LANE)
            first = slots[pl.ds(r, slot_total, stride=2 * chunks), :]
            second = slots[pl.ds(chunks + r, slot_total, stride=2 * chunks), :]
            for k in range(per_boxes):
                part = slice(k * slot_total, (k + 1) * slot_total)
                o_re = summed[part, cols]
                o_im = summed[part, (chunks + r) * LANE : (chunks + r + 1) * LANE]
                incoming_ref[start + k, r : r + 1] = jnp.sum(
                    o_re * first - o_im * second, 0, keepdims=True
                )
                incoming_ref[boxes + start + k, r : r + 1] = jnp.sum(
                    o_re * second + o_im * first, 0, keepdims=True
                )
        return carry

    lax.fori_loop(0, steps, step_boxes, 0)
    for g in range(boxes):
        row = 2 * g
        near_ref[row : row + 2] = acc[g, 0:2] + 0.5 * dens3[pl.ds(2 * boxes + row, 2), :]


def last_kernel(
    parent_ref,
    incoming_ref,
    shift_hbm,
    interp_hbm,
    receive_ref,
    near_ref,
    out_ref,
    receive,
    shift_ref,
    interp_ref,
    down,
    blend,
    sems,
    extra,
):
    boxes = receive.shape[0]
    per_step = 4
    steps = boxes // per_step
    others = fetch([(shift_hbm, shift_ref), (interp_hbm, interp_ref)], extra)
    copies = []
    for step in range(steps):
        part = pl.ds(step * per_step, per_step)
        copies.append(pltpu.make_async_copy(receive_ref.at[part], receive.at[part], sems.at[step]))
        copies[-1].start()
    own_parents = boxes // 8
    hi_chunks = down.shape[1] // LANE
    chunks = incoming_ref.shape[1]
    share = hi_chunks // parent_ref.shape[0]
    others[0].wait()
    for r in range(hi_chunks):
        s_re = shift_ref[pl.ds(2 * r, 8, stride=2 * hi_chunks), :]
        s_im = shift_ref[pl.ds(2 * r + 1, 8, stride=2 * hi_chunks), :]
        re_rows, im_rows = [], []
        for p in range(own_parents):
            row = p * 2 * share + r % share
            t_re = parent_ref[r // share, row : row + 1]
            t_im = parent_ref[r // share, row + share : row + share + 1]
            re_rows.append(s_re * t_re + s_im * t_im)
            im_rows.append(s_re * t_im - s_im * t_re)
        cols = slice(r * LANE, (r + 1) * LANE)
        down[:, cols] = jnp.concatenate(re_rows + im_rows, 0).astype(BF16)
    others[1].wait()
    total = jnp.concatenate([incoming_ref[:, r, :] for r in range(chunks)], 1)
    total = total + dot_nt(down[...], interp_ref[...])
    total = total.astype(BF16).astype(F32)
    for r in range(chunks):
        re_part = total[:boxes, r * LANE : (r + 1) * LANE]
        im_part = total[boxes:, r * LANE : (r + 1) * LANE]
        blend[pl.ds(0, boxes, stride=2), r, :] = re_part
        blend[pl.ds(1, boxes, stride=2), r, :] = im_part
        blend[pl.ds(0, boxes, stride=2), chunks + r, :] = -im_part
        blend[pl.ds(1, boxes, stride=2), chunks + r, :] = re_part
    owner = (iota((2 * per_step, LANE), 0) // 2) % per_step
    for step in range(steps):
        rows = slice(step * 2 * per_step, (step + 1) * 2 * per_step)
        lhs = jnp.concatenate([blend[rows, r, :] for r in range(2 * chunks)], 1).astype(BF16)
        copies[step].wait()
        weights = receive[step * per_step : (step + 1) * per_step]
        product = dot_nt(lhs, weights.reshape(per_step * LANE, 2 * chunks * LANE))
        total = near_ref[rows]
        for b in range(per_step):
            total = total + jnp.where(owner == b, product[:, b * LANE : (b + 1) * LANE], 0.0)
        out_ref[rows] = total


def in_hbm(array):
    return pltpu.with_memory_space_constraint(array, pltpu.HBM)


def in_vmem(array):
    return pltpu.with_memory_space_constraint(array, pltpu.VMEM)


def tiled_rows(array):
    count, parts, width = array.shape
    cut = array.reshape(count, parts, width // LANE, LANE)
    return cut.transpose(0, 2, 1, 3).reshape(-1, LANE)


def on_device(
    density,
    radiate,
    receive,
    near_tiles,
    near_src,
    near_tile,
    send_box,
    distant_pattern_slot,
    far_type,
    trans_lo,
    interp_matrix,
    shifts,
    par_far,
    par_type,
    trans_hi,
):
    boxes, _, panels = density.shape
    devices = lax.axis_size("box") * lax.axis_size("samp")
    slots = send_box.shape[2]
    types, _, width_lo = trans_lo.shape
    width_hi = trans_hi.shape[2]
    parents = boxes // 8
    slot_total = devices * slots
    par_total = devices * parents
    type_pad = -(-types // 8) * 8
    samp_count = lax.axis_size("samp")
    group = min(samp_count, 8)
    share = width_hi // LANE // group
    lo_lines = slots * 2 * width_lo // LANE
    hi_lines = parents * 2 * share
    lines = lo_lines + hi_lines
    members = None
    if group < samp_count:
        members = [list(range(k, k + group)) for k in range(0, samp_count, group)]
    rows = density.reshape(boxes * 2, panels)
    shift_rows = tiled_rows(shifts)
    send = send_box[0].T
    outgoing = pl.pallas_call(
        functools.partial(radiate_kernel, group),
        out_shape=jax.ShapeDtypeStruct((devices, lines, LANE), BF16),
        in_specs=[HBM_SPEC] * 5,
        out_specs=VMEM_SPEC,
        scratch_shapes=[
            pltpu.VMEM(radiate.shape, BF16),
            pltpu.VMEM(rows.shape, BF16),
            pltpu.SMEM(send.shape, jnp.int32),
            pltpu.VMEM(interp_matrix.shape, BF16),
            pltpu.VMEM(shift_rows.shape, F32),
            pltpu.VMEM((2 * boxes, 2 * width_lo // LANE, LANE), F32),
            pltpu.VMEM((boxes * 8 + 8, LANE), F32),
            pltpu.VMEM((parents * 2 * width_hi // LANE, LANE), F32),
            pltpu.SemaphoreType.DMA((boxes // 4,)),
            pltpu.SemaphoreType.DMA((4,)),
        ],
        compiler_params=pltpu.CompilerParams(vmem_limit_bytes=12 * MIB),
        cost_estimate=pl.CostEstimate(flops=10**9, bytes_accessed=8 * MIB, transcendentals=0),
    )(*(in_hbm(x) for x in (rows, radiate, send, interp_matrix, shift_rows)))
    outgoing, near_rows = lax.optimization_barrier((outgoing, rows))
    arrived = lax.all_to_all(outgoing, ("box", "samp"), split_axis=0, concat_axis=0, tiled=True)
    both = ("box", "samp")
    even = exchanged(near_rows, both, 0)
    odd = exchanged(near_rows, both, 1)
    tile_count = near_tiles.shape[0]
    far = far_type.shape
    op_hi_rows = tiled_rows(trans_hi)
    op_lo_rows = tiled_rows(trans_lo)
    code, counts, op_lo, d_hi = pl.pallas_call(
        functools.partial(index_kernel, types, group, boxes * devices),
        out_shape=(
            jax.ShapeDtypeStruct((tile_count + 8,), jnp.int32),
            pltpu.VMEM((boxes * slot_total, type_pad), BF16),
            pltpu.VMEM((type_pad, 2 * width_lo), BF16),
            pltpu.VMEM((parents * group, par_total, 2 * share * LANE), F32),
        ),
        in_specs=[HBM_SPEC] * 8,
        out_specs=(SMEM_SPEC,) + (VMEM_SPEC,) * 3,
        scratch_shapes=[
            pltpu.SMEM(near_src.shape, jnp.int32),
            pltpu.SMEM(near_src.shape, jnp.int32),
            pltpu.VMEM(far, jnp.int32),
            pltpu.VMEM(far, jnp.int32),
            pltpu.VMEM(par_far.shape, jnp.int32),
            pltpu.VMEM(par_far.shape, jnp.int32),
            pltpu.VMEM(op_lo_rows.shape, BF16),
            pltpu.VMEM(op_hi_rows.shape, BF16),
            pltpu.VMEM((2 * boxes + 2 * par_far.shape[0], 2 * LANE), jnp.int32),
            pltpu.VMEM((type_pad * 2 * width_lo // LANE, LANE), F32),
            pltpu.VMEM((type_pad * 16, LANE), F32),
            pltpu.VMEM((type_pad, 2 * share * LANE), BF16),
            pltpu.VMEM((parents * group * par_total, type_pad), BF16),
            pltpu.SemaphoreType.DMA((8,)),
        ],
        compiler_params=pltpu.CompilerParams(vmem_limit_bytes=16 * MIB),
        cost_estimate=pl.CostEstimate(flops=10**9, bytes_accessed=16 * MIB, transcendentals=0),
    )(
        *(
            in_hbm(x)
            for x in (
                near_src,
                near_tile,
                distant_pattern_slot,
                far_type,
                par_far,
                par_type,
                op_lo_rows,
                op_hi_rows,
            )
        )
    )
    above = pl.pallas_call(
        functools.partial(parent_kernel, lo_lines),
        out_shape=jax.ShapeDtypeStruct((group, hi_lines, LANE), F32),
        in_specs=[VMEM_SPEC] * 2,
        out_specs=VMEM_SPEC,
        scratch_shapes=[pltpu.VMEM((devices * hi_lines, LANE), F32)],
        compiler_params=pltpu.CompilerParams(vmem_limit_bytes=4 * MIB),
        cost_estimate=pl.CostEstimate(flops=10**8, bytes_accessed=MIB, transcendentals=0),
    )(arrived, in_vmem(d_hi))
    above, even, odd = lax.optimization_barrier((above, even, odd))
    own_above = lax.all_to_all(
        above, "samp", split_axis=0, concat_axis=0, axis_index_groups=members, tiled=True
    )
    steps = 4
    near, incoming = pl.pallas_call(
        middle_kernel,
        out_shape=(
            jax.ShapeDtypeStruct((2 * boxes, panels), F32),
            jax.ShapeDtypeStruct((2 * boxes, width_lo // LANE, LANE), F32),
        ),
        in_specs=[ANY_SPEC, HBM_SPEC, ANY_SPEC, HBM_SPEC, ANY_SPEC] + [VMEM_SPEC] * 3,
        out_specs=(VMEM_SPEC,) * 2,
        scratch_shapes=[
            pltpu.VMEM(near_tiles.shape, BF16),
            pltpu.VMEM((3, 2 * boxes, panels), BF16),
            pltpu.VMEM((6 * boxes, panels), F32),
            pltpu.VMEM((3 * boxes * 8, LANE), F32),
            pltpu.VMEM((3 * boxes * 8, LANE), F32),
            pltpu.VMEM((boxes, 8, LANE), F32),
            pltpu.SMEM((tile_count + 8,), jnp.int32),
            pltpu.VMEM((boxes // steps * slot_total, 2 * width_lo), F32),
            pltpu.VMEM((devices * lo_lines, LANE), F32),
            pltpu.SemaphoreType.DMA((steps,)),
            pltpu.SemaphoreType.DMA((4,)),
        ],
        compiler_params=pltpu.CompilerParams(
            vmem_limit_bytes=(22 if slot_total <= 128 else 36) * MIB
        ),
        cost_estimate=pl.CostEstimate(flops=10**10, bytes_accessed=20 * MIB, transcendentals=0),
    )(
        even,
        in_hbm(rows),
        odd,
        in_hbm(near_tiles),
        code,
        in_vmem(counts),
        in_vmem(op_lo),
        arrived,
    )
    field = pl.pallas_call(
        last_kernel,
        out_shape=jax.ShapeDtypeStruct((2 * boxes, panels), F32),
        in_specs=[VMEM_SPEC] * 2 + [HBM_SPEC] * 3 + [VMEM_SPEC],
        out_specs=VMEM_SPEC,
        scratch_shapes=[
            pltpu.VMEM(receive.shape, BF16),
            pltpu.VMEM(shift_rows.shape, F32),
            pltpu.VMEM(interp_matrix.shape, BF16),
            pltpu.VMEM((2 * boxes, width_hi), BF16),
            pltpu.VMEM((2 * boxes, 2 * width_lo // LANE, LANE), F32),
            pltpu.SemaphoreType.DMA((boxes // 4,)),
            pltpu.SemaphoreType.DMA((2,)),
        ],
        compiler_params=pltpu.CompilerParams(vmem_limit_bytes=12 * MIB),
        cost_estimate=pl.CostEstimate(flops=10**9, bytes_accessed=8 * MIB, transcendentals=0),
    )(own_above, incoming, shift_rows, interp_matrix, in_hbm(receive), near)
    return field.reshape(boxes, 2, panels)


def solution(mesh):
    both = ("box", "samp")
    return jax.shard_map(
        on_device,
        mesh=mesh,
        in_specs=(
            P(both, None, None),
            P(both, None, None),
            P(both, None, None),
            P(both, None, None, None),
            P(both, None),
            P(both, None),
            P(both, None, None),
            P(both, None),
            P(both, None),
            P(),
            P(),
            P(),
            P("box", None),
            P("box", None),
            P(),
        ),
        out_specs=P(both, None, None),
        check_vma=False,
    )
```

```python
import functools

import jax
import jax.numpy as jnp
from jax import lax
from jax.experimental import pallas as pl
from jax.experimental.pallas import tpu as pltpu
from jax.sharding import PartitionSpec as P

F32 = jnp.float32
BF16 = jnp.bfloat16
LANE = 128
VMEM_SPEC = pl.BlockSpec(memory_space=pltpu.VMEM)
SMEM_SPEC = pl.BlockSpec(memory_space=pltpu.SMEM)
ANY_SPEC = pl.BlockSpec(memory_space=pl.ANY)
HBM_SPEC = pl.BlockSpec(memory_space=pltpu.HBM)
MIB = 1 << 20


def iota(shape, dim):
    return lax.broadcasted_iota(jnp.int32, shape, dim)


def dot_nn(lhs, rhs):
    return lax.dot_general(lhs, rhs, (((1,), (0,)), ((), ())), preferred_element_type=F32)


def dot_nt(lhs, rhs):
    return lax.dot_general(lhs, rhs, (((1,), (1,)), ((), ())), preferred_element_type=F32)


def exchanged(value, axes, first):
    count = lax.axis_size(axes)
    pairs = []
    for low in range(first, count - 1, 2):
        pairs += [(low, low + 1), (low + 1, low)]
    return lax.ppermute(value, axes, pairs)


def fetch(pairs, sems, first=0):
    copies = []
    for k, (source, target) in enumerate(pairs):
        copies.append(pltpu.make_async_copy(source, target, sems.at[first + k]))
        copies[-1].start()
    return copies


def radiate_kernel(
    group,
    dens_hbm,
    radiate_ref,
    send_hbm,
    interp_hbm,
    shift_hbm,
    out_ref,
    rad,
    dens_ref,
    send_ref,
    interp_ref,
    shift_ref,
    summed,
    table,
    parent,
    sems,
    extra,
):
    boxes = rad.shape[0]
    width = rad.shape[2] // 2
    per_step = 4
    steps = boxes // per_step
    others = fetch(
        [(dens_hbm, dens_ref), (send_hbm, send_ref), (shift_hbm, shift_ref)], extra
    )
    copies = []
    for step in range(steps):
        part = pl.ds(step * per_step, per_step)
        copies.append(pltpu.make_async_copy(radiate_ref.at[part], rad.at[part], sems.at[step]))
        copies[-1].start()
    others += fetch([(interp_hbm, interp_ref)], extra, 3)
    others[0].wait()
    dens = dens_ref[...].astype(F32)
    owner = (iota(dens.shape, 0) // 2) % per_step
    blocks = jnp.concatenate([jnp.where(owner == b, dens, 0.0) for b in range(per_step)], 1)
    for step in range(steps):
        copies[step].wait()
        rows = slice(step * 2 * per_step, (step + 1) * 2 * per_step)
        weights = rad[step * per_step : (step + 1) * per_step].reshape(per_step * LANE, 2 * width)
        summed[rows] = dot_nn(blocks[rows].astype(BF16), weights).reshape(
            2 * per_step, 2 * width // LANE, LANE
        )
    chunks = width // LANE
    re_chunks, im_chunks = [], []
    for r in range(chunks):
        first_lo = summed[pl.ds(0, boxes, stride=2), r, :]
        first_hi = summed[pl.ds(0, boxes, stride=2), chunks + r, :]
        second_lo = summed[pl.ds(1, boxes, stride=2), r, :]
        second_hi = summed[pl.ds(1, boxes, stride=2), chunks + r, :]
        re_chunks.append((first_lo - second_hi).astype(BF16))
        im_chunks.append((first_hi + second_lo).astype(BF16))
    re_part = jnp.concatenate(re_chunks, 1)
    im_part = jnp.concatenate(im_chunks, 1)
    for r in range(chunks):
        table[pl.ds(r, boxes, stride=8), :] = re_chunks[r].astype(F32)
        table[pl.ds(chunks + r, boxes, stride=8), :] = im_chunks[r].astype(F32)
    table[pl.ds(boxes * 8, 8), :] = jnp.zeros((8, LANE), F32)
    for copy in others[1:]:
        copy.wait()
    wide = dot_nn(jnp.concatenate([re_part, im_part], 0), interp_ref[...])
    hi_chunks = wide.shape[1] // LANE
    parents = boxes // 8
    share = hi_chunks // group
    for r in range(hi_chunks):
        cols = slice(r * LANE, (r + 1) * LANE)
        s_re = shift_ref[pl.ds(2 * r, 8, stride=2 * hi_chunks), :]
        s_im = shift_ref[pl.ds(2 * r + 1, 8, stride=2 * hi_chunks), :]
        for p in range(parents):
            w_re = wide[p * 8 : (p + 1) * 8, cols]
            w_im = wide[boxes + p * 8 : boxes + (p + 1) * 8, cols]
            row = ((r // share) * parents + p) * 2 * share + r % share
            parent[row : row + 1] = jnp.sum(w_re * s_re - w_im * s_im, 0, keepdims=True)
            row += share
            parent[row : row + 1] = jnp.sum(w_re * s_im + w_im * s_re, 0, keepdims=True)
    slots, devices = send_ref.shape
    hi_rows = parents * 2 * share

    def fill(d, carry):
        for k in range(slots // 2):
            pair = [
                table[pl.ds(pl.multiple_of(send_ref[2 * k + h, d] * 8, 8), 8), :] for h in range(2)
            ]
            out_ref[d, 16 * k : 16 * (k + 1)] = jnp.concatenate(pair, 0).astype(BF16)
        member = pl.multiple_of(lax.rem(d, group) * hi_rows, 8)
        out_ref[d, 8 * slots : 8 * slots + hi_rows] = parent[pl.ds(member, hi_rows)].astype(BF16)
        return carry

    lax.fori_loop(0, devices, fill, 0, unroll=4)


def tally(index, source_row, type_row, sources, types):
    source = index[pl.ds(source_row, 1), :]
    kind = index[pl.ds(type_row, 1), :]
    faces = index.shape[1]
    by_source = jnp.where(iota((sources, faces), 0) == source, 1.0, 0.0).astype(BF16)
    by_type = jnp.where(iota((types, faces), 0) == kind, 1.0, 0.0).astype(BF16)
    return dot_nt(by_source, by_type).astype(BF16)


def index_kernel(
    types,
    group,
    box_total,
    near_src_hbm,
    near_tile_hbm,
    slot_hbm,
    type_hbm,
    par_far_hbm,
    par_type_hbm,
    op_lo_hbm,
    op_hi_hbm,
    code_ref,
    d_lo_hbm,
    d_ref,
    near_src_ref,
    near_tile_ref,
    slot_ref,
    type_ref,
    par_far_ref,
    par_type_ref,
    op_lo_ref,
    op_hi_ref,
    index,
    wide_lo,
    wide_hi,
    op_lo,
    op_hi,
    counts_hi,
    d_lo,
    sems,
    extra,
):
    others = fetch(
        [
            (op_lo_hbm, op_lo_ref),
            (near_src_hbm, near_src_ref),
            (near_tile_hbm, near_tile_ref),
            (slot_hbm, slot_ref),
            (type_hbm, type_ref),
            (par_far_hbm, par_far_ref),
            (par_type_hbm, par_type_ref),
            (op_hi_hbm, op_hi_ref),
        ],
        extra,
    )
    boxes, near = near_src_ref.shape
    rows, far = par_far_ref.shape
    parents, sources, _ = d_ref.shape
    slot_total = d_lo.shape[1]
    type_pad = op_hi.shape[0]
    chunks = op_lo.shape[1] // (2 * LANE)
    lines = op_hi_ref.shape[0] // types
    share = lines // (2 * group)
    tile_count = code_ref.shape[0] - 8
    samp = lax.axis_index("samp")
    position = lax.axis_index("box") * lax.axis_size("samp") + samp
    member = lax.rem(samp, group)
    first_parent = 2 * boxes + (samp - member) * (parents // group)
    place = member * (2 * share)
    base = place // 16 * 16
    index[...] = jnp.full(index.shape, -1, jnp.int32)
    tail = (type_pad - types) * 2 * chunks
    wide_lo[types * 2 * chunks : type_pad * 2 * chunks] = jnp.zeros((tail, LANE), F32)
    wide_hi[types * 16 : type_pad * 16] = jnp.zeros(((type_pad - types) * 16, LANE), F32)
    for copy in others[:7]:
        copy.wait()

    index[0:boxes, 0:far] = slot_ref[...]
    index[boxes : 2 * boxes, 0:far] = type_ref[...]
    index[2 * boxes : 2 * boxes + rows, 0:far] = par_far_ref[...]
    index[2 * boxes + rows : 2 * boxes + 2 * rows, 0:far] = par_type_ref[...]
    batch = 4

    wide_lo[0 : types * 2 * chunks] = op_lo_ref[...].astype(F32)
    for c in range(2):
        for r in range(chunks):
            col = (c * chunks + r) * LANE
            op_lo[:, col : col + LANE] = wide_lo[
                pl.ds(2 * r + c, type_pad, stride=2 * chunks), :
            ].astype(BF16)

    def lo_copy(step):
        part = pl.ds(step * batch, batch)
        return pltpu.make_async_copy(d_lo.at[part], d_lo_hbm.at[part], sems.at[step])

    def step_boxes(step, carry):
        counts = jnp.concatenate(
            [
                tally(index, step * batch + k, boxes + step * batch + k, slot_total, type_pad)
                for k in range(batch)
            ],
            0,
        )
        d_lo[pl.ds(step * batch, batch)] = (
            dot_nn(counts, op_lo[...]).astype(BF16).reshape(batch, slot_total, 2 * chunks * LANE)
        )
        lo_copy(step).start()
        return carry

    lax.fori_loop(0, boxes // batch, step_boxes, 0)
    def locate(g, carry):
        for n in range(near):
            source = near_src_ref[g, n]
            live = source < box_total
            tile = jnp.where(live, near_tile_ref[g, n] - position * tile_count, tile_count)
            code_ref[tile] = g * 64 + source - (position - 1) * boxes
        return carry

    lax.fori_loop(0, boxes, locate, 0)
    def step_parents(step, carry):
        for k in range(batch):
            p = step * batch + k
            at = pl.ds(pl.multiple_of(p * sources, sources), sources)
            row = first_parent + p
            counts_hi[at] = tally(index, row, rows + row, sources, type_pad)
        return carry

    lax.fori_loop(0, parents // batch, step_parents, 0)
    others[7].wait()

    def widen(t, carry):
        source = pl.ds(pl.multiple_of(t * lines + base, 16), 16)
        wide_hi[pl.ds(pl.multiple_of(t * 16, 16), 16)] = op_hi_ref[source].astype(F32)
        return carry

    lax.fori_loop(0, types, widen, 0, unroll=4)
    for c in range(2):
        for k in range(share):
            col = (c * share + k) * LANE
            start = place - base + 2 * k + c
            op_hi[:, col : col + LANE] = wide_hi[pl.ds(start, type_pad, stride=16), :].astype(BF16)

    def sum_parents(step, carry):
        at = pl.ds(pl.multiple_of(step * batch * sources, batch * sources), batch * sources)
        d_ref[pl.ds(step * batch, batch)] = dot_nn(counts_hi[at], op_hi[...]).reshape(
            batch, sources, 2 * share * LANE
        )
        return carry

    lax.fori_loop(0, parents // batch, sum_parents, 0)
    for step in range(boxes // batch):
        lo_copy(step).wait()


def parent_kernel(lo_lines, arrived_ref, d_ref, out_ref, wide):
    parents, sources, width = d_ref.shape
    share = width // (2 * LANE)
    rows = out_ref.shape[1]
    wide[...] = arrived_ref[:, lo_lines:, :].astype(F32).reshape(wide.shape)
    for k in range(share):
        first = wide[pl.ds(k, sources, stride=2 * share), :]
        second = wide[pl.ds(share + k, sources, stride=2 * share), :]
        for p in range(parents):
            o_re = d_ref[p, :, k * LANE : (k + 1) * LANE]
            o_im = d_ref[p, :, (share + k) * LANE : (share + k + 1) * LANE]
            row = p * 2 * share + k
            to, row = row // rows, row % rows
            out_ref[to, row : row + 1] = jnp.sum(o_re * first - o_im * second, 0, keepdims=True)
            row += share
            out_ref[to, row : row + 1] = jnp.sum(o_re * second + o_im * first, 0, keepdims=True)


def middle_kernel(
    even_ref,
    dens_hbm,
    odd_ref,
    tiles_hbm,
    code_hbm,
    d_lo_hbm,
    arrived_ref,
    near_ref,
    incoming_ref,
    tiles,
    halo,
    dens3,
    left,
    right,
    acc,
    code,
    d_lo,
    slots,
    sems,
    lo_sems,
    extra,
):
    boxes = near_ref.shape[0] // 2
    tile_count = tiles.shape[0]
    steps = sems.shape[0]
    per_step = tile_count // steps
    odd = lax.rem(lax.axis_index("samp"), 2)
    others = fetch(
        [
            (code_hbm, code),
            (even_ref, halo.at[2 - 2 * odd]),
            (dens_hbm, halo.at[1]),
            (odd_ref, halo.at[2 * odd]),
        ],
        extra,
    )

    def tile_copy(step):
        part = pl.ds(step * per_step, per_step)
        return pltpu.make_async_copy(tiles_hbm.at[part], tiles.at[part], sems.at[step])

    per_boxes = boxes // steps

    def lo_copy(step):
        part = pl.ds(step * per_boxes, per_boxes)
        return pltpu.make_async_copy(d_lo_hbm.at[part], d_lo.at[part], lo_sems.at[step])

    for step in range(steps):
        tile_copy(step).start()
        lo_copy(step).start()
    acc[...] = jnp.zeros(acc.shape, F32)
    left[...] = jnp.zeros(left.shape, F32)
    right[...] = jnp.zeros(right.shape, F32)
    lo_lines = slots.shape[0] // arrived_ref.shape[0]
    slots[...] = arrived_ref[:, :lo_lines, :].astype(F32).reshape(slots.shape)
    for copy in others:
        copy.wait()
    for k in range(3):
        dens3[pl.ds(2 * boxes * k, 2 * boxes), :] = halo[k].astype(F32)
    first = dens3[pl.ds(0, 3 * boxes, stride=2), :]
    second = dens3[pl.ds(1, 3 * boxes, stride=2), :]
    left[pl.ds(0, 3 * boxes, stride=8), :] = first
    left[pl.ds(1, 3 * boxes, stride=8), :] = second
    right[pl.ds(0, 3 * boxes, stride=8), :] = -second
    right[pl.ds(1, 3 * boxes, stride=8), :] = first

    chunks = d_lo.shape[2] // (2 * LANE)
    slot_total = d_lo.shape[1]

    def step_boxes(step, carry):
        start = step * per_boxes
        tile_copy(step).wait()
        for pair in range(per_step // 2):
            tile = step * per_step + 2 * pair
            both = tiles[pl.ds(tile, 2)]
            weights = jnp.concatenate(
                [both[:, 0].reshape(2 * LANE, LANE), both[:, 1].reshape(2 * LANE, LANE)], 1
            )
            owners, lefts, rights = [], [], []
            for h in range(2):
                entry = code[tile + h]
                row = pl.ds(pl.multiple_of((entry & 63) * 8, 8), 8)
                owners.append(entry >> 6)
                lefts.append(left[row])
                rights.append(right[row])
            lhs = jnp.concatenate([jnp.concatenate(lefts, 0), jnp.concatenate(rights, 0)], 1)
            product = dot_nt(lhs.astype(BF16), weights)
            for h in range(2):
                acc[owners[h]] = (
                    acc[owners[h]] + product[8 * h : 8 * (h + 1), h * LANE : (h + 1) * LANE]
                )
        lo_copy(step).wait()
        for r in range(chunks):
            cols = slice(r * LANE, (r + 1) * LANE)
            first = slots[pl.ds(r, slot_total, stride=2 * chunks), :]
            second = slots[pl.ds(chunks + r, slot_total, stride=2 * chunks), :]
            for k in range(per_boxes):
                o_re = d_lo[start + k, :, cols].astype(F32)
                o_im = d_lo[start + k, :, (chunks + r) * LANE : (chunks + r + 1) * LANE].astype(F32)
                incoming_ref[start + k, r : r + 1] = jnp.sum(
                    o_re * first - o_im * second, 0, keepdims=True
                )
                incoming_ref[boxes + start + k, r : r + 1] = jnp.sum(
                    o_re * second + o_im * first, 0, keepdims=True
                )
        return carry

    lax.fori_loop(0, steps, step_boxes, 0)
    for g in range(boxes):
        row = 2 * g
        near_ref[row : row + 2] = acc[g, 0:2] + 0.5 * dens3[pl.ds(2 * boxes + row, 2), :]


def last_kernel(
    parent_ref,
    incoming_ref,
    shift_hbm,
    interp_hbm,
    receive_ref,
    near_ref,
    out_ref,
    receive,
    shift_ref,
    interp_ref,
    down,
    blend,
    sems,
    extra,
):
    boxes = receive.shape[0]
    per_step = 4
    steps = boxes // per_step
    others = fetch([(shift_hbm, shift_ref), (interp_hbm, interp_ref)], extra)
    copies = []
    for step in range(steps):
        part = pl.ds(step * per_step, per_step)
        copies.append(pltpu.make_async_copy(receive_ref.at[part], receive.at[part], sems.at[step]))
        copies[-1].start()
    own_parents = boxes // 8
    hi_chunks = down.shape[1] // LANE
    chunks = incoming_ref.shape[1]
    share = hi_chunks // parent_ref.shape[0]
    others[0].wait()
    for r in range(hi_chunks):
        s_re = shift_ref[pl.ds(2 * r, 8, stride=2 * hi_chunks), :]
        s_im = shift_ref[pl.ds(2 * r + 1, 8, stride=2 * hi_chunks), :]
        re_rows, im_rows = [], []
        for p in range(own_parents):
            row = p * 2 * share + r % share
            t_re = parent_ref[r // share, row : row + 1]
            t_im = parent_ref[r // share, row + share : row + share + 1]
            re_rows.append(s_re * t_re + s_im * t_im)
            im_rows.append(s_re * t_im - s_im * t_re)
        cols = slice(r * LANE, (r + 1) * LANE)
        down[:, cols] = jnp.concatenate(re_rows + im_rows, 0).astype(BF16)
    others[1].wait()
    total = jnp.concatenate([incoming_ref[:, r, :] for r in range(chunks)], 1)
    total = total + dot_nt(down[...], interp_ref[...])
    total = total.astype(BF16).astype(F32)
    for r in range(chunks):
        re_part = total[:boxes, r * LANE : (r + 1) * LANE]
        im_part = total[boxes:, r * LANE : (r + 1) * LANE]
        blend[pl.ds(0, boxes, stride=2), r, :] = re_part
        blend[pl.ds(1, boxes, stride=2), r, :] = im_part
        blend[pl.ds(0, boxes, stride=2), chunks + r, :] = -im_part
        blend[pl.ds(1, boxes, stride=2), chunks + r, :] = re_part
    owner = (iota((2 * per_step, LANE), 0) // 2) % per_step
    for step in range(steps):
        rows = slice(step * 2 * per_step, (step + 1) * 2 * per_step)
        lhs = jnp.concatenate([blend[rows, r, :] for r in range(2 * chunks)], 1).astype(BF16)
        copies[step].wait()
        weights = receive[step * per_step : (step + 1) * per_step]
        product = dot_nt(lhs, weights.reshape(per_step * LANE, 2 * chunks * LANE))
        total = near_ref[rows]
        for b in range(per_step):
            total = total + jnp.where(owner == b, product[:, b * LANE : (b + 1) * LANE], 0.0)
        out_ref[rows] = total


def in_hbm(array):
    return pltpu.with_memory_space_constraint(array, pltpu.HBM)


def in_vmem(array):
    return pltpu.with_memory_space_constraint(array, pltpu.VMEM)


def tiled_rows(array):
    count, parts, width = array.shape
    cut = array.reshape(count, parts, width // LANE, LANE)
    return cut.transpose(0, 2, 1, 3).reshape(-1, LANE)


def on_device(
    density,
    radiate,
    receive,
    near_tiles,
    near_src,
    near_tile,
    send_box,
    distant_pattern_slot,
    far_type,
    trans_lo,
    interp_matrix,
    shifts,
    par_far,
    par_type,
    trans_hi,
):
    boxes, _, panels = density.shape
    devices = lax.axis_size("box") * lax.axis_size("samp")
    slots = send_box.shape[2]
    types, _, width_lo = trans_lo.shape
    width_hi = trans_hi.shape[2]
    parents = boxes // 8
    slot_total = devices * slots
    par_total = devices * parents
    type_pad = -(-types // 8) * 8
    samp_count = lax.axis_size("samp")
    group = min(samp_count, 8)
    share = width_hi // LANE // group
    lo_lines = slots * 2 * width_lo // LANE
    hi_lines = parents * 2 * share
    lines = lo_lines + hi_lines
    members = None
    if group < samp_count:
        members = [list(range(k, k + group)) for k in range(0, samp_count, group)]
    rows = density.reshape(boxes * 2, panels)
    shift_rows = tiled_rows(shifts)
    send = send_box[0].T
    outgoing = pl.pallas_call(
        functools.partial(radiate_kernel, group),
        out_shape=jax.ShapeDtypeStruct((devices, lines, LANE), BF16),
        in_specs=[HBM_SPEC] * 5,
        out_specs=VMEM_SPEC,
        scratch_shapes=[
            pltpu.VMEM(radiate.shape, BF16),
            pltpu.VMEM(rows.shape, BF16),
            pltpu.SMEM(send.shape, jnp.int32),
            pltpu.VMEM(interp_matrix.shape, BF16),
            pltpu.VMEM(shift_rows.shape, F32),
            pltpu.VMEM((2 * boxes, 2 * width_lo // LANE, LANE), F32),
            pltpu.VMEM((boxes * 8 + 8, LANE), F32),
            pltpu.VMEM((parents * 2 * width_hi // LANE, LANE), F32),
            pltpu.SemaphoreType.DMA((boxes // 4,)),
            pltpu.SemaphoreType.DMA((4,)),
        ],
        compiler_params=pltpu.CompilerParams(vmem_limit_bytes=12 * MIB),
        cost_estimate=pl.CostEstimate(flops=10**9, bytes_accessed=8 * MIB, transcendentals=0),
    )(*(in_hbm(x) for x in (rows, radiate, send, interp_matrix, shift_rows)))
    arrived = lax.all_to_all(outgoing, ("box", "samp"), split_axis=0, concat_axis=0, tiled=True)
    tile_count = near_tiles.shape[0]
    far = far_type.shape
    op_hi_rows = tiled_rows(trans_hi)
    op_lo_rows = tiled_rows(trans_lo)
    code, d_lo, d_hi = pl.pallas_call(
        functools.partial(index_kernel, types, group, boxes * devices),
        out_shape=(
            jax.ShapeDtypeStruct((tile_count + 8,), jnp.int32),
            pltpu.HBM((boxes, slot_total, 2 * width_lo), BF16),
            pltpu.VMEM((parents * group, par_total, 2 * share * LANE), F32),
        ),
        in_specs=[HBM_SPEC] * 8,
        out_specs=(SMEM_SPEC, HBM_SPEC, VMEM_SPEC),
        scratch_shapes=[
            pltpu.SMEM(near_src.shape, jnp.int32),
            pltpu.SMEM(near_src.shape, jnp.int32),
            pltpu.VMEM(far, jnp.int32),
            pltpu.VMEM(far, jnp.int32),
            pltpu.VMEM(par_far.shape, jnp.int32),
            pltpu.VMEM(par_far.shape, jnp.int32),
            pltpu.VMEM(op_lo_rows.shape, BF16),
            pltpu.VMEM(op_hi_rows.shape, BF16),
            pltpu.VMEM((2 * boxes + 2 * par_far.shape[0], 2 * LANE), jnp.int32),
            pltpu.VMEM((type_pad * 2 * width_lo // LANE, LANE), F32),
            pltpu.VMEM((type_pad * 16, LANE), F32),
            pltpu.VMEM((type_pad, 2 * width_lo), BF16),
            pltpu.VMEM((type_pad, 2 * share * LANE), BF16),
            pltpu.VMEM((parents * group * par_total, type_pad), BF16),
            pltpu.VMEM((boxes, slot_total, 2 * width_lo), BF16),
            pltpu.SemaphoreType.DMA((boxes // 4,)),
            pltpu.SemaphoreType.DMA((8,)),
        ],
        compiler_params=pltpu.CompilerParams(
            vmem_limit_bytes=(20 if slot_total <= 128 else 46) * MIB
        ),
        cost_estimate=pl.CostEstimate(flops=10**9, bytes_accessed=16 * MIB, transcendentals=0),
    )(
        *(
            in_hbm(x)
            for x in (
                near_src,
                near_tile,
                distant_pattern_slot,
                far_type,
                par_far,
                par_type,
                op_lo_rows,
                op_hi_rows,
            )
        )
    )
    above = pl.pallas_call(
        functools.partial(parent_kernel, lo_lines),
        out_shape=jax.ShapeDtypeStruct((group, hi_lines, LANE), F32),
        in_specs=[VMEM_SPEC] * 2,
        out_specs=VMEM_SPEC,
        scratch_shapes=[pltpu.VMEM((devices * hi_lines, LANE), F32)],
        compiler_params=pltpu.CompilerParams(vmem_limit_bytes=4 * MIB),
        cost_estimate=pl.CostEstimate(flops=10**8, bytes_accessed=MIB, transcendentals=0),
    )(arrived, in_vmem(d_hi))
    above, near_rows = lax.optimization_barrier((above, rows))
    even = exchanged(near_rows, ("box", "samp"), 0)
    odd = exchanged(near_rows, ("box", "samp"), 1)
    own_above = lax.all_to_all(
        above, "samp", split_axis=0, concat_axis=0, axis_index_groups=members, tiled=True
    )
    steps = 4
    near, incoming = pl.pallas_call(
        middle_kernel,
        out_shape=(
            jax.ShapeDtypeStruct((2 * boxes, panels), F32),
            jax.ShapeDtypeStruct((2 * boxes, width_lo // LANE, LANE), F32),
        ),
        in_specs=[ANY_SPEC, HBM_SPEC, ANY_SPEC, HBM_SPEC, ANY_SPEC, HBM_SPEC, VMEM_SPEC],
        out_specs=(VMEM_SPEC,) * 2,
        scratch_shapes=[
            pltpu.VMEM(near_tiles.shape, BF16),
            pltpu.VMEM((3, 2 * boxes, panels), BF16),
            pltpu.VMEM((6 * boxes, panels), F32),
            pltpu.VMEM((3 * boxes * 8, LANE), F32),
            pltpu.VMEM((3 * boxes * 8, LANE), F32),
            pltpu.VMEM((boxes, 8, LANE), F32),
            pltpu.SMEM((tile_count + 8,), jnp.int32),
            pltpu.VMEM((boxes, slot_total, 2 * width_lo), BF16),
            pltpu.VMEM((devices * lo_lines, LANE), F32),
            pltpu.SemaphoreType.DMA((steps,)),
            pltpu.SemaphoreType.DMA((steps,)),
            pltpu.SemaphoreType.DMA((4,)),
        ],
        compiler_params=pltpu.CompilerParams(
            vmem_limit_bytes=(24 if slot_total <= 128 else 42) * MIB
        ),
        cost_estimate=pl.CostEstimate(flops=10**10, bytes_accessed=20 * MIB, transcendentals=0),
    )(
        even,
        in_hbm(rows),
        odd,
        in_hbm(near_tiles),
        code,
        in_hbm(d_lo),
        arrived,
    )
    field = pl.pallas_call(
        last_kernel,
        out_shape=jax.ShapeDtypeStruct((2 * boxes, panels), F32),
        in_specs=[VMEM_SPEC] * 2 + [HBM_SPEC] * 3 + [VMEM_SPEC],
        out_specs=VMEM_SPEC,
        scratch_shapes=[
            pltpu.VMEM(receive.shape, BF16),
            pltpu.VMEM(shift_rows.shape, F32),
            pltpu.VMEM(interp_matrix.shape, BF16),
            pltpu.VMEM((2 * boxes, width_hi), BF16),
            pltpu.VMEM((2 * boxes, 2 * width_lo // LANE, LANE), F32),
            pltpu.SemaphoreType.DMA((boxes // 4,)),
            pltpu.SemaphoreType.DMA((2,)),
        ],
        compiler_params=pltpu.CompilerParams(vmem_limit_bytes=12 * MIB),
        cost_estimate=pl.CostEstimate(flops=10**9, bytes_accessed=8 * MIB, transcendentals=0),
    )(own_above, incoming, shift_rows, interp_matrix, in_hbm(receive), near)
    return field.reshape(boxes, 2, panels)


def solution(mesh):
    both = ("box", "samp")
    return jax.shard_map(
        on_device,
        mesh=mesh,
        in_specs=(
            P(both, None, None),
            P(both, None, None),
            P(both, None, None),
            P(both, None, None, None),
            P(both, None),
            P(both, None),
            P(both, None, None),
            P(both, None),
            P(both, None),
            P(),
            P(),
            P(),
            P("box", None),
            P("box", None),
            P(),
        ),
        out_specs=P(both, None, None),
        check_vma=False,
    )
```

```python
import functools

import jax
import jax.numpy as jnp
from jax import lax
from jax.experimental import pallas as pl
from jax.experimental.pallas import tpu as pltpu
from jax.sharding import PartitionSpec as P

F32 = jnp.float32
BF16 = jnp.bfloat16
LANE = 128
VMEM_SPEC = pl.BlockSpec(memory_space=pltpu.VMEM)
SMEM_SPEC = pl.BlockSpec(memory_space=pltpu.SMEM)
ANY_SPEC = pl.BlockSpec(memory_space=pl.ANY)
HBM_SPEC = pl.BlockSpec(memory_space=pltpu.HBM)
MIB = 1 << 20


def iota(shape, dim):
    return lax.broadcasted_iota(jnp.int32, shape, dim)


def dot_nn(lhs, rhs):
    return lax.dot_general(lhs, rhs, (((1,), (0,)), ((), ())), preferred_element_type=F32)


def dot_nt(lhs, rhs):
    return lax.dot_general(lhs, rhs, (((1,), (1,)), ((), ())), preferred_element_type=F32)


def exchanged(value, axes, first):
    count = lax.axis_size(axes)
    pairs = []
    for low in range(first, count - 1, 2):
        pairs += [(low, low + 1), (low + 1, low)]
    return lax.ppermute(value, axes, pairs)


def fetch(pairs, sems, first=0):
    copies = []
    for k, (source, target) in enumerate(pairs):
        copies.append(pltpu.make_async_copy(source, target, sems.at[first + k]))
        copies[-1].start()
    return copies


def radiate_kernel(
    group,
    dens_hbm,
    radiate_ref,
    send_hbm,
    interp_hbm,
    shift_hbm,
    out_ref,
    rad,
    dens_ref,
    send_ref,
    interp_ref,
    shift_ref,
    summed,
    table,
    parent,
    sems,
    extra,
):
    boxes = rad.shape[0]
    width = rad.shape[2] // 2
    per_step = 4
    steps = boxes // per_step
    others = fetch(
        [(dens_hbm, dens_ref), (send_hbm, send_ref), (shift_hbm, shift_ref)], extra
    )
    copies = []
    for step in range(steps):
        part = pl.ds(step * per_step, per_step)
        copies.append(pltpu.make_async_copy(radiate_ref.at[part], rad.at[part], sems.at[step]))
        copies[-1].start()
    others += fetch([(interp_hbm, interp_ref)], extra, 3)
    others[0].wait()
    dens = dens_ref[...].astype(F32)
    owner = (iota(dens.shape, 0) // 2) % per_step
    blocks = jnp.concatenate([jnp.where(owner == b, dens, 0.0) for b in range(per_step)], 1)
    for step in range(steps):
        copies[step].wait()
        rows = slice(step * 2 * per_step, (step + 1) * 2 * per_step)
        weights = rad[step * per_step : (step + 1) * per_step].reshape(per_step * LANE, 2 * width)
        summed[rows] = dot_nn(blocks[rows].astype(BF16), weights).reshape(
            2 * per_step, 2 * width // LANE, LANE
        )
    chunks = width // LANE
    re_chunks, im_chunks = [], []
    for r in range(chunks):
        first_lo = summed[pl.ds(0, boxes, stride=2), r, :]
        first_hi = summed[pl.ds(0, boxes, stride=2), chunks + r, :]
        second_lo = summed[pl.ds(1, boxes, stride=2), r, :]
        second_hi = summed[pl.ds(1, boxes, stride=2), chunks + r, :]
        re_chunks.append((first_lo - second_hi).astype(BF16))
        im_chunks.append((first_hi + second_lo).astype(BF16))
    re_part = jnp.concatenate(re_chunks, 1)
    im_part = jnp.concatenate(im_chunks, 1)
    for r in range(chunks):
        table[pl.ds(r, boxes, stride=8), :] = re_chunks[r].astype(F32)
        table[pl.ds(chunks + r, boxes, stride=8), :] = im_chunks[r].astype(F32)
    table[pl.ds(boxes * 8, 8), :] = jnp.zeros((8, LANE), F32)
    for copy in others[1:]:
        copy.wait()
    wide = dot_nn(jnp.concatenate([re_part, im_part], 0), interp_ref[...])
    hi_chunks = wide.shape[1] // LANE
    parents = boxes // 8
    share = hi_chunks // group
    for r in range(hi_chunks):
        cols = slice(r * LANE, (r + 1) * LANE)
        s_re = shift_ref[pl.ds(2 * r, 8, stride=2 * hi_chunks), :]
        s_im = shift_ref[pl.ds(2 * r + 1, 8, stride=2 * hi_chunks), :]
        for p in range(parents):
            w_re = wide[p * 8 : (p + 1) * 8, cols]
            w_im = wide[boxes + p * 8 : boxes + (p + 1) * 8, cols]
            row = ((r // share) * parents + p) * 2 * share + r % share
            parent[row : row + 1] = jnp.sum(w_re * s_re - w_im * s_im, 0, keepdims=True)
            row += share
            parent[row : row + 1] = jnp.sum(w_re * s_im + w_im * s_re, 0, keepdims=True)
    slots, devices = send_ref.shape
    hi_rows = parents * 2 * share

    def fill(d, carry):
        for k in range(slots // 2):
            pair = [
                table[pl.ds(pl.multiple_of(send_ref[2 * k + h, d] * 8, 8), 8), :] for h in range(2)
            ]
            out_ref[d, 16 * k : 16 * (k + 1)] = jnp.concatenate(pair, 0).astype(BF16)
        member = pl.multiple_of(lax.rem(d, group) * hi_rows, 8)
        out_ref[d, 8 * slots : 8 * slots + hi_rows] = parent[pl.ds(member, hi_rows)].astype(BF16)
        return carry

    lax.fori_loop(0, devices, fill, 0, unroll=4)


def tally(index, source_row, type_row, sources, types):
    source = index[pl.ds(source_row, 1), :]
    kind = index[pl.ds(type_row, 1), :]
    faces = index.shape[1]
    by_source = jnp.where(iota((sources, faces), 0) == source, 1.0, 0.0).astype(BF16)
    by_type = jnp.where(iota((types, faces), 0) == kind, 1.0, 0.0).astype(BF16)
    return dot_nt(by_source, by_type).astype(BF16)


def index_kernel(
    types,
    group,
    box_total,
    near_src_hbm,
    near_tile_hbm,
    slot_hbm,
    type_hbm,
    par_far_hbm,
    par_type_hbm,
    op_lo_hbm,
    op_hi_hbm,
    code_ref,
    d_lo_hbm,
    d_ref,
    near_src_ref,
    near_tile_ref,
    slot_ref,
    type_ref,
    par_far_ref,
    par_type_ref,
    op_lo_ref,
    op_hi_ref,
    index,
    wide_lo,
    wide_hi,
    op_lo,
    op_hi,
    counts_hi,
    d_lo,
    sems,
    extra,
):
    others = fetch(
        [
            (op_lo_hbm, op_lo_ref),
            (near_src_hbm, near_src_ref),
            (near_tile_hbm, near_tile_ref),
            (slot_hbm, slot_ref),
            (type_hbm, type_ref),
            (par_far_hbm, par_far_ref),
            (par_type_hbm, par_type_ref),
            (op_hi_hbm, op_hi_ref),
        ],
        extra,
    )
    boxes, near = near_src_ref.shape
    rows, far = par_far_ref.shape
    parents, sources, _ = d_ref.shape
    slot_total = d_lo.shape[1]
    type_pad = op_hi.shape[0]
    chunks = op_lo.shape[1] // (2 * LANE)
    lines = op_hi_ref.shape[0] // types
    share = lines // (2 * group)
    tile_count = code_ref.shape[0] - 8
    samp = lax.axis_index("samp")
    position = lax.axis_index("box") * lax.axis_size("samp") + samp
    member = lax.rem(samp, group)
    first_parent = 2 * boxes + (samp - member) * (parents // group)
    place = member * (2 * share)
    base = place // 16 * 16
    index[...] = jnp.full(index.shape, -1, jnp.int32)
    tail = (type_pad - types) * 2 * chunks
    wide_lo[types * 2 * chunks : type_pad * 2 * chunks] = jnp.zeros((tail, LANE), F32)
    wide_hi[types * 16 : type_pad * 16] = jnp.zeros(((type_pad - types) * 16, LANE), F32)
    for copy in others[:7]:
        copy.wait()

    index[0:boxes, 0:far] = slot_ref[...]
    index[boxes : 2 * boxes, 0:far] = type_ref[...]
    index[2 * boxes : 2 * boxes + rows, 0:far] = par_far_ref[...]
    index[2 * boxes + rows : 2 * boxes + 2 * rows, 0:far] = par_type_ref[...]
    batch = 4

    wide_lo[0 : types * 2 * chunks] = op_lo_ref[...].astype(F32)
    for c in range(2):
        for r in range(chunks):
            col = (c * chunks + r) * LANE
            op_lo[:, col : col + LANE] = wide_lo[
                pl.ds(2 * r + c, type_pad, stride=2 * chunks), :
            ].astype(BF16)

    def lo_copy(step):
        part = pl.ds(step * batch, batch)
        return pltpu.make_async_copy(d_lo.at[part], d_lo_hbm.at[part], sems.at[step])

    def locate(g):
        for n in range(near):
            source = near_src_ref[g, n]
            live = source < box_total
            tile = jnp.where(live, near_tile_ref[g, n] - position * tile_count, tile_count)
            code_ref[tile] = g * 64 + source - (position - 1) * boxes

    def step_lists(step, carry):
        counts = []
        for k in range(batch):
            g = step * batch + k
            locate(g)
            counts.append(tally(index, g, boxes + g, slot_total, type_pad))
        counts = jnp.concatenate(counts, 0)
        part = 2 * chunks * LANE // batch
        for k in range(batch):
            p = step * batch + k
            at = pl.ds(pl.multiple_of(p * sources, sources), sources)
            row = first_parent + p
            counts_hi[at] = tally(index, row, rows + row, sources, type_pad)
            cols = slice(k * part, (k + 1) * part)
            d_lo[pl.ds(step * batch, batch), :, cols] = (
                dot_nn(counts, op_lo[:, cols]).astype(BF16).reshape(batch, slot_total, part)
            )
        lo_copy(step).start()
        return carry

    lax.fori_loop(0, boxes // batch, step_lists, 0)
    others[7].wait()

    def widen(t, carry):
        source = pl.ds(pl.multiple_of(t * lines + base, 16), 16)
        wide_hi[pl.ds(pl.multiple_of(t * 16, 16), 16)] = op_hi_ref[source].astype(F32)
        return carry

    lax.fori_loop(0, types, widen, 0, unroll=4)
    for c in range(2):
        for k in range(share):
            col = (c * share + k) * LANE
            start = place - base + 2 * k + c
            op_hi[:, col : col + LANE] = wide_hi[pl.ds(start, type_pad, stride=16), :].astype(BF16)

    def sum_parents(step, carry):
        at = pl.ds(pl.multiple_of(step * batch * sources, batch * sources), batch * sources)
        d_ref[pl.ds(step * batch, batch)] = dot_nn(counts_hi[at], op_hi[...]).reshape(
            batch, sources, 2 * share * LANE
        )
        return carry

    lax.fori_loop(0, parents // batch, sum_parents, 0)
    for step in range(boxes // batch):
        lo_copy(step).wait()


def parent_kernel(lo_lines, arrived_ref, d_ref, out_ref, wide):
    parents, sources, width = d_ref.shape
    share = width // (2 * LANE)
    rows = out_ref.shape[1]
    wide[...] = arrived_ref[:, lo_lines:, :].astype(F32).reshape(wide.shape)
    for k in range(share):
        first = wide[pl.ds(k, sources, stride=2 * share), :]
        second = wide[pl.ds(share + k, sources, stride=2 * share), :]
        for p in range(parents):
            o_re = d_ref[p, :, k * LANE : (k + 1) * LANE]
            o_im = d_ref[p, :, (share + k) * LANE : (share + k + 1) * LANE]
            row = p * 2 * share + k
            to, row = row // rows, row % rows
            out_ref[to, row : row + 1] = jnp.sum(o_re * first - o_im * second, 0, keepdims=True)
            row += share
            out_ref[to, row : row + 1] = jnp.sum(o_re * second + o_im * first, 0, keepdims=True)


def middle_kernel(
    even_ref,
    dens_hbm,
    odd_ref,
    tiles_hbm,
    code_hbm,
    d_lo_hbm,
    arrived_ref,
    near_ref,
    incoming_ref,
    tiles,
    halo,
    dens3,
    left,
    right,
    acc,
    code,
    d_lo,
    slots,
    received,
    sems,
    lo_sems,
    extra,
):
    boxes = near_ref.shape[0] // 2
    tile_count = tiles.shape[0]
    steps = sems.shape[0]
    per_step = tile_count // steps
    odd = lax.rem(lax.axis_index("samp"), 2)
    others = fetch(
        [
            (code_hbm, code),
            (even_ref, halo.at[2 - 2 * odd]),
            (dens_hbm, halo.at[1]),
            (odd_ref, halo.at[2 * odd]),
        ],
        extra,
    )

    def tile_copy(step):
        part = pl.ds(step * per_step, per_step)
        return pltpu.make_async_copy(tiles_hbm.at[part], tiles.at[part], sems.at[step])

    per_boxes = boxes // steps

    def lo_copy(step):
        part = pl.ds(step * per_boxes, per_boxes)
        return pltpu.make_async_copy(d_lo_hbm.at[part], d_lo.at[part], lo_sems.at[step])

    for step in range(steps):
        tile_copy(step).start()
        lo_copy(step).start()
    acc[...] = jnp.zeros(acc.shape, F32)
    left[...] = jnp.zeros(left.shape, F32)
    right[...] = jnp.zeros(right.shape, F32)
    lo_lines = slots.shape[0] // arrived_ref.shape[0]
    slots[...] = arrived_ref[:, :lo_lines, :].astype(F32).reshape(slots.shape)
    for copy in others:
        copy.wait()
    for k in range(3):
        dens3[pl.ds(2 * boxes * k, 2 * boxes), :] = halo[k].astype(F32)
    first = dens3[pl.ds(0, 3 * boxes, stride=2), :]
    second = dens3[pl.ds(1, 3 * boxes, stride=2), :]
    left[pl.ds(0, 3 * boxes, stride=8), :] = first
    left[pl.ds(1, 3 * boxes, stride=8), :] = second
    right[pl.ds(0, 3 * boxes, stride=8), :] = -second
    right[pl.ds(1, 3 * boxes, stride=8), :] = first

    chunks = d_lo.shape[2] // (2 * LANE)
    slot_total = d_lo.shape[1]
    for r in range(2 * chunks):
        received[:, r * LANE : (r + 1) * LANE] = slots[pl.ds(r, slot_total, stride=2 * chunks), :]

    def step_boxes(step, carry):
        start = step * per_boxes
        tile_copy(step).wait()
        lo_copy(step).wait()

        def multiply_pair(pair):
            tile = step * per_step + 2 * pair
            both = tiles[pl.ds(tile, 2)]
            weights = jnp.concatenate(
                [both[:, 0].reshape(2 * LANE, LANE), both[:, 1].reshape(2 * LANE, LANE)], 1
            )
            owners, lefts, rights = [], [], []
            for h in range(2):
                entry = code[tile + h]
                row = pl.ds(pl.multiple_of((entry & 63) * 8, 8), 8)
                owners.append(entry >> 6)
                lefts.append(left[row])
                rights.append(right[row])
            lhs = jnp.concatenate([jnp.concatenate(lefts, 0), jnp.concatenate(rights, 0)], 1)
            product = dot_nt(lhs.astype(BF16), weights)
            for h in range(2):
                acc[owners[h]] = (
                    acc[owners[h]] + product[8 * h : 8 * (h + 1), h * LANE : (h + 1) * LANE]
                )

        def multiply_slots(r, k):
            first = received[:, r * LANE : (r + 1) * LANE]
            second = received[:, (chunks + r) * LANE : (chunks + r + 1) * LANE]
            o_re = d_lo[start + k, :, r * LANE : (r + 1) * LANE].astype(F32)
            o_im = d_lo[start + k, :, (chunks + r) * LANE : (chunks + r + 1) * LANE].astype(F32)
            incoming_ref[start + k, r : r + 1] = jnp.sum(
                o_re * first - o_im * second, 0, keepdims=True
            )
            incoming_ref[boxes + start + k, r : r + 1] = jnp.sum(
                o_re * second + o_im * first, 0, keepdims=True
            )

        pairs = per_step // 2
        parts = [(r, k) for r in range(chunks) for k in range(per_boxes)]
        done = 0
        for pair in range(pairs):
            multiply_pair(pair)
            upto = len(parts) * (pair + 1) // pairs
            for r, k in parts[done:upto]:
                multiply_slots(r, k)
            done = upto
        return carry

    lax.fori_loop(0, steps, step_boxes, 0)
    for g in range(boxes):
        row = 2 * g
        near_ref[row : row + 2] = acc[g, 0:2] + 0.5 * dens3[pl.ds(2 * boxes + row, 2), :]


def last_kernel(
    parent_ref,
    incoming_ref,
    shift_hbm,
    interp_hbm,
    receive_ref,
    near_ref,
    out_ref,
    receive,
    shift_ref,
    interp_ref,
    down,
    blend,
    sems,
    extra,
):
    boxes = receive.shape[0]
    per_step = 4
    steps = boxes // per_step
    others = fetch([(shift_hbm, shift_ref), (interp_hbm, interp_ref)], extra)
    copies = []
    for step in range(steps):
        part = pl.ds(step * per_step, per_step)
        copies.append(pltpu.make_async_copy(receive_ref.at[part], receive.at[part], sems.at[step]))
        copies[-1].start()
    own_parents = boxes // 8
    hi_chunks = down.shape[1] // LANE
    chunks = incoming_ref.shape[1]
    share = hi_chunks // parent_ref.shape[0]
    others[0].wait()
    for r in range(hi_chunks):
        s_re = shift_ref[pl.ds(2 * r, 8, stride=2 * hi_chunks), :]
        s_im = shift_ref[pl.ds(2 * r + 1, 8, stride=2 * hi_chunks), :]
        re_rows, im_rows = [], []
        for p in range(own_parents):
            row = p * 2 * share + r % share
            t_re = parent_ref[r // share, row : row + 1]
            t_im = parent_ref[r // share, row + share : row + share + 1]
            re_rows.append(s_re * t_re + s_im * t_im)
            im_rows.append(s_re * t_im - s_im * t_re)
        cols = slice(r * LANE, (r + 1) * LANE)
        down[:, cols] = jnp.concatenate(re_rows + im_rows, 0).astype(BF16)
    others[1].wait()
    total = jnp.concatenate([incoming_ref[:, r, :] for r in range(chunks)], 1)
    total = total + dot_nt(down[...], interp_ref[...])
    total = total.astype(BF16).astype(F32)
    for r in range(chunks):
        re_part = total[:boxes, r * LANE : (r + 1) * LANE]
        im_part = total[boxes:, r * LANE : (r + 1) * LANE]
        blend[pl.ds(0, boxes, stride=2), r, :] = re_part
        blend[pl.ds(1, boxes, stride=2), r, :] = im_part
        blend[pl.ds(0, boxes, stride=2), chunks + r, :] = -im_part
        blend[pl.ds(1, boxes, stride=2), chunks + r, :] = re_part
    owner = (iota((2 * per_step, LANE), 0) // 2) % per_step
    for step in range(steps):
        rows = slice(step * 2 * per_step, (step + 1) * 2 * per_step)
        lhs = jnp.concatenate([blend[rows, r, :] for r in range(2 * chunks)], 1).astype(BF16)
        copies[step].wait()
        weights = receive[step * per_step : (step + 1) * per_step]
        product = dot_nt(lhs, weights.reshape(per_step * LANE, 2 * chunks * LANE))
        total = near_ref[rows]
        for b in range(per_step):
            total = total + jnp.where(owner == b, product[:, b * LANE : (b + 1) * LANE], 0.0)
        out_ref[rows] = total


def in_hbm(array):
    return pltpu.with_memory_space_constraint(array, pltpu.HBM)


def in_vmem(array):
    return pltpu.with_memory_space_constraint(array, pltpu.VMEM)


def tiled_rows(array):
    count, parts, width = array.shape
    cut = array.reshape(count, parts, width // LANE, LANE)
    return cut.transpose(0, 2, 1, 3).reshape(-1, LANE)


def on_device(
    density,
    radiate,
    receive,
    near_tiles,
    near_src,
    near_tile,
    send_box,
    distant_pattern_slot,
    far_type,
    trans_lo,
    interp_matrix,
    shifts,
    par_far,
    par_type,
    trans_hi,
):
    boxes, _, panels = density.shape
    devices = lax.axis_size("box") * lax.axis_size("samp")
    slots = send_box.shape[2]
    types, _, width_lo = trans_lo.shape
    width_hi = trans_hi.shape[2]
    parents = boxes // 8
    slot_total = devices * slots
    par_total = devices * parents
    type_pad = -(-types // 8) * 8
    samp_count = lax.axis_size("samp")
    group = min(samp_count, 8)
    share = width_hi // LANE // group
    lo_lines = slots * 2 * width_lo // LANE
    hi_lines = parents * 2 * share
    lines = lo_lines + hi_lines
    members = None
    if group < samp_count:
        members = [list(range(k, k + group)) for k in range(0, samp_count, group)]
    rows = density.reshape(boxes * 2, panels)
    shift_rows = tiled_rows(shifts)
    send = send_box[0].T
    outgoing = pl.pallas_call(
        functools.partial(radiate_kernel, group),
        out_shape=jax.ShapeDtypeStruct((devices, lines, LANE), BF16),
        in_specs=[HBM_SPEC] * 5,
        out_specs=VMEM_SPEC,
        scratch_shapes=[
            pltpu.VMEM(radiate.shape, BF16),
            pltpu.VMEM(rows.shape, BF16),
            pltpu.SMEM(send.shape, jnp.int32),
            pltpu.VMEM(interp_matrix.shape, BF16),
            pltpu.VMEM(shift_rows.shape, F32),
            pltpu.VMEM((2 * boxes, 2 * width_lo // LANE, LANE), F32),
            pltpu.VMEM((boxes * 8 + 8, LANE), F32),
            pltpu.VMEM((parents * 2 * width_hi // LANE, LANE), F32),
            pltpu.SemaphoreType.DMA((boxes // 4,)),
            pltpu.SemaphoreType.DMA((4,)),
        ],
        compiler_params=pltpu.CompilerParams(vmem_limit_bytes=12 * MIB),
        cost_estimate=pl.CostEstimate(flops=10**9, bytes_accessed=8 * MIB, transcendentals=0),
    )(*(in_hbm(x) for x in (rows, radiate, send, interp_matrix, shift_rows)))
    arrived = lax.all_to_all(outgoing, ("box", "samp"), split_axis=0, concat_axis=0, tiled=True)
    tile_count = near_tiles.shape[0]
    far = far_type.shape
    op_hi_rows = tiled_rows(trans_hi)
    op_lo_rows = tiled_rows(trans_lo)
    code, d_lo, d_hi = pl.pallas_call(
        functools.partial(index_kernel, types, group, boxes * devices),
        out_shape=(
            jax.ShapeDtypeStruct((tile_count + 8,), jnp.int32),
            pltpu.HBM((boxes, slot_total, 2 * width_lo), BF16),
            pltpu.VMEM((parents * group, par_total, 2 * share * LANE), F32),
        ),
        in_specs=[HBM_SPEC] * 8,
        out_specs=(SMEM_SPEC, HBM_SPEC, VMEM_SPEC),
        scratch_shapes=[
            pltpu.SMEM(near_src.shape, jnp.int32),
            pltpu.SMEM(near_src.shape, jnp.int32),
            pltpu.VMEM(far, jnp.int32),
            pltpu.VMEM(far, jnp.int32),
            pltpu.VMEM(par_far.shape, jnp.int32),
            pltpu.VMEM(par_far.shape, jnp.int32),
            pltpu.VMEM(op_lo_rows.shape, BF16),
            pltpu.VMEM(op_hi_rows.shape, BF16),
            pltpu.VMEM((2 * boxes + 2 * par_far.shape[0], 2 * LANE), jnp.int32),
            pltpu.VMEM((type_pad * 2 * width_lo // LANE, LANE), F32),
            pltpu.VMEM((type_pad * 16, LANE), F32),
            pltpu.VMEM((type_pad, 2 * width_lo), BF16),
            pltpu.VMEM((type_pad, 2 * share * LANE), BF16),
            pltpu.VMEM((parents * group * par_total, type_pad), BF16),
            pltpu.VMEM((boxes, slot_total, 2 * width_lo), BF16),
            pltpu.SemaphoreType.DMA((boxes // 4,)),
            pltpu.SemaphoreType.DMA((8,)),
        ],
        compiler_params=pltpu.CompilerParams(
            vmem_limit_bytes=(20 if slot_total <= 128 else 46) * MIB
        ),
        cost_estimate=pl.CostEstimate(flops=10**9, bytes_accessed=16 * MIB, transcendentals=0),
    )(
        *(
            in_hbm(x)
            for x in (
                near_src,
                near_tile,
                distant_pattern_slot,
                far_type,
                par_far,
                par_type,
                op_lo_rows,
                op_hi_rows,
            )
        )
    )
    above = pl.pallas_call(
        functools.partial(parent_kernel, lo_lines),
        out_shape=jax.ShapeDtypeStruct((group, hi_lines, LANE), F32),
        in_specs=[VMEM_SPEC] * 2,
        out_specs=VMEM_SPEC,
        scratch_shapes=[pltpu.VMEM((devices * hi_lines, LANE), F32)],
        compiler_params=pltpu.CompilerParams(vmem_limit_bytes=4 * MIB),
        cost_estimate=pl.CostEstimate(flops=10**8, bytes_accessed=MIB, transcendentals=0),
    )(arrived, in_vmem(d_hi))
    above, near_rows = lax.optimization_barrier((above, rows))
    even = exchanged(near_rows, ("box", "samp"), 0)
    odd = exchanged(near_rows, ("box", "samp"), 1)
    own_above = lax.all_to_all(
        above, "samp", split_axis=0, concat_axis=0, axis_index_groups=members, tiled=True
    )
    steps = 4
    near, incoming = pl.pallas_call(
        middle_kernel,
        out_shape=(
            jax.ShapeDtypeStruct((2 * boxes, panels), F32),
            jax.ShapeDtypeStruct((2 * boxes, width_lo // LANE, LANE), F32),
        ),
        in_specs=[ANY_SPEC, HBM_SPEC, ANY_SPEC, HBM_SPEC, ANY_SPEC, HBM_SPEC, VMEM_SPEC],
        out_specs=(VMEM_SPEC,) * 2,
        scratch_shapes=[
            pltpu.VMEM(near_tiles.shape, BF16),
            pltpu.VMEM((3, 2 * boxes, panels), BF16),
            pltpu.VMEM((6 * boxes, panels), F32),
            pltpu.VMEM((3 * boxes * 8, LANE), F32),
            pltpu.VMEM((3 * boxes * 8, LANE), F32),
            pltpu.VMEM((boxes, 8, LANE), F32),
            pltpu.SMEM((tile_count + 8,), jnp.int32),
            pltpu.VMEM((boxes, slot_total, 2 * width_lo), BF16),
            pltpu.VMEM((devices * lo_lines, LANE), F32),
            pltpu.VMEM((slot_total, 2 * width_lo), F32),
            pltpu.SemaphoreType.DMA((steps,)),
            pltpu.SemaphoreType.DMA((steps,)),
            pltpu.SemaphoreType.DMA((4,)),
        ],
        compiler_params=pltpu.CompilerParams(
            vmem_limit_bytes=(24 if slot_total <= 128 else 42) * MIB
        ),
        cost_estimate=pl.CostEstimate(flops=10**10, bytes_accessed=20 * MIB, transcendentals=0),
    )(
        even,
        in_hbm(rows),
        odd,
        in_hbm(near_tiles),
        code,
        in_hbm(d_lo),
        arrived,
    )
    field = pl.pallas_call(
        last_kernel,
        out_shape=jax.ShapeDtypeStruct((2 * boxes, panels), F32),
        in_specs=[VMEM_SPEC] * 2 + [HBM_SPEC] * 3 + [VMEM_SPEC],
        out_specs=VMEM_SPEC,
        scratch_shapes=[
            pltpu.VMEM(receive.shape, BF16),
            pltpu.VMEM(shift_rows.shape, F32),
            pltpu.VMEM(interp_matrix.shape, BF16),
            pltpu.VMEM((2 * boxes, width_hi), BF16),
            pltpu.VMEM((2 * boxes, 2 * width_lo // LANE, LANE), F32),
            pltpu.SemaphoreType.DMA((boxes // 4,)),
            pltpu.SemaphoreType.DMA((2,)),
        ],
        compiler_params=pltpu.CompilerParams(vmem_limit_bytes=12 * MIB),
        cost_estimate=pl.CostEstimate(flops=10**9, bytes_accessed=8 * MIB, transcendentals=0),
    )(own_above, incoming, shift_rows, interp_matrix, in_hbm(receive), near)
    return field.reshape(boxes, 2, panels)


def solution(mesh):
    both = ("box", "samp")
    return jax.shard_map(
        on_device,
        mesh=mesh,
        in_specs=(
            P(both, None, None),
            P(both, None, None),
            P(both, None, None),
            P(both, None, None, None),
            P(both, None),
            P(both, None),
            P(both, None, None),
            P(both, None),
            P(both, None),
            P(),
            P(),
            P(),
            P("box", None),
            P("box", None),
            P(),
        ),
        out_specs=P(both, None, None),
        check_vma=False,
    )
```

```python
import functools

import jax
import jax.numpy as jnp
from jax import lax
from jax.experimental import pallas as pl
from jax.experimental.pallas import tpu as pltpu
from jax.sharding import PartitionSpec as P

F32 = jnp.float32
BF16 = jnp.bfloat16
LANE = 128
VMEM_SPEC = pl.BlockSpec(memory_space=pltpu.VMEM)
SMEM_SPEC = pl.BlockSpec(memory_space=pltpu.SMEM)
ANY_SPEC = pl.BlockSpec(memory_space=pl.ANY)
HBM_SPEC = pl.BlockSpec(memory_space=pltpu.HBM)
MIB = 1 << 20


def iota(shape, dim):
    return lax.broadcasted_iota(jnp.int32, shape, dim)


def dot_nn(lhs, rhs):
    return lax.dot_general(lhs, rhs, (((1,), (0,)), ((), ())), preferred_element_type=F32)


def dot_nt(lhs, rhs):
    return lax.dot_general(lhs, rhs, (((1,), (1,)), ((), ())), preferred_element_type=F32)


def exchanged(value, axes, first):
    count = lax.axis_size(axes)
    pairs = []
    for low in range(first, count - 1, 2):
        pairs += [(low, low + 1), (low + 1, low)]
    return lax.ppermute(value, axes, pairs)


def fetch(pairs, sems, first=0):
    copies = []
    for k, (source, target) in enumerate(pairs):
        copies.append(pltpu.make_async_copy(source, target, sems.at[first + k]))
        copies[-1].start()
    return copies


def radiate_kernel(
    group,
    dens_hbm,
    radiate_ref,
    send_hbm,
    interp_hbm,
    shift_hbm,
    out_ref,
    rad,
    dens_ref,
    send_ref,
    interp_ref,
    shift_ref,
    summed,
    table,
    parent,
    sems,
    extra,
):
    boxes = rad.shape[0]
    width = rad.shape[2] // 2
    per_step = 4
    steps = boxes // per_step
    others = fetch(
        [(dens_hbm, dens_ref), (send_hbm, send_ref), (shift_hbm, shift_ref)], extra
    )
    copies = []
    for step in range(steps):
        part = pl.ds(step * per_step, per_step)
        copies.append(pltpu.make_async_copy(radiate_ref.at[part], rad.at[part], sems.at[step]))
        copies[-1].start()
    others += fetch([(interp_hbm, interp_ref)], extra, 3)
    others[0].wait()
    dens = dens_ref[...].astype(F32)
    owner = (iota(dens.shape, 0) // 2) % per_step
    blocks = jnp.concatenate([jnp.where(owner == b, dens, 0.0) for b in range(per_step)], 1)
    for step in range(steps):
        copies[step].wait()
        rows = slice(step * 2 * per_step, (step + 1) * 2 * per_step)
        weights = rad[step * per_step : (step + 1) * per_step].reshape(per_step * LANE, 2 * width)
        summed[rows] = dot_nn(blocks[rows].astype(BF16), weights).reshape(
            2 * per_step, 2 * width // LANE, LANE
        )
    chunks = width // LANE
    re_chunks, im_chunks = [], []
    for r in range(chunks):
        first_lo = summed[pl.ds(0, boxes, stride=2), r, :]
        first_hi = summed[pl.ds(0, boxes, stride=2), chunks + r, :]
        second_lo = summed[pl.ds(1, boxes, stride=2), r, :]
        second_hi = summed[pl.ds(1, boxes, stride=2), chunks + r, :]
        re_chunks.append((first_lo - second_hi).astype(BF16))
        im_chunks.append((first_hi + second_lo).astype(BF16))
    re_part = jnp.concatenate(re_chunks, 1)
    im_part = jnp.concatenate(im_chunks, 1)
    for r in range(chunks):
        table[pl.ds(r, boxes, stride=8), :] = re_chunks[r].astype(F32)
        table[pl.ds(chunks + r, boxes, stride=8), :] = im_chunks[r].astype(F32)
    table[pl.ds(boxes * 8, 8), :] = jnp.zeros((8, LANE), F32)
    for copy in others[1:]:
        copy.wait()
    wide = dot_nn(jnp.concatenate([re_part, im_part], 0), interp_ref[...])
    hi_chunks = wide.shape[1] // LANE
    parents = boxes // 8
    share = hi_chunks // group
    for r in range(hi_chunks):
        cols = slice(r * LANE, (r + 1) * LANE)
        s_re = shift_ref[pl.ds(2 * r, 8, stride=2 * hi_chunks), :]
        s_im = shift_ref[pl.ds(2 * r + 1, 8, stride=2 * hi_chunks), :]
        for p in range(parents):
            w_re = wide[p * 8 : (p + 1) * 8, cols]
            w_im = wide[boxes + p * 8 : boxes + (p + 1) * 8, cols]
            row = ((r // share) * parents + p) * 2 * share + r % share
            parent[row : row + 1] = jnp.sum(w_re * s_re - w_im * s_im, 0, keepdims=True)
            row += share
            parent[row : row + 1] = jnp.sum(w_re * s_im + w_im * s_re, 0, keepdims=True)
    slots, devices = send_ref.shape
    hi_rows = parents * 2 * share

    def fill(d, carry):
        for k in range(slots // 2):
            pair = [
                table[pl.ds(pl.multiple_of(send_ref[2 * k + h, d] * 8, 8), 8), :] for h in range(2)
            ]
            out_ref[d, 16 * k : 16 * (k + 1)] = jnp.concatenate(pair, 0).astype(BF16)
        member = pl.multiple_of(lax.rem(d, group) * hi_rows, 8)
        out_ref[d, 8 * slots : 8 * slots + hi_rows] = parent[pl.ds(member, hi_rows)].astype(BF16)
        return carry

    lax.fori_loop(0, devices, fill, 0, unroll=4)


def tally(index, source_row, type_row, sources, types):
    source = index[pl.ds(source_row, 1), :]
    kind = index[pl.ds(type_row, 1), :]
    faces = index.shape[1]
    by_source = jnp.where(iota((sources, faces), 0) == source, 1.0, 0.0).astype(BF16)
    by_type = jnp.where(iota((types, faces), 0) == kind, 1.0, 0.0).astype(BF16)
    return dot_nt(by_source, by_type).astype(BF16)


def index_kernel(
    types,
    group,
    slot_hbm,
    type_hbm,
    par_far_hbm,
    par_type_hbm,
    op_lo_hbm,
    op_hi_hbm,
    d_lo_hbm,
    d_ref,
    slot_ref,
    type_ref,
    par_far_ref,
    par_type_ref,
    op_lo_ref,
    op_hi_ref,
    index,
    wide_lo,
    wide_hi,
    op_lo,
    op_hi,
    counts_hi,
    d_lo,
    sems,
    extra,
):
    others = fetch(
        [
            (op_lo_hbm, op_lo_ref),
            (slot_hbm, slot_ref),
            (type_hbm, type_ref),
            (par_far_hbm, par_far_ref),
            (par_type_hbm, par_type_ref),
            (op_hi_hbm, op_hi_ref),
        ],
        extra,
    )
    boxes = slot_ref.shape[0]
    rows, far = par_far_ref.shape
    parents, sources, _ = d_ref.shape
    slot_total = d_lo.shape[1]
    type_pad = op_hi.shape[0]
    chunks = op_lo.shape[1] // (2 * LANE)
    lines = op_hi_ref.shape[0] // types
    share = lines // (2 * group)
    samp = lax.axis_index("samp")
    member = lax.rem(samp, group)
    first_parent = 2 * boxes + (samp - member) * (parents // group)
    place = member * (2 * share)
    base = place // 16 * 16
    index[...] = jnp.full(index.shape, -1, jnp.int32)
    tail = (type_pad - types) * 2 * chunks
    wide_lo[types * 2 * chunks : type_pad * 2 * chunks] = jnp.zeros((tail, LANE), F32)
    wide_hi[types * 16 : type_pad * 16] = jnp.zeros(((type_pad - types) * 16, LANE), F32)
    for copy in others[:5]:
        copy.wait()

    index[0:boxes, 0:far] = slot_ref[...]
    index[boxes : 2 * boxes, 0:far] = type_ref[...]
    index[2 * boxes : 2 * boxes + rows, 0:far] = par_far_ref[...]
    index[2 * boxes + rows : 2 * boxes + 2 * rows, 0:far] = par_type_ref[...]
    batch = 4
    share_parents = parents * batch // boxes

    wide_lo[0 : types * 2 * chunks] = op_lo_ref[...].astype(F32)
    for c in range(2):
        for r in range(chunks):
            col = (c * chunks + r) * LANE
            op_lo[:, col : col + LANE] = wide_lo[
                pl.ds(2 * r + c, type_pad, stride=2 * chunks), :
            ].astype(BF16)

    def lo_copy(step):
        part = pl.ds(step * batch, batch)
        return pltpu.make_async_copy(d_lo.at[part], d_lo_hbm.at[part], sems.at[step])

    def step_lists(step, carry):
        counts = []
        for k in range(batch):
            g = step * batch + k
            counts.append(tally(index, g, boxes + g, slot_total, type_pad))
        counts = jnp.concatenate(counts, 0)
        part = 2 * chunks * LANE // batch
        for k in range(batch):
            cols = slice(k * part, (k + 1) * part)
            d_lo[pl.ds(step * batch, batch), :, cols] = (
                dot_nn(counts, op_lo[:, cols]).astype(BF16).reshape(batch, slot_total, part)
            )
            if k < share_parents:
                p = step * share_parents + k
                at = pl.ds(pl.multiple_of(p * sources, sources), sources)
                row = first_parent + p
                counts_hi[at] = tally(index, row, rows + row, sources, type_pad)
        lo_copy(step).start()
        return carry

    lax.fori_loop(0, boxes // batch, step_lists, 0)
    others[5].wait()

    def widen(t, carry):
        source = pl.ds(pl.multiple_of(t * lines + base, 16), 16)
        wide_hi[pl.ds(pl.multiple_of(t * 16, 16), 16)] = op_hi_ref[source].astype(F32)
        return carry

    lax.fori_loop(0, types, widen, 0, unroll=4)
    for c in range(2):
        for k in range(share):
            col = (c * share + k) * LANE
            start = place - base + 2 * k + c
            op_hi[:, col : col + LANE] = wide_hi[pl.ds(start, type_pad, stride=16), :].astype(BF16)

    for first in range(0, 2 * share * LANE, 2 * LANE):
        cols = slice(first, first + 2 * LANE)
        d_ref[:, :, cols] = dot_nn(counts_hi[...], op_hi[:, cols]).reshape(
            parents, sources, 2 * LANE
        )
    for step in range(boxes // batch):
        lo_copy(step).wait()


def parent_kernel(lo_lines, arrived_ref, d_ref, mine_ref, theirs_ref, wide):
    parents, sources, width = d_ref.shape
    share = width // (2 * LANE)
    own = parents // 2
    member = lax.rem(lax.axis_index("samp"), 2)
    wide[...] = arrived_ref[:, lo_lines:, :].astype(F32).reshape(wide.shape)
    for k in range(share):
        first = wide[pl.ds(k, sources, stride=2 * share), :]
        second = wide[pl.ds(share + k, sources, stride=2 * share), :]
        for out_ref, start in ((theirs_ref, (1 - member) * own), (mine_ref, member * own)):
            for q in range(own):
                o_re = d_ref[start + q, :, k * LANE : (k + 1) * LANE]
                o_im = d_ref[start + q, :, (share + k) * LANE : (share + k + 1) * LANE]
                row = q * 2 * share + k
                out_ref[row : row + 1] = jnp.sum(o_re * first - o_im * second, 0, keepdims=True)
                row += share
                out_ref[row : row + 1] = jnp.sum(o_re * second + o_im * first, 0, keepdims=True)


def near_kernel(
    box_total,
    even_ref,
    dens_hbm,
    odd_ref,
    near_src_hbm,
    near_tile_hbm,
    tiles_hbm,
    near_ref,
    tiles,
    halo,
    near_src_ref,
    near_tile_ref,
    dens3,
    left,
    right,
    acc,
    code,
    sems,
    extra,
):
    boxes, near = near_src_ref.shape
    tile_count = tiles.shape[0]
    steps = sems.shape[0]
    per_step = tile_count // steps
    samp = lax.axis_index("samp")
    position = lax.axis_index("box") * lax.axis_size("samp") + samp
    odd = lax.rem(samp, 2)
    others = fetch(
        [
            (near_src_hbm, near_src_ref),
            (near_tile_hbm, near_tile_ref),
            (even_ref, halo.at[2 - 2 * odd]),
            (dens_hbm, halo.at[1]),
            (odd_ref, halo.at[2 * odd]),
        ],
        extra,
    )

    def tile_copy(step):
        part = pl.ds(step * per_step, per_step)
        return pltpu.make_async_copy(tiles_hbm.at[part], tiles.at[part], sems.at[step])

    for step in range(steps):
        tile_copy(step).start()
    acc[...] = jnp.zeros(acc.shape, F32)
    left[...] = jnp.zeros(left.shape, F32)
    right[...] = jnp.zeros(right.shape, F32)
    for copy in others:
        copy.wait()
    for k in range(3):
        dens3[pl.ds(2 * boxes * k, 2 * boxes), :] = halo[k].astype(F32)
    first = dens3[pl.ds(0, 3 * boxes, stride=2), :]
    second = dens3[pl.ds(1, 3 * boxes, stride=2), :]
    left[pl.ds(0, 3 * boxes, stride=8), :] = first
    left[pl.ds(1, 3 * boxes, stride=8), :] = second
    right[pl.ds(0, 3 * boxes, stride=8), :] = -second
    right[pl.ds(1, 3 * boxes, stride=8), :] = first


    def locate(g, carry):
        for n in range(near):
            source = near_src_ref[g, n]
            live = source < box_total
            tile = jnp.where(live, near_tile_ref[g, n] - position * tile_count, tile_count)
            code[tile] = g * 64 + source - (position - 1) * boxes
        return carry

    lax.fori_loop(0, boxes, locate, 0)

    def multiply_pair(tile):
        both = tiles[pl.ds(tile, 2)]
        weights = jnp.concatenate(
            [both[:, 0].reshape(2 * LANE, LANE), both[:, 1].reshape(2 * LANE, LANE)], 1
        )
        owners, lefts, rights = [], [], []
        for h in range(2):
            entry = code[tile + h]
            row = pl.ds(pl.multiple_of((entry & 63) * 8, 8), 8)
            owners.append(entry >> 6)
            lefts.append(left[row])
            rights.append(right[row])
        lhs = jnp.concatenate([jnp.concatenate(lefts, 0), jnp.concatenate(rights, 0)], 1)
        product = dot_nt(lhs.astype(BF16), weights)
        for h in range(2):
            acc[owners[h]] = (
                acc[owners[h]] + product[8 * h : 8 * (h + 1), h * LANE : (h + 1) * LANE]
            )


    def step_tiles(step, carry):
        tile_copy(step).wait()
        for pair in range(per_step // 2):
            multiply_pair(step * per_step + 2 * pair)
        return carry

    lax.fori_loop(0, steps, step_tiles, 0)
    for g in range(boxes):
        row = 2 * g
        near_ref[row : row + 2] = acc[g, 0:2] + 0.5 * dens3[pl.ds(2 * boxes + row, 2), :]


def leaf_kernel(d_lo_hbm, arrived_ref, incoming_ref, d_lo, slots, received, sems):
    boxes, slot_total, width = d_lo.shape
    chunks = width // (2 * LANE)
    steps = sems.shape[0]
    per_boxes = boxes // steps
    copies = []
    for step in range(steps):
        part = pl.ds(step * per_boxes, per_boxes)
        copies.append(pltpu.make_async_copy(d_lo_hbm.at[part], d_lo.at[part], sems.at[step]))
        copies[-1].start()
    lo_lines = slots.shape[0] // arrived_ref.shape[0]
    slots[...] = arrived_ref[:, :lo_lines, :].astype(F32).reshape(slots.shape)
    for r in range(2 * chunks):
        received[:, r * LANE : (r + 1) * LANE] = slots[pl.ds(r, slot_total, stride=2 * chunks), :]

    def multiply_slots(r, g):
        first = received[:, r * LANE : (r + 1) * LANE]
        second = received[:, (chunks + r) * LANE : (chunks + r + 1) * LANE]
        o_re = d_lo[g, :, r * LANE : (r + 1) * LANE].astype(F32)
        o_im = d_lo[g, :, (chunks + r) * LANE : (chunks + r + 1) * LANE].astype(F32)
        incoming_ref[g, r : r + 1] = jnp.sum(
            o_re * first - o_im * second, 0, keepdims=True
        )
        incoming_ref[boxes + g, r : r + 1] = jnp.sum(
            o_re * second + o_im * first, 0, keepdims=True
        )

    for step in range(steps):
        copies[step].wait()
        for r in range(chunks):
            for k in range(per_boxes):
                multiply_slots(r, step * per_boxes + k)


def last_kernel(
    mine_ref,
    other_ref,
    incoming_ref,
    shift_hbm,
    interp_hbm,
    receive_ref,
    near_ref,
    out_ref,
    receive,
    shift_ref,
    interp_ref,
    parent_ref,
    down,
    blend,
    sems,
    extra,
):
    boxes = receive.shape[0]
    per_step = 4
    steps = boxes // per_step
    others = fetch([(shift_hbm, shift_ref), (interp_hbm, interp_ref)], extra)
    copies = []
    for step in range(steps):
        part = pl.ds(step * per_step, per_step)
        copies.append(pltpu.make_async_copy(receive_ref.at[part], receive.at[part], sems.at[step]))
        copies[-1].start()
    member = lax.rem(lax.axis_index("samp"), 2)
    parent_ref[member] = mine_ref[...]
    parent_ref[1 - member] = other_ref[...]
    own_parents = boxes // 8
    hi_chunks = down.shape[1] // LANE
    chunks = incoming_ref.shape[1]
    share = hi_chunks // parent_ref.shape[0]
    others[0].wait()
    for r in range(hi_chunks):
        s_re = shift_ref[pl.ds(2 * r, 8, stride=2 * hi_chunks), :]
        s_im = shift_ref[pl.ds(2 * r + 1, 8, stride=2 * hi_chunks), :]
        re_rows, im_rows = [], []
        for p in range(own_parents):
            row = p * 2 * share + r % share
            t_re = parent_ref[r // share, row : row + 1]
            t_im = parent_ref[r // share, row + share : row + share + 1]
            re_rows.append(s_re * t_re + s_im * t_im)
            im_rows.append(s_re * t_im - s_im * t_re)
        cols = slice(r * LANE, (r + 1) * LANE)
        down[:, cols] = jnp.concatenate(re_rows + im_rows, 0).astype(BF16)
    others[1].wait()
    total = jnp.concatenate([incoming_ref[:, r, :] for r in range(chunks)], 1)
    total = total + dot_nt(down[...], interp_ref[...])
    total = total.astype(BF16).astype(F32)
    for r in range(chunks):
        re_part = total[:boxes, r * LANE : (r + 1) * LANE]
        im_part = total[boxes:, r * LANE : (r + 1) * LANE]
        blend[pl.ds(0, boxes, stride=2), r, :] = re_part
        blend[pl.ds(1, boxes, stride=2), r, :] = im_part
        blend[pl.ds(0, boxes, stride=2), chunks + r, :] = -im_part
        blend[pl.ds(1, boxes, stride=2), chunks + r, :] = re_part
    owner = (iota((2 * per_step, LANE), 0) // 2) % per_step
    for step in range(steps):
        rows = slice(step * 2 * per_step, (step + 1) * 2 * per_step)
        lhs = jnp.concatenate([blend[rows, r, :] for r in range(2 * chunks)], 1).astype(BF16)
        copies[step].wait()
        weights = receive[step * per_step : (step + 1) * per_step]
        product = dot_nt(lhs, weights.reshape(per_step * LANE, 2 * chunks * LANE))
        total = near_ref[rows]
        for b in range(per_step):
            total = total + jnp.where(owner == b, product[:, b * LANE : (b + 1) * LANE], 0.0)
        out_ref[rows] = total


def in_hbm(array):
    return pltpu.with_memory_space_constraint(array, pltpu.HBM)


def in_vmem(array):
    return pltpu.with_memory_space_constraint(array, pltpu.VMEM)


def tiled_rows(array):
    count, parts, width = array.shape
    cut = array.reshape(count, parts, width // LANE, LANE)
    return cut.transpose(0, 2, 1, 3).reshape(-1, LANE)


def on_device(
    density,
    radiate,
    receive,
    near_tiles,
    near_src,
    near_tile,
    send_box,
    distant_pattern_slot,
    far_type,
    trans_lo,
    interp_matrix,
    shifts,
    par_far,
    par_type,
    trans_hi,
):
    boxes, _, panels = density.shape
    devices = lax.axis_size("box") * lax.axis_size("samp")
    slots = send_box.shape[2]
    types, _, width_lo = trans_lo.shape
    width_hi = trans_hi.shape[2]
    parents = boxes // 8
    slot_total = devices * slots
    par_total = devices * parents
    type_pad = -(-types // 8) * 8
    group = 2
    share = width_hi // LANE // group
    lo_lines = slots * 2 * width_lo // LANE
    hi_lines = parents * 2 * share
    lines = lo_lines + hi_lines
    rows = density.reshape(boxes * 2, panels)
    shift_rows = tiled_rows(shifts)
    send = send_box[0].T
    outgoing = pl.pallas_call(
        functools.partial(radiate_kernel, group),
        out_shape=jax.ShapeDtypeStruct((devices, lines, LANE), BF16),
        in_specs=[HBM_SPEC] * 5,
        out_specs=VMEM_SPEC,
        scratch_shapes=[
            pltpu.VMEM(radiate.shape, BF16),
            pltpu.VMEM(rows.shape, BF16),
            pltpu.SMEM(send.shape, jnp.int32),
            pltpu.VMEM(interp_matrix.shape, BF16),
            pltpu.VMEM(shift_rows.shape, F32),
            pltpu.VMEM((2 * boxes, 2 * width_lo // LANE, LANE), F32),
            pltpu.VMEM((boxes * 8 + 8, LANE), F32),
            pltpu.VMEM((parents * 2 * width_hi // LANE, LANE), F32),
            pltpu.SemaphoreType.DMA((boxes // 4,)),
            pltpu.SemaphoreType.DMA((4,)),
        ],
        compiler_params=pltpu.CompilerParams(vmem_limit_bytes=12 * MIB),
        cost_estimate=pl.CostEstimate(flops=10**9, bytes_accessed=8 * MIB, transcendentals=0),
    )(*(in_hbm(x) for x in (rows, radiate, send, interp_matrix, shift_rows)))
    both = ("box", "samp")
    even = exchanged(rows, both, 0)
    odd = exchanged(rows, both, 1)
    outgoing, even, odd = lax.optimization_barrier((outgoing, even, odd))
    arrived = lax.all_to_all(outgoing, ("box", "samp"), split_axis=0, concat_axis=0, tiled=True)
    tile_count = near_tiles.shape[0]
    far = far_type.shape
    op_hi_rows = tiled_rows(trans_hi)
    op_lo_rows = tiled_rows(trans_lo)
    steps = 8
    near = pl.pallas_call(
        functools.partial(near_kernel, boxes * devices),
        out_shape=jax.ShapeDtypeStruct((2 * boxes, panels), F32),
        in_specs=[ANY_SPEC, HBM_SPEC, ANY_SPEC] + [HBM_SPEC] * 3,
        out_specs=VMEM_SPEC,
        scratch_shapes=[
            pltpu.VMEM(near_tiles.shape, BF16),
            pltpu.VMEM((3, 2 * boxes, panels), BF16),
            pltpu.SMEM(near_src.shape, jnp.int32),
            pltpu.SMEM(near_src.shape, jnp.int32),
            pltpu.VMEM((6 * boxes, panels), F32),
            pltpu.VMEM((3 * boxes * 8, LANE), F32),
            pltpu.VMEM((3 * boxes * 8, LANE), F32),
            pltpu.VMEM((boxes, 8, LANE), F32),
            pltpu.SMEM((tile_count + 8,), jnp.int32),
            pltpu.SemaphoreType.DMA((steps,)),
            pltpu.SemaphoreType.DMA((5,)),
        ],
        compiler_params=pltpu.CompilerParams(vmem_limit_bytes=20 * MIB),
        cost_estimate=pl.CostEstimate(flops=10**10, bytes_accessed=16 * MIB, transcendentals=0),
    )(even, in_hbm(rows), odd, in_hbm(near_src), in_hbm(near_tile), in_hbm(near_tiles))
    near, far_type = lax.optimization_barrier((near, far_type))
    d_lo, d_hi = pl.pallas_call(
        functools.partial(index_kernel, types, group),
        out_shape=(
            pltpu.HBM((boxes, slot_total, 2 * width_lo), BF16),
            pltpu.VMEM((parents * group, par_total, 2 * share * LANE), F32),
        ),
        in_specs=[HBM_SPEC] * 6,
        out_specs=(HBM_SPEC, VMEM_SPEC),
        scratch_shapes=[
            pltpu.VMEM(far, jnp.int32),
            pltpu.VMEM(far, jnp.int32),
            pltpu.VMEM(par_far.shape, jnp.int32),
            pltpu.VMEM(par_far.shape, jnp.int32),
            pltpu.VMEM(op_lo_rows.shape, BF16),
            pltpu.VMEM(op_hi_rows.shape, BF16),
            pltpu.VMEM((2 * boxes + 2 * par_far.shape[0], 2 * LANE), jnp.int32),
            pltpu.VMEM((type_pad * 2 * width_lo // LANE, LANE), F32),
            pltpu.VMEM((type_pad * 16, LANE), F32),
            pltpu.VMEM((type_pad, 2 * width_lo), BF16),
            pltpu.VMEM((type_pad, 2 * share * LANE), BF16),
            pltpu.VMEM((parents * group * par_total, type_pad), BF16),
            pltpu.VMEM((boxes, slot_total, 2 * width_lo), BF16),
            pltpu.SemaphoreType.DMA((boxes // 4,)),
            pltpu.SemaphoreType.DMA((6,)),
        ],
        compiler_params=pltpu.CompilerParams(
            vmem_limit_bytes=(20 if slot_total <= 128 else 46) * MIB
        ),
        cost_estimate=pl.CostEstimate(flops=10**9, bytes_accessed=16 * MIB, transcendentals=0),
    )(
        *(
            in_hbm(x)
            for x in (
                distant_pattern_slot,
                far_type,
                par_far,
                par_type,
                op_lo_rows,
                op_hi_rows,
            )
        )
    )
    mine, theirs = pl.pallas_call(
        functools.partial(parent_kernel, lo_lines),
        out_shape=(jax.ShapeDtypeStruct((hi_lines, LANE), F32),) * 2,
        in_specs=[VMEM_SPEC] * 2,
        out_specs=(VMEM_SPEC,) * 2,
        scratch_shapes=[pltpu.VMEM((devices * hi_lines, LANE), F32)],
        compiler_params=pltpu.CompilerParams(vmem_limit_bytes=8 * MIB),
        cost_estimate=pl.CostEstimate(flops=10**8, bytes_accessed=MIB, transcendentals=0),
    )(arrived, in_vmem(d_hi))
    theirs, d_lo = lax.optimization_barrier((theirs, d_lo))
    other = exchanged(theirs, both, 0)
    incoming = pl.pallas_call(
        leaf_kernel,
        out_shape=jax.ShapeDtypeStruct((2 * boxes, width_lo // LANE, LANE), F32),
        in_specs=[HBM_SPEC, VMEM_SPEC],
        out_specs=VMEM_SPEC,
        scratch_shapes=[
            pltpu.VMEM((boxes, slot_total, 2 * width_lo), BF16),
            pltpu.VMEM((devices * lo_lines, LANE), F32),
            pltpu.VMEM((slot_total, 2 * width_lo), F32),
            pltpu.SemaphoreType.DMA((boxes // 2,)),
        ],
        compiler_params=pltpu.CompilerParams(
            vmem_limit_bytes=(10 if slot_total <= 128 else 32) * MIB
        ),
        cost_estimate=pl.CostEstimate(flops=10**9, bytes_accessed=5 * MIB, transcendentals=0),
    )(in_hbm(d_lo), arrived)
    field = pl.pallas_call(
        last_kernel,
        out_shape=jax.ShapeDtypeStruct((2 * boxes, panels), F32),
        in_specs=[VMEM_SPEC] * 3 + [HBM_SPEC] * 3 + [VMEM_SPEC],
        out_specs=VMEM_SPEC,
        scratch_shapes=[
            pltpu.VMEM(receive.shape, BF16),
            pltpu.VMEM(shift_rows.shape, F32),
            pltpu.VMEM(interp_matrix.shape, BF16),
            pltpu.VMEM((group, hi_lines, LANE), F32),
            pltpu.VMEM((2 * boxes, width_hi), BF16),
            pltpu.VMEM((2 * boxes, 2 * width_lo // LANE, LANE), F32),
            pltpu.SemaphoreType.DMA((boxes // 4,)),
            pltpu.SemaphoreType.DMA((2,)),
        ],
        compiler_params=pltpu.CompilerParams(vmem_limit_bytes=12 * MIB),
        cost_estimate=pl.CostEstimate(flops=10**9, bytes_accessed=8 * MIB, transcendentals=0),
    )(mine, other, incoming, shift_rows, interp_matrix, in_hbm(receive), near)
    return field.reshape(boxes, 2, panels)


def solution(mesh):
    both = ("box", "samp")
    return jax.shard_map(
        on_device,
        mesh=mesh,
        in_specs=(
            P(both, None, None),
            P(both, None, None),
            P(both, None, None),
            P(both, None, None, None),
            P(both, None),
            P(both, None),
            P(both, None, None),
            P(both, None),
            P(both, None),
            P(),
            P(),
            P(),
            P("box", None),
            P("box", None),
            P(),
        ),
        out_specs=P(both, None, None),
        check_vma=False,
    )
```

```python
import functools

import jax
import jax.numpy as jnp
from jax import lax
from jax.experimental import pallas as pl
from jax.experimental.pallas import tpu as pltpu
from jax.sharding import PartitionSpec as P

F32 = jnp.float32
BF16 = jnp.bfloat16
LANE = 128
VMEM_SPEC = pl.BlockSpec(memory_space=pltpu.VMEM)
SMEM_SPEC = pl.BlockSpec(memory_space=pltpu.SMEM)
ANY_SPEC = pl.BlockSpec(memory_space=pl.ANY)
HBM_SPEC = pl.BlockSpec(memory_space=pltpu.HBM)
MIB = 1 << 20


def iota(shape, dim):
    return lax.broadcasted_iota(jnp.int32, shape, dim)


def dot_nn(lhs, rhs):
    return lax.dot_general(lhs, rhs, (((1,), (0,)), ((), ())), preferred_element_type=F32)


def dot_nt(lhs, rhs):
    return lax.dot_general(lhs, rhs, (((1,), (1,)), ((), ())), preferred_element_type=F32)


def exchanged(value, axes, first):
    count = lax.axis_size(axes)
    pairs = []
    for low in range(first, count - 1, 2):
        pairs += [(low, low + 1), (low + 1, low)]
    return lax.ppermute(value, axes, pairs)


def fetch(pairs, sems, first=0):
    copies = []
    for k, (source, target) in enumerate(pairs):
        copies.append(pltpu.make_async_copy(source, target, sems.at[first + k]))
        copies[-1].start()
    return copies


def radiate_kernel(
    group,
    dens_hbm,
    radiate_ref,
    send_hbm,
    interp_hbm,
    shift_hbm,
    out_ref,
    rad,
    dens_ref,
    send_ref,
    interp_ref,
    shift_ref,
    summed,
    table,
    parent,
    sems,
    extra,
):
    boxes = rad.shape[0]
    width = rad.shape[2] // 2
    per_step = 4
    steps = boxes // per_step
    others = fetch(
        [(dens_hbm, dens_ref), (send_hbm, send_ref), (shift_hbm, shift_ref)], extra
    )
    copies = []
    for step in range(steps):
        part = pl.ds(step * per_step, per_step)
        copies.append(pltpu.make_async_copy(radiate_ref.at[part], rad.at[part], sems.at[step]))
        copies[-1].start()
    others += fetch([(interp_hbm, interp_ref)], extra, 3)
    others[0].wait()
    dens = dens_ref[...].astype(F32)
    owner = (iota(dens.shape, 0) // 2) % per_step
    blocks = jnp.concatenate([jnp.where(owner == b, dens, 0.0) for b in range(per_step)], 1)
    for step in range(steps):
        copies[step].wait()
        rows = slice(step * 2 * per_step, (step + 1) * 2 * per_step)
        weights = rad[step * per_step : (step + 1) * per_step].reshape(per_step * LANE, 2 * width)
        summed[rows] = dot_nn(blocks[rows].astype(BF16), weights).reshape(
            2 * per_step, 2 * width // LANE, LANE
        )
    chunks = width // LANE
    re_chunks, im_chunks = [], []
    for r in range(chunks):
        first_lo = summed[pl.ds(0, boxes, stride=2), r, :]
        first_hi = summed[pl.ds(0, boxes, stride=2), chunks + r, :]
        second_lo = summed[pl.ds(1, boxes, stride=2), r, :]
        second_hi = summed[pl.ds(1, boxes, stride=2), chunks + r, :]
        re_chunks.append((first_lo - second_hi).astype(BF16))
        im_chunks.append((first_hi + second_lo).astype(BF16))
    re_part = jnp.concatenate(re_chunks, 1)
    im_part = jnp.concatenate(im_chunks, 1)
    for r in range(chunks):
        table[pl.ds(r, boxes, stride=8), :] = re_chunks[r].astype(F32)
        table[pl.ds(chunks + r, boxes, stride=8), :] = im_chunks[r].astype(F32)
    table[pl.ds(boxes * 8, 8), :] = jnp.zeros((8, LANE), F32)
    for copy in others[1:]:
        copy.wait()
    wide = dot_nn(jnp.concatenate([re_part, im_part], 0), interp_ref[...])
    hi_chunks = wide.shape[1] // LANE
    parents = boxes // 8
    share = hi_chunks // group
    for r in range(hi_chunks):
        cols = slice(r * LANE, (r + 1) * LANE)
        s_re = shift_ref[pl.ds(2 * r, 8, stride=2 * hi_chunks), :]
        s_im = shift_ref[pl.ds(2 * r + 1, 8, stride=2 * hi_chunks), :]
        for p in range(parents):
            w_re = wide[p * 8 : (p + 1) * 8, cols]
            w_im = wide[boxes + p * 8 : boxes + (p + 1) * 8, cols]
            row = ((r // share) * parents + p) * 2 * share + r % share
            parent[row : row + 1] = jnp.sum(w_re * s_re - w_im * s_im, 0, keepdims=True)
            row += share
            parent[row : row + 1] = jnp.sum(w_re * s_im + w_im * s_re, 0, keepdims=True)
    slots, devices = send_ref.shape
    hi_rows = parents * 2 * share

    def fill(d, carry):
        for k in range(slots // 2):
            pair = [
                table[pl.ds(pl.multiple_of(send_ref[2 * k + h, d] * 8, 8), 8), :] for h in range(2)
            ]
            out_ref[d, 16 * k : 16 * (k + 1)] = jnp.concatenate(pair, 0).astype(BF16)
        member = pl.multiple_of(lax.rem(d, group) * hi_rows, 8)
        out_ref[d, 8 * slots : 8 * slots + hi_rows] = parent[pl.ds(member, hi_rows)].astype(BF16)
        return carry

    lax.fori_loop(0, devices, fill, 0, unroll=4)


def tally(index, source_row, type_row, sources, types):
    source = index[pl.ds(source_row, 1), :]
    kind = index[pl.ds(type_row, 1), :]
    faces = index.shape[1]
    by_source = jnp.where(iota((sources, faces), 0) == source, 1.0, 0.0).astype(BF16)
    by_type = jnp.where(iota((types, faces), 0) == kind, 1.0, 0.0).astype(BF16)
    return dot_nt(by_source, by_type).astype(BF16)


def index_kernel(
    types,
    group,
    slot_hbm,
    type_hbm,
    par_far_hbm,
    par_type_hbm,
    op_lo_hbm,
    op_hi_hbm,
    d_lo_hbm,
    d_hi_hbm,
    slot_ref,
    type_ref,
    par_far_ref,
    par_type_ref,
    op_lo_ref,
    op_hi_ref,
    index,
    wide_lo,
    wide_hi,
    op_lo,
    op_hi,
    counts_hi,
    d_lo,
    d_hi,
    sems,
    hi_sems,
    extra,
):
    others = fetch(
        [
            (op_lo_hbm, op_lo_ref),
            (slot_hbm, slot_ref),
            (type_hbm, type_ref),
            (par_far_hbm, par_far_ref),
            (par_type_hbm, par_type_ref),
            (op_hi_hbm, op_hi_ref),
        ],
        extra,
    )
    boxes = slot_ref.shape[0]
    rows, far = par_far_ref.shape
    parents, sources, _ = d_hi.shape
    slot_total = d_lo.shape[1]
    type_pad = op_hi.shape[0]
    chunks = op_lo.shape[1] // (2 * LANE)
    lines = op_hi_ref.shape[0] // types
    share = lines // (2 * group)
    samp = lax.axis_index("samp")
    member = lax.rem(samp, group)
    first_parent = 2 * boxes + (samp - member) * (parents // group)
    place = member * (2 * share)
    base = place // 16 * 16
    index[...] = jnp.full(index.shape, -1, jnp.int32)
    tail = (type_pad - types) * 2 * chunks
    wide_lo[types * 2 * chunks : type_pad * 2 * chunks] = jnp.zeros((tail, LANE), F32)
    wide_hi[types * 16 : type_pad * 16] = jnp.zeros(((type_pad - types) * 16, LANE), F32)
    for copy in others[:5]:
        copy.wait()

    index[0:boxes, 0:far] = slot_ref[...]
    index[boxes : 2 * boxes, 0:far] = type_ref[...]
    index[2 * boxes : 2 * boxes + rows, 0:far] = par_far_ref[...]
    index[2 * boxes + rows : 2 * boxes + 2 * rows, 0:far] = par_type_ref[...]
    batch = 4
    share_parents = parents * batch // boxes

    wide_lo[0 : types * 2 * chunks] = op_lo_ref[...].astype(F32)
    for c in range(2):
        for r in range(chunks):
            col = (c * chunks + r) * LANE
            op_lo[:, col : col + LANE] = wide_lo[
                pl.ds(2 * r + c, type_pad, stride=2 * chunks), :
            ].astype(BF16)

    def lo_copy(step):
        part = pl.ds(step * batch, batch)
        return pltpu.make_async_copy(d_lo.at[part], d_lo_hbm.at[part], sems.at[step])

    def step_lists(step, carry):
        counts = []
        for k in range(batch):
            g = step * batch + k
            counts.append(tally(index, g, boxes + g, slot_total, type_pad))
        counts = jnp.concatenate(counts, 0)
        part = 2 * chunks * LANE // batch
        for k in range(batch):
            cols = slice(k * part, (k + 1) * part)
            d_lo[pl.ds(step * batch, batch), :, cols] = (
                dot_nn(counts, op_lo[:, cols]).astype(BF16).reshape(batch, slot_total, part)
            )
            if k < share_parents:
                p = step * share_parents + k
                at = pl.ds(pl.multiple_of(p * sources, sources), sources)
                row = first_parent + p
                counts_hi[at] = tally(index, row, rows + row, sources, type_pad)
        lo_copy(step).start()
        return carry

    lax.fori_loop(0, boxes // batch, step_lists, 0)
    others[5].wait()

    def widen(t, carry):
        source = pl.ds(pl.multiple_of(t * lines + base, 16), 16)
        wide_hi[pl.ds(pl.multiple_of(t * 16, 16), 16)] = op_hi_ref[source].astype(F32)
        return carry

    lax.fori_loop(0, types, widen, 0, unroll=4)
    for c in range(2):
        for k in range(share):
            col = (c * share + k) * LANE
            start = place - base + 2 * k + c
            op_hi[:, col : col + LANE] = wide_hi[pl.ds(start, type_pad, stride=16), :].astype(BF16)

    hi_copies = []
    for step in range(share):
        cols = slice(step * 2 * LANE, (step + 1) * 2 * LANE)
        d_hi[:, :, cols] = (
            dot_nn(counts_hi[...], op_hi[:, cols]).astype(BF16).reshape(parents, sources, 2 * LANE)
        )
        hi_copies.append(
            pltpu.make_async_copy(d_hi.at[:, :, cols], d_hi_hbm.at[:, :, cols], hi_sems.at[step])
        )
        hi_copies[-1].start()
    for copy in hi_copies:
        copy.wait()
    for step in range(boxes // batch):
        lo_copy(step).wait()


def parent_kernel(lo_lines, arrived_ref, d_hi_hbm, mine_ref, theirs_ref, d_hi, wide, sems):
    parents, sources, width = d_hi.shape
    share = width // (2 * LANE)
    own = parents // 2
    member = lax.rem(lax.axis_index("samp"), 2)
    copies = fetch([(d_hi_hbm.at[p], d_hi.at[p]) for p in range(parents)], sems)
    wide[...] = arrived_ref[:, lo_lines:, :].astype(F32).reshape(wide.shape)
    for copy in copies:
        copy.wait()
    for k in range(share):
        first = wide[pl.ds(k, sources, stride=2 * share), :]
        second = wide[pl.ds(share + k, sources, stride=2 * share), :]
        for out_ref, start in ((theirs_ref, (1 - member) * own), (mine_ref, member * own)):
            for q in range(own):
                o_re = d_hi[start + q, :, k * LANE : (k + 1) * LANE].astype(F32)
                o_im = d_hi[start + q, :, (share + k) * LANE : (share + k + 1) * LANE].astype(F32)
                row = q * 2 * share + k
                out_ref[row : row + 1] = jnp.sum(o_re * first - o_im * second, 0, keepdims=True)
                row += share
                out_ref[row : row + 1] = jnp.sum(o_re * second + o_im * first, 0, keepdims=True)


def near_kernel(
    box_total,
    even_ref,
    dens_hbm,
    odd_ref,
    near_src_hbm,
    near_tile_hbm,
    tiles_hbm,
    near_ref,
    tiles,
    halo,
    near_src_ref,
    near_tile_ref,
    dens3,
    left,
    right,
    acc,
    code,
    sems,
    extra,
):
    boxes, near = near_src_ref.shape
    tile_count = tiles.shape[0]
    steps = sems.shape[0]
    per_step = tile_count // steps
    samp = lax.axis_index("samp")
    position = lax.axis_index("box") * lax.axis_size("samp") + samp
    odd = lax.rem(samp, 2)
    others = fetch(
        [
            (near_src_hbm, near_src_ref),
            (near_tile_hbm, near_tile_ref),
            (even_ref, halo.at[2 - 2 * odd]),
            (dens_hbm, halo.at[1]),
            (odd_ref, halo.at[2 * odd]),
        ],
        extra,
    )

    def tile_copy(step):
        part = pl.ds(step * per_step, per_step)
        return pltpu.make_async_copy(tiles_hbm.at[part], tiles.at[part], sems.at[step])

    for step in range(steps):
        tile_copy(step).start()
    acc[...] = jnp.zeros(acc.shape, F32)
    left[...] = jnp.zeros(left.shape, F32)
    right[...] = jnp.zeros(right.shape, F32)
    for copy in others:
        copy.wait()
    for k in range(3):
        dens3[pl.ds(2 * boxes * k, 2 * boxes), :] = halo[k].astype(F32)
    first = dens3[pl.ds(0, 3 * boxes, stride=2), :]
    second = dens3[pl.ds(1, 3 * boxes, stride=2), :]
    left[pl.ds(0, 3 * boxes, stride=8), :] = first
    left[pl.ds(1, 3 * boxes, stride=8), :] = second
    right[pl.ds(0, 3 * boxes, stride=8), :] = -second
    right[pl.ds(1, 3 * boxes, stride=8), :] = first


    def locate(g, carry):
        for n in range(near):
            source = near_src_ref[g, n]
            live = source < box_total
            tile = jnp.where(live, near_tile_ref[g, n] - position * tile_count, tile_count)
            code[tile] = g * 64 + source - (position - 1) * boxes
        return carry

    lax.fori_loop(0, boxes, locate, 0)

    def multiply_pair(tile):
        both = tiles[pl.ds(tile, 2)]
        weights = jnp.concatenate(
            [both[:, 0].reshape(2 * LANE, LANE), both[:, 1].reshape(2 * LANE, LANE)], 1
        )
        owners, lefts, rights = [], [], []
        for h in range(2):
            entry = code[tile + h]
            row = pl.ds(pl.multiple_of((entry & 63) * 8, 8), 8)
            owners.append(entry >> 6)
            lefts.append(left[row])
            rights.append(right[row])
        lhs = jnp.concatenate([jnp.concatenate(lefts, 0), jnp.concatenate(rights, 0)], 1)
        product = dot_nt(lhs.astype(BF16), weights)
        for h in range(2):
            acc[owners[h]] = (
                acc[owners[h]] + product[8 * h : 8 * (h + 1), h * LANE : (h + 1) * LANE]
            )


    def step_tiles(step, carry):
        tile_copy(step).wait()
        for pair in range(per_step // 2):
            multiply_pair(step * per_step + 2 * pair)
        return carry

    lax.fori_loop(0, steps, step_tiles, 0)
    for g in range(boxes):
        row = 2 * g
        near_ref[row : row + 2] = acc[g, 0:2] + 0.5 * dens3[pl.ds(2 * boxes + row, 2), :]


def last_kernel(
    mine_ref,
    other_ref,
    d_lo_hbm,
    arrived_ref,
    shift_hbm,
    interp_hbm,
    receive_ref,
    near_ref,
    out_ref,
    receive,
    shift_ref,
    interp_ref,
    parent_ref,
    down,
    blend,
    d_lo,
    slots,
    received,
    incoming_ref,
    sems,
    lo_sems,
    extra,
):
    boxes, slot_total, width = d_lo.shape
    chunks = width // (2 * LANE)
    lo_steps = lo_sems.shape[0]
    per_boxes = boxes // lo_steps
    lo_copies = []
    for step in range(lo_steps):
        part = pl.ds(step * per_boxes, per_boxes)
        lo_copies.append(pltpu.make_async_copy(d_lo_hbm.at[part], d_lo.at[part], lo_sems.at[step]))
        lo_copies[-1].start()
    others = fetch([(shift_hbm, shift_ref), (interp_hbm, interp_ref)], extra)
    per_step = 4
    steps = boxes // per_step
    copies = []
    for step in range(steps):
        part = pl.ds(step * per_step, per_step)
        copies.append(pltpu.make_async_copy(receive_ref.at[part], receive.at[part], sems.at[step]))
        copies[-1].start()
    member = lax.rem(lax.axis_index("samp"), 2)
    parent_ref[member] = mine_ref[...]
    parent_ref[1 - member] = other_ref[...]
    own_parents = boxes // 8
    hi_chunks = down.shape[1] // LANE
    share = hi_chunks // parent_ref.shape[0]
    others[0].wait()
    for r in range(hi_chunks):
        s_re = shift_ref[pl.ds(2 * r, 8, stride=2 * hi_chunks), :]
        s_im = shift_ref[pl.ds(2 * r + 1, 8, stride=2 * hi_chunks), :]
        re_rows, im_rows = [], []
        for p in range(own_parents):
            row = p * 2 * share + r % share
            t_re = parent_ref[r // share, row : row + 1]
            t_im = parent_ref[r // share, row + share : row + share + 1]
            re_rows.append(s_re * t_re + s_im * t_im)
            im_rows.append(s_re * t_im - s_im * t_re)
        cols = slice(r * LANE, (r + 1) * LANE)
        down[:, cols] = jnp.concatenate(re_rows + im_rows, 0).astype(BF16)
    lo_lines = slots.shape[0] // arrived_ref.shape[0]
    slots[...] = arrived_ref[:, :lo_lines, :].astype(F32).reshape(slots.shape)
    for r in range(2 * chunks):
        received[:, r * LANE : (r + 1) * LANE] = slots[pl.ds(r, slot_total, stride=2 * chunks), :]

    def multiply_slots(r, g):
        first = received[:, r * LANE : (r + 1) * LANE]
        second = received[:, (chunks + r) * LANE : (chunks + r + 1) * LANE]
        o_re = d_lo[g, :, r * LANE : (r + 1) * LANE].astype(F32)
        o_im = d_lo[g, :, (chunks + r) * LANE : (chunks + r + 1) * LANE].astype(F32)
        incoming_ref[g, r : r + 1] = jnp.sum(
            o_re * first - o_im * second, 0, keepdims=True
        )
        incoming_ref[boxes + g, r : r + 1] = jnp.sum(
            o_re * second + o_im * first, 0, keepdims=True
        )

    for step in range(lo_steps):
        lo_copies[step].wait()
        for r in range(chunks):
            for k in range(per_boxes):
                multiply_slots(r, step * per_boxes + k)
    others[1].wait()
    total = jnp.concatenate([incoming_ref[:, r, :] for r in range(chunks)], 1)
    total = total + dot_nt(down[...], interp_ref[...])
    total = total.astype(BF16).astype(F32)
    for r in range(chunks):
        re_part = total[:boxes, r * LANE : (r + 1) * LANE]
        im_part = total[boxes:, r * LANE : (r + 1) * LANE]
        blend[pl.ds(0, boxes, stride=2), r, :] = re_part
        blend[pl.ds(1, boxes, stride=2), r, :] = im_part
        blend[pl.ds(0, boxes, stride=2), chunks + r, :] = -im_part
        blend[pl.ds(1, boxes, stride=2), chunks + r, :] = re_part
    owner = (iota((2 * per_step, LANE), 0) // 2) % per_step
    for step in range(steps):
        rows = slice(step * 2 * per_step, (step + 1) * 2 * per_step)
        lhs = jnp.concatenate([blend[rows, r, :] for r in range(2 * chunks)], 1).astype(BF16)
        copies[step].wait()
        weights = receive[step * per_step : (step + 1) * per_step]
        product = dot_nt(lhs, weights.reshape(per_step * LANE, 2 * chunks * LANE))
        total = near_ref[rows]
        for b in range(per_step):
            total = total + jnp.where(owner == b, product[:, b * LANE : (b + 1) * LANE], 0.0)
        out_ref[rows] = total


def in_hbm(array):
    return pltpu.with_memory_space_constraint(array, pltpu.HBM)


def in_vmem(array):
    return pltpu.with_memory_space_constraint(array, pltpu.VMEM)


def tiled_rows(array):
    count, parts, width = array.shape
    cut = array.reshape(count, parts, width // LANE, LANE)
    return cut.transpose(0, 2, 1, 3).reshape(-1, LANE)


def on_device(
    density,
    radiate,
    receive,
    near_tiles,
    near_src,
    near_tile,
    send_box,
    distant_pattern_slot,
    far_type,
    trans_lo,
    interp_matrix,
    shifts,
    par_far,
    par_type,
    trans_hi,
):
    boxes, _, panels = density.shape
    devices = lax.axis_size("box") * lax.axis_size("samp")
    slots = send_box.shape[2]
    types, _, width_lo = trans_lo.shape
    width_hi = trans_hi.shape[2]
    parents = boxes // 8
    slot_total = devices * slots
    par_total = devices * parents
    type_pad = -(-types // 8) * 8
    group = 2
    share = width_hi // LANE // group
    lo_lines = slots * 2 * width_lo // LANE
    hi_lines = parents * 2 * share
    lines = lo_lines + hi_lines
    rows = density.reshape(boxes * 2, panels)
    shift_rows = tiled_rows(shifts)
    send = send_box[0].T
    outgoing = pl.pallas_call(
        functools.partial(radiate_kernel, group),
        out_shape=jax.ShapeDtypeStruct((devices, lines, LANE), BF16),
        in_specs=[HBM_SPEC] * 5,
        out_specs=VMEM_SPEC,
        scratch_shapes=[
            pltpu.VMEM(radiate.shape, BF16),
            pltpu.VMEM(rows.shape, BF16),
            pltpu.SMEM(send.shape, jnp.int32),
            pltpu.VMEM(interp_matrix.shape, BF16),
            pltpu.VMEM(shift_rows.shape, F32),
            pltpu.VMEM((2 * boxes, 2 * width_lo // LANE, LANE), F32),
            pltpu.VMEM((boxes * 8 + 8, LANE), F32),
            pltpu.VMEM((parents * 2 * width_hi // LANE, LANE), F32),
            pltpu.SemaphoreType.DMA((boxes // 4,)),
            pltpu.SemaphoreType.DMA((4,)),
        ],
        compiler_params=pltpu.CompilerParams(vmem_limit_bytes=12 * MIB),
        cost_estimate=pl.CostEstimate(flops=10**9, bytes_accessed=8 * MIB, transcendentals=0),
    )(*(in_hbm(x) for x in (rows, radiate, send, interp_matrix, shift_rows)))
    both = ("box", "samp")
    even = exchanged(rows, both, 0)
    odd = exchanged(rows, both, 1)
    outgoing, even, odd = lax.optimization_barrier((outgoing, even, odd))
    arrived = lax.all_to_all(outgoing, ("box", "samp"), split_axis=0, concat_axis=0, tiled=True)
    tile_count = near_tiles.shape[0]
    far = far_type.shape
    op_hi_rows = tiled_rows(trans_hi)
    op_lo_rows = tiled_rows(trans_lo)
    steps = 8
    near = pl.pallas_call(
        functools.partial(near_kernel, boxes * devices),
        out_shape=jax.ShapeDtypeStruct((2 * boxes, panels), F32),
        in_specs=[ANY_SPEC, HBM_SPEC, ANY_SPEC] + [HBM_SPEC] * 3,
        out_specs=VMEM_SPEC,
        scratch_shapes=[
            pltpu.VMEM(near_tiles.shape, BF16),
            pltpu.VMEM((3, 2 * boxes, panels), BF16),
            pltpu.SMEM(near_src.shape, jnp.int32),
            pltpu.SMEM(near_src.shape, jnp.int32),
            pltpu.VMEM((6 * boxes, panels), F32),
            pltpu.VMEM((3 * boxes * 8, LANE), F32),
            pltpu.VMEM((3 * boxes * 8, LANE), F32),
            pltpu.VMEM((boxes, 8, LANE), F32),
            pltpu.SMEM((tile_count + 8,), jnp.int32),
            pltpu.SemaphoreType.DMA((steps,)),
            pltpu.SemaphoreType.DMA((5,)),
        ],
        compiler_params=pltpu.CompilerParams(vmem_limit_bytes=20 * MIB),
        cost_estimate=pl.CostEstimate(flops=10**10, bytes_accessed=16 * MIB, transcendentals=0),
    )(even, in_hbm(rows), odd, in_hbm(near_src), in_hbm(near_tile), in_hbm(near_tiles))
    near, far_type = lax.optimization_barrier((near, far_type))
    d_lo, d_hi = pl.pallas_call(
        functools.partial(index_kernel, types, group),
        out_shape=(
            pltpu.HBM((boxes, slot_total, 2 * width_lo), BF16),
            pltpu.HBM((parents * group, par_total, 2 * share * LANE), BF16),
        ),
        in_specs=[HBM_SPEC] * 6,
        out_specs=(HBM_SPEC,) * 2,
        scratch_shapes=[
            pltpu.VMEM(far, jnp.int32),
            pltpu.VMEM(far, jnp.int32),
            pltpu.VMEM(par_far.shape, jnp.int32),
            pltpu.VMEM(par_far.shape, jnp.int32),
            pltpu.VMEM(op_lo_rows.shape, BF16),
            pltpu.VMEM(op_hi_rows.shape, BF16),
            pltpu.VMEM((2 * boxes + 2 * par_far.shape[0], 2 * LANE), jnp.int32),
            pltpu.VMEM((type_pad * 2 * width_lo // LANE, LANE), F32),
            pltpu.VMEM((type_pad * 16, LANE), F32),
            pltpu.VMEM((type_pad, 2 * width_lo), BF16),
            pltpu.VMEM((type_pad, 2 * share * LANE), BF16),
            pltpu.VMEM((parents * group * par_total, type_pad), BF16),
            pltpu.VMEM((boxes, slot_total, 2 * width_lo), BF16),
            pltpu.VMEM((parents * group, par_total, 2 * share * LANE), BF16),
            pltpu.SemaphoreType.DMA((boxes // 4,)),
            pltpu.SemaphoreType.DMA((share,)),
            pltpu.SemaphoreType.DMA((6,)),
        ],
        compiler_params=pltpu.CompilerParams(
            vmem_limit_bytes=(28 if slot_total <= 128 else 52) * MIB
        ),
        cost_estimate=pl.CostEstimate(flops=10**9, bytes_accessed=16 * MIB, transcendentals=0),
    )(
        *(
            in_hbm(x)
            for x in (
                distant_pattern_slot,
                far_type,
                par_far,
                par_type,
                op_lo_rows,
                op_hi_rows,
            )
        )
    )
    mine, theirs = pl.pallas_call(
        functools.partial(parent_kernel, lo_lines),
        out_shape=(jax.ShapeDtypeStruct((hi_lines, LANE), F32),) * 2,
        in_specs=[VMEM_SPEC, HBM_SPEC],
        out_specs=(VMEM_SPEC,) * 2,
        scratch_shapes=[
            pltpu.VMEM((parents * group, par_total, 2 * share * LANE), BF16),
            pltpu.VMEM((devices * hi_lines, LANE), F32),
            pltpu.SemaphoreType.DMA((parents * group,)),
        ],
        compiler_params=pltpu.CompilerParams(vmem_limit_bytes=8 * MIB),
        cost_estimate=pl.CostEstimate(flops=10**8, bytes_accessed=MIB, transcendentals=0),
    )(arrived, in_hbm(d_hi))
    other = exchanged(theirs, both, 0)
    field = pl.pallas_call(
        last_kernel,
        out_shape=jax.ShapeDtypeStruct((2 * boxes, panels), F32),
        in_specs=[VMEM_SPEC] * 2 + [HBM_SPEC, VMEM_SPEC] + [HBM_SPEC] * 3 + [VMEM_SPEC],
        out_specs=VMEM_SPEC,
        scratch_shapes=[
            pltpu.VMEM(receive.shape, BF16),
            pltpu.VMEM(shift_rows.shape, F32),
            pltpu.VMEM(interp_matrix.shape, BF16),
            pltpu.VMEM((group, hi_lines, LANE), F32),
            pltpu.VMEM((2 * boxes, width_hi), BF16),
            pltpu.VMEM((2 * boxes, 2 * width_lo // LANE, LANE), F32),
            pltpu.VMEM((boxes, slot_total, 2 * width_lo), BF16),
            pltpu.VMEM((devices * lo_lines, LANE), F32),
            pltpu.VMEM((slot_total, 2 * width_lo), F32),
            pltpu.VMEM((2 * boxes, width_lo // LANE, LANE), F32),
            pltpu.SemaphoreType.DMA((boxes // 4,)),
            pltpu.SemaphoreType.DMA((boxes // 2,)),
            pltpu.SemaphoreType.DMA((2,)),
        ],
        compiler_params=pltpu.CompilerParams(
            vmem_limit_bytes=(22 if slot_total <= 128 else 40) * MIB
        ),
        cost_estimate=pl.CostEstimate(flops=10**9, bytes_accessed=12 * MIB, transcendentals=0),
    )(
        mine,
        other,
        in_hbm(d_lo),
        arrived,
        in_hbm(shift_rows),
        in_hbm(interp_matrix),
        in_hbm(receive),
        near,
    )
    return field.reshape(boxes, 2, panels)


def solution(mesh):
    both = ("box", "samp")
    return jax.shard_map(
        on_device,
        mesh=mesh,
        in_specs=(
            P(both, None, None),
            P(both, None, None),
            P(both, None, None),
            P(both, None, None, None),
            P(both, None),
            P(both, None),
            P(both, None, None),
            P(both, None),
            P(both, None),
            P(),
            P(),
            P(),
            P("box", None),
            P("box", None),
            P(),
        ),
        out_specs=P(both, None, None),
        check_vma=False,
    )
```

```python
import functools

import jax
import jax.numpy as jnp
from jax import lax
from jax.experimental import pallas as pl
from jax.experimental.pallas import tpu as pltpu
from jax.sharding import PartitionSpec as P

F32 = jnp.float32
BF16 = jnp.bfloat16
LANE = 128
VMEM_SPEC = pl.BlockSpec(memory_space=pltpu.VMEM)
SMEM_SPEC = pl.BlockSpec(memory_space=pltpu.SMEM)
ANY_SPEC = pl.BlockSpec(memory_space=pl.ANY)
HBM_SPEC = pl.BlockSpec(memory_space=pltpu.HBM)
MIB = 1 << 20


def iota(shape, dim):
    return lax.broadcasted_iota(jnp.int32, shape, dim)


def dot_nn(lhs, rhs):
    return lax.dot_general(lhs, rhs, (((1,), (0,)), ((), ())), preferred_element_type=F32)


def dot_nt(lhs, rhs):
    return lax.dot_general(lhs, rhs, (((1,), (1,)), ((), ())), preferred_element_type=F32)


def exchanged(value, axes, first):
    count = lax.axis_size(axes)
    pairs = []
    for low in range(first, count - 1, 2):
        pairs += [(low, low + 1), (low + 1, low)]
    return lax.ppermute(value, axes, pairs)


def fetch(pairs, sems, first=0):
    copies = []
    for k, (source, target) in enumerate(pairs):
        copies.append(pltpu.make_async_copy(source, target, sems.at[first + k]))
        copies[-1].start()
    return copies


def radiate_kernel(
    group,
    dens_hbm,
    radiate_ref,
    send_hbm,
    interp_hbm,
    shift_hbm,
    out_ref,
    rad,
    dens_ref,
    send_ref,
    interp_ref,
    shift_ref,
    summed,
    table,
    parent,
    sems,
    extra,
):
    boxes = rad.shape[0]
    width = rad.shape[2] // 2
    per_step = 4
    steps = boxes // per_step
    others = fetch(
        [(dens_hbm, dens_ref), (send_hbm, send_ref), (shift_hbm, shift_ref)], extra
    )
    copies = []
    for step in range(steps):
        part = pl.ds(step * per_step, per_step)
        copies.append(pltpu.make_async_copy(radiate_ref.at[part], rad.at[part], sems.at[step]))
        copies[-1].start()
    others += fetch([(interp_hbm, interp_ref)], extra, 3)
    others[0].wait()
    dens = dens_ref[...].astype(F32)
    owner = (iota(dens.shape, 0) // 2) % per_step
    blocks = jnp.concatenate([jnp.where(owner == b, dens, 0.0) for b in range(per_step)], 1)
    for step in range(steps):
        copies[step].wait()
        rows = slice(step * 2 * per_step, (step + 1) * 2 * per_step)
        weights = rad[step * per_step : (step + 1) * per_step].reshape(per_step * LANE, 2 * width)
        summed[rows] = dot_nn(blocks[rows].astype(BF16), weights).reshape(
            2 * per_step, 2 * width // LANE, LANE
        )
    chunks = width // LANE
    re_chunks, im_chunks = [], []
    for r in range(chunks):
        first_lo = summed[pl.ds(0, boxes, stride=2), r, :]
        first_hi = summed[pl.ds(0, boxes, stride=2), chunks + r, :]
        second_lo = summed[pl.ds(1, boxes, stride=2), r, :]
        second_hi = summed[pl.ds(1, boxes, stride=2), chunks + r, :]
        re_chunks.append((first_lo - second_hi).astype(BF16))
        im_chunks.append((first_hi + second_lo).astype(BF16))
    re_part = jnp.concatenate(re_chunks, 1)
    im_part = jnp.concatenate(im_chunks, 1)
    for r in range(chunks):
        table[pl.ds(r, boxes, stride=8), :] = re_chunks[r].astype(F32)
        table[pl.ds(chunks + r, boxes, stride=8), :] = im_chunks[r].astype(F32)
    table[pl.ds(boxes * 8, 8), :] = jnp.zeros((8, LANE), F32)
    for copy in others[1:]:
        copy.wait()
    wide = dot_nn(jnp.concatenate([re_part, im_part], 0), interp_ref[...])
    hi_chunks = wide.shape[1] // LANE
    parents = boxes // 8
    share = hi_chunks // group
    for r in range(hi_chunks):
        cols = slice(r * LANE, (r + 1) * LANE)
        s_re = shift_ref[pl.ds(2 * r, 8, stride=2 * hi_chunks), :]
        s_im = shift_ref[pl.ds(2 * r + 1, 8, stride=2 * hi_chunks), :]
        for p in range(parents):
            w_re = wide[p * 8 : (p + 1) * 8, cols]
            w_im = wide[boxes + p * 8 : boxes + (p + 1) * 8, cols]
            row = ((r // share) * parents + p) * 2 * share + r % share
            parent[row : row + 1] = jnp.sum(w_re * s_re - w_im * s_im, 0, keepdims=True)
            row += share
            parent[row : row + 1] = jnp.sum(w_re * s_im + w_im * s_re, 0, keepdims=True)
    slots, devices = send_ref.shape
    hi_rows = parents * 2 * share

    def fill(d, carry):
        for k in range(slots // 2):
            pair = [
                table[pl.ds(pl.multiple_of(send_ref[2 * k + h, d] * 8, 8), 8), :] for h in range(2)
            ]
            out_ref[d, 16 * k : 16 * (k + 1)] = jnp.concatenate(pair, 0).astype(BF16)
        member = pl.multiple_of(lax.rem(d, group) * hi_rows, 8)
        out_ref[d, 8 * slots : 8 * slots + hi_rows] = parent[pl.ds(member, hi_rows)].astype(BF16)
        return carry

    lax.fori_loop(0, devices, fill, 0, unroll=4)


def tally(index, source_row, type_row, sources, types):
    source = index[pl.ds(source_row, 1), :]
    kind = index[pl.ds(type_row, 1), :]
    faces = index.shape[1]
    by_source = jnp.where(iota((sources, faces), 0) == source, 1.0, 0.0).astype(BF16)
    by_type = jnp.where(iota((types, faces), 0) == kind, 1.0, 0.0).astype(BF16)
    return dot_nt(by_source, by_type).astype(BF16)


def index_kernel(
    types,
    group,
    slot_hbm,
    type_hbm,
    par_far_hbm,
    par_type_hbm,
    op_lo_hbm,
    op_hi_hbm,
    d_lo_hbm,
    d_ref,
    slot_ref,
    type_ref,
    par_far_ref,
    par_type_ref,
    op_lo_ref,
    op_hi_ref,
    index,
    wide_lo,
    wide_hi,
    op_lo,
    op_hi,
    counts_hi,
    d_lo,
    sems,
    extra,
):
    others = fetch(
        [
            (op_lo_hbm, op_lo_ref),
            (slot_hbm, slot_ref),
            (type_hbm, type_ref),
            (par_far_hbm, par_far_ref),
            (par_type_hbm, par_type_ref),
            (op_hi_hbm, op_hi_ref),
        ],
        extra,
    )
    boxes = slot_ref.shape[0]
    rows, far = par_far_ref.shape
    parents, sources, _ = d_ref.shape
    slot_total = d_lo.shape[1]
    type_pad = op_hi.shape[0]
    chunks = op_lo.shape[1] // (2 * LANE)
    lines = op_hi_ref.shape[0] // types
    share = lines // (2 * group)
    samp = lax.axis_index("samp")
    member = lax.rem(samp, group)
    first_parent = 2 * boxes + (samp - member) * (parents // group)
    place = member * (2 * share)
    base = place // 16 * 16
    index[...] = jnp.full(index.shape, -1, jnp.int32)
    tail = (type_pad - types) * 2 * chunks
    wide_lo[types * 2 * chunks : type_pad * 2 * chunks] = jnp.zeros((tail, LANE), F32)
    wide_hi[types * 16 : type_pad * 16] = jnp.zeros(((type_pad - types) * 16, LANE), F32)
    for copy in others[:5]:
        copy.wait()

    index[0:boxes, 0:far] = slot_ref[...]
    index[boxes : 2 * boxes, 0:far] = type_ref[...]
    index[2 * boxes : 2 * boxes + rows, 0:far] = par_far_ref[...]
    index[2 * boxes + rows : 2 * boxes + 2 * rows, 0:far] = par_type_ref[...]
    batch = 4
    share_parents = parents * batch // boxes

    wide_lo[0 : types * 2 * chunks] = op_lo_ref[...].astype(F32)
    for c in range(2):
        for r in range(chunks):
            col = (c * chunks + r) * LANE
            op_lo[:, col : col + LANE] = wide_lo[
                pl.ds(2 * r + c, type_pad, stride=2 * chunks), :
            ].astype(BF16)

    def lo_copy(step):
        part = pl.ds(step * batch, batch)
        return pltpu.make_async_copy(d_lo.at[part], d_lo_hbm.at[part], sems.at[step])

    def step_lists(step, carry):
        counts = []
        for k in range(batch):
            g = step * batch + k
            counts.append(tally(index, g, boxes + g, slot_total, type_pad))
        counts = jnp.concatenate(counts, 0)
        part = 2 * chunks * LANE // batch
        for k in range(batch):
            cols = slice(k * part, (k + 1) * part)
            d_lo[pl.ds(step * batch, batch), :, cols] = (
                dot_nn(counts, op_lo[:, cols]).astype(BF16).reshape(batch, slot_total, part)
            )
            if k < share_parents:
                p = step * share_parents + k
                at = pl.ds(pl.multiple_of(p * sources, sources), sources)
                row = first_parent + p
                counts_hi[at] = tally(index, row, rows + row, sources, type_pad)
        lo_copy(step).start()
        return carry

    lax.fori_loop(0, boxes // batch, step_lists, 0)
    others[5].wait()

    def widen(t, carry):
        source = pl.ds(pl.multiple_of(t * lines + base, 16), 16)
        wide_hi[pl.ds(pl.multiple_of(t * 16, 16), 16)] = op_hi_ref[source].astype(F32)
        return carry

    lax.fori_loop(0, types, widen, 0, unroll=4)
    for c in range(2):
        for k in range(share):
            col = (c * share + k) * LANE
            start = place - base + 2 * k + c
            op_hi[:, col : col + LANE] = wide_hi[pl.ds(start, type_pad, stride=16), :].astype(BF16)

    for first in range(0, 2 * share * LANE, 2 * LANE):
        cols = slice(first, first + 2 * LANE)
        d_ref[:, :, cols] = (
            dot_nn(counts_hi[...], op_hi[:, cols]).astype(BF16).reshape(parents, sources, 2 * LANE)
        )
    for step in range(boxes // batch):
        lo_copy(step).wait()


def parent_kernel(lo_lines, arrived_ref, d_ref, mine_ref, theirs_ref, wide):
    parents, sources, width = d_ref.shape
    share = width // (2 * LANE)
    own = parents // 2
    member = lax.rem(lax.axis_index("samp"), 2)
    wide[...] = arrived_ref[:, lo_lines:, :].astype(F32).reshape(wide.shape)
    for k in range(share):
        first = wide[pl.ds(k, sources, stride=2 * share), :]
        second = wide[pl.ds(share + k, sources, stride=2 * share), :]
        for out_ref, start in ((theirs_ref, (1 - member) * own), (mine_ref, member * own)):
            for q in range(own):
                o_re = d_ref[start + q, :, k * LANE : (k + 1) * LANE].astype(F32)
                o_im = d_ref[start + q, :, (share + k) * LANE : (share + k + 1) * LANE].astype(F32)
                row = q * 2 * share + k
                out_ref[row : row + 1] = jnp.sum(o_re * first - o_im * second, 0, keepdims=True)
                row += share
                out_ref[row : row + 1] = jnp.sum(o_re * second + o_im * first, 0, keepdims=True)


def near_kernel(
    box_total,
    even_ref,
    dens_hbm,
    odd_ref,
    near_src_hbm,
    near_tile_hbm,
    tiles_hbm,
    near_ref,
    tiles,
    halo,
    near_src_ref,
    near_tile_ref,
    dens3,
    left,
    right,
    acc,
    code,
    sems,
    extra,
):
    boxes, near = near_src_ref.shape
    tile_count = tiles.shape[0]
    steps = sems.shape[0]
    per_step = tile_count // steps
    samp = lax.axis_index("samp")
    position = lax.axis_index("box") * lax.axis_size("samp") + samp
    odd = lax.rem(samp, 2)
    others = fetch(
        [
            (near_src_hbm, near_src_ref),
            (near_tile_hbm, near_tile_ref),
            (even_ref, halo.at[2 - 2 * odd]),
            (dens_hbm, halo.at[1]),
            (odd_ref, halo.at[2 * odd]),
        ],
        extra,
    )

    def tile_copy(step):
        part = pl.ds(step * per_step, per_step)
        return pltpu.make_async_copy(tiles_hbm.at[part], tiles.at[part], sems.at[step])

    for step in range(steps):
        tile_copy(step).start()
    acc[...] = jnp.zeros(acc.shape, F32)
    left[...] = jnp.zeros(left.shape, F32)
    right[...] = jnp.zeros(right.shape, F32)
    for copy in others:
        copy.wait()
    for k in range(3):
        dens3[pl.ds(2 * boxes * k, 2 * boxes), :] = halo[k].astype(F32)
    first = dens3[pl.ds(0, 3 * boxes, stride=2), :]
    second = dens3[pl.ds(1, 3 * boxes, stride=2), :]
    left[pl.ds(0, 3 * boxes, stride=8), :] = first
    left[pl.ds(1, 3 * boxes, stride=8), :] = second
    right[pl.ds(0, 3 * boxes, stride=8), :] = -second
    right[pl.ds(1, 3 * boxes, stride=8), :] = first


    def locate(g, carry):
        for n in range(near):
            source = near_src_ref[g, n]
            live = source < box_total
            tile = jnp.where(live, near_tile_ref[g, n] - position * tile_count, tile_count)
            code[tile] = g * 64 + source - (position - 1) * boxes
        return carry

    lax.fori_loop(0, boxes, locate, 0)

    def multiply_pair(tile):
        both = tiles[pl.ds(tile, 2)]
        weights = jnp.concatenate(
            [both[:, 0].reshape(2 * LANE, LANE), both[:, 1].reshape(2 * LANE, LANE)], 1
        )
        owners, lefts, rights = [], [], []
        for h in range(2):
            entry = code[tile + h]
            row = pl.ds(pl.multiple_of((entry & 63) * 8, 8), 8)
            owners.append(entry >> 6)
            lefts.append(left[row])
            rights.append(right[row])
        lhs = jnp.concatenate([jnp.concatenate(lefts, 0), jnp.concatenate(rights, 0)], 1)
        product = dot_nt(lhs.astype(BF16), weights)
        for h in range(2):
            acc[owners[h]] = (
                acc[owners[h]] + product[8 * h : 8 * (h + 1), h * LANE : (h + 1) * LANE]
            )


    def step_tiles(step, carry):
        tile_copy(step).wait()
        for pair in range(per_step // 2):
            multiply_pair(step * per_step + 2 * pair)
        return carry

    lax.fori_loop(0, steps, step_tiles, 0)
    for g in range(boxes):
        row = 2 * g
        near_ref[row : row + 2] = acc[g, 0:2] + 0.5 * dens3[pl.ds(2 * boxes + row, 2), :]


def leaf_kernel(d_lo_hbm, arrived_ref, incoming_ref, d_lo, slots, received, sems):
    boxes, slot_total, width = d_lo.shape
    chunks = width // (2 * LANE)
    steps = sems.shape[0]
    per_boxes = boxes // steps
    copies = []
    for step in range(steps):
        part = pl.ds(step * per_boxes, per_boxes)
        copies.append(pltpu.make_async_copy(d_lo_hbm.at[part], d_lo.at[part], sems.at[step]))
        copies[-1].start()
    lo_lines = slots.shape[0] // arrived_ref.shape[0]
    slots[...] = arrived_ref[:, :lo_lines, :].astype(F32).reshape(slots.shape)
    for r in range(2 * chunks):
        received[:, r * LANE : (r + 1) * LANE] = slots[pl.ds(r, slot_total, stride=2 * chunks), :]

    def multiply_slots(r, g):
        first = received[:, r * LANE : (r + 1) * LANE]
        second = received[:, (chunks + r) * LANE : (chunks + r + 1) * LANE]
        o_re = d_lo[g, :, r * LANE : (r + 1) * LANE].astype(F32)
        o_im = d_lo[g, :, (chunks + r) * LANE : (chunks + r + 1) * LANE].astype(F32)
        incoming_ref[g, r : r + 1] = jnp.sum(
            o_re * first - o_im * second, 0, keepdims=True
        )
        incoming_ref[boxes + g, r : r + 1] = jnp.sum(
            o_re * second + o_im * first, 0, keepdims=True
        )

    for step in range(steps):
        copies[step].wait()
        for r in range(chunks):
            for k in range(per_boxes):
                multiply_slots(r, step * per_boxes + k)


def last_kernel(
    mine_ref,
    other_ref,
    incoming_ref,
    shift_hbm,
    interp_hbm,
    receive_ref,
    near_ref,
    out_ref,
    receive,
    shift_ref,
    interp_ref,
    parent_ref,
    down,
    blend,
    sems,
    extra,
):
    boxes = receive.shape[0]
    per_step = 4
    steps = boxes // per_step
    others = fetch([(shift_hbm, shift_ref), (interp_hbm, interp_ref)], extra)
    copies = []
    for step in range(steps):
        part = pl.ds(step * per_step, per_step)
        copies.append(pltpu.make_async_copy(receive_ref.at[part], receive.at[part], sems.at[step]))
        copies[-1].start()
    member = lax.rem(lax.axis_index("samp"), 2)
    parent_ref[member] = mine_ref[...]
    parent_ref[1 - member] = other_ref[...]
    own_parents = boxes // 8
    hi_chunks = down.shape[1] // LANE
    chunks = incoming_ref.shape[1]
    share = hi_chunks // parent_ref.shape[0]
    others[0].wait()
    for r in range(hi_chunks):
        s_re = shift_ref[pl.ds(2 * r, 8, stride=2 * hi_chunks), :]
        s_im = shift_ref[pl.ds(2 * r + 1, 8, stride=2 * hi_chunks), :]
        re_rows, im_rows = [], []
        for p in range(own_parents):
            row = p * 2 * share + r % share
            t_re = parent_ref[r // share, row : row + 1]
            t_im = parent_ref[r // share, row + share : row + share + 1]
            re_rows.append(s_re * t_re + s_im * t_im)
            im_rows.append(s_re * t_im - s_im * t_re)
        cols = slice(r * LANE, (r + 1) * LANE)
        down[:, cols] = jnp.concatenate(re_rows + im_rows, 0).astype(BF16)
    others[1].wait()
    total = jnp.concatenate([incoming_ref[:, r, :] for r in range(chunks)], 1)
    total = total + dot_nt(down[...], interp_ref[...])
    total = total.astype(BF16).astype(F32)
    for r in range(chunks):
        re_part = total[:boxes, r * LANE : (r + 1) * LANE]
        im_part = total[boxes:, r * LANE : (r + 1) * LANE]
        blend[pl.ds(0, boxes, stride=2), r, :] = re_part
        blend[pl.ds(1, boxes, stride=2), r, :] = im_part
        blend[pl.ds(0, boxes, stride=2), chunks + r, :] = -im_part
        blend[pl.ds(1, boxes, stride=2), chunks + r, :] = re_part
    owner = (iota((2 * per_step, LANE), 0) // 2) % per_step
    for step in range(steps):
        rows = slice(step * 2 * per_step, (step + 1) * 2 * per_step)
        lhs = jnp.concatenate([blend[rows, r, :] for r in range(2 * chunks)], 1).astype(BF16)
        copies[step].wait()
        weights = receive[step * per_step : (step + 1) * per_step]
        product = dot_nt(lhs, weights.reshape(per_step * LANE, 2 * chunks * LANE))
        total = near_ref[rows]
        for b in range(per_step):
            total = total + jnp.where(owner == b, product[:, b * LANE : (b + 1) * LANE], 0.0)
        out_ref[rows] = total


def in_hbm(array):
    return pltpu.with_memory_space_constraint(array, pltpu.HBM)


def in_vmem(array):
    return pltpu.with_memory_space_constraint(array, pltpu.VMEM)


def tiled_rows(array):
    count, parts, width = array.shape
    cut = array.reshape(count, parts, width // LANE, LANE)
    return cut.transpose(0, 2, 1, 3).reshape(-1, LANE)


def on_device(
    density,
    radiate,
    receive,
    near_tiles,
    near_src,
    near_tile,
    send_box,
    distant_pattern_slot,
    far_type,
    trans_lo,
    interp_matrix,
    shifts,
    par_far,
    par_type,
    trans_hi,
):
    boxes, _, panels = density.shape
    devices = lax.axis_size("box") * lax.axis_size("samp")
    slots = send_box.shape[2]
    types, _, width_lo = trans_lo.shape
    width_hi = trans_hi.shape[2]
    parents = boxes // 8
    slot_total = devices * slots
    par_total = devices * parents
    type_pad = -(-types // 8) * 8
    group = 2
    share = width_hi // LANE // group
    lo_lines = slots * 2 * width_lo // LANE
    hi_lines = parents * 2 * share
    lines = lo_lines + hi_lines
    rows = density.reshape(boxes * 2, panels)
    shift_rows = tiled_rows(shifts)
    send = send_box[0].T
    outgoing = pl.pallas_call(
        functools.partial(radiate_kernel, group),
        out_shape=jax.ShapeDtypeStruct((devices, lines, LANE), BF16),
        in_specs=[HBM_SPEC] * 5,
        out_specs=VMEM_SPEC,
        scratch_shapes=[
            pltpu.VMEM(radiate.shape, BF16),
            pltpu.VMEM(rows.shape, BF16),
            pltpu.SMEM(send.shape, jnp.int32),
            pltpu.VMEM(interp_matrix.shape, BF16),
            pltpu.VMEM(shift_rows.shape, F32),
            pltpu.VMEM((2 * boxes, 2 * width_lo // LANE, LANE), F32),
            pltpu.VMEM((boxes * 8 + 8, LANE), F32),
            pltpu.VMEM((parents * 2 * width_hi // LANE, LANE), F32),
            pltpu.SemaphoreType.DMA((boxes // 4,)),
            pltpu.SemaphoreType.DMA((4,)),
        ],
        compiler_params=pltpu.CompilerParams(vmem_limit_bytes=12 * MIB),
        cost_estimate=pl.CostEstimate(flops=10**9, bytes_accessed=8 * MIB, transcendentals=0),
    )(*(in_hbm(x) for x in (rows, radiate, send, interp_matrix, shift_rows)))
    both = ("box", "samp")
    even = exchanged(rows, both, 0)
    odd = exchanged(rows, both, 1)
    outgoing, even, odd = lax.optimization_barrier((outgoing, even, odd))
    arrived = lax.all_to_all(outgoing, ("box", "samp"), split_axis=0, concat_axis=0, tiled=True)
    tile_count = near_tiles.shape[0]
    far = far_type.shape
    op_hi_rows = tiled_rows(trans_hi)
    op_lo_rows = tiled_rows(trans_lo)
    steps = 8
    near = pl.pallas_call(
        functools.partial(near_kernel, boxes * devices),
        out_shape=jax.ShapeDtypeStruct((2 * boxes, panels), F32),
        in_specs=[ANY_SPEC, HBM_SPEC, ANY_SPEC] + [HBM_SPEC] * 3,
        out_specs=VMEM_SPEC,
        scratch_shapes=[
            pltpu.VMEM(near_tiles.shape, BF16),
            pltpu.VMEM((3, 2 * boxes, panels), BF16),
            pltpu.SMEM(near_src.shape, jnp.int32),
            pltpu.SMEM(near_src.shape, jnp.int32),
            pltpu.VMEM((6 * boxes, panels), F32),
            pltpu.VMEM((3 * boxes * 8, LANE), F32),
            pltpu.VMEM((3 * boxes * 8, LANE), F32),
            pltpu.VMEM((boxes, 8, LANE), F32),
            pltpu.SMEM((tile_count + 8,), jnp.int32),
            pltpu.SemaphoreType.DMA((steps,)),
            pltpu.SemaphoreType.DMA((5,)),
        ],
        compiler_params=pltpu.CompilerParams(vmem_limit_bytes=20 * MIB),
        cost_estimate=pl.CostEstimate(flops=10**10, bytes_accessed=16 * MIB, transcendentals=0),
    )(even, in_hbm(rows), odd, in_hbm(near_src), in_hbm(near_tile), in_hbm(near_tiles))
    near, far_type = lax.optimization_barrier((near, far_type))
    d_lo, d_hi = pl.pallas_call(
        functools.partial(index_kernel, types, group),
        out_shape=(
            pltpu.HBM((boxes, slot_total, 2 * width_lo), BF16),
            pltpu.VMEM((parents * group, par_total, 2 * share * LANE), BF16),
        ),
        in_specs=[HBM_SPEC] * 6,
        out_specs=(HBM_SPEC, VMEM_SPEC),
        scratch_shapes=[
            pltpu.VMEM(far, jnp.int32),
            pltpu.VMEM(far, jnp.int32),
            pltpu.VMEM(par_far.shape, jnp.int32),
            pltpu.VMEM(par_far.shape, jnp.int32),
            pltpu.VMEM(op_lo_rows.shape, BF16),
            pltpu.VMEM(op_hi_rows.shape, BF16),
            pltpu.VMEM((2 * boxes + 2 * par_far.shape[0], 2 * LANE), jnp.int32),
            pltpu.VMEM((type_pad * 2 * width_lo // LANE, LANE), F32),
            pltpu.VMEM((type_pad * 16, LANE), F32),
            pltpu.VMEM((type_pad, 2 * width_lo), BF16),
            pltpu.VMEM((type_pad, 2 * share * LANE), BF16),
            pltpu.VMEM((parents * group * par_total, type_pad), BF16),
            pltpu.VMEM((boxes, slot_total, 2 * width_lo), BF16),
            pltpu.SemaphoreType.DMA((boxes // 4,)),
            pltpu.SemaphoreType.DMA((6,)),
        ],
        compiler_params=pltpu.CompilerParams(
            vmem_limit_bytes=(20 if slot_total <= 128 else 46) * MIB
        ),
        cost_estimate=pl.CostEstimate(flops=10**9, bytes_accessed=16 * MIB, transcendentals=0),
    )(
        *(
            in_hbm(x)
            for x in (
                distant_pattern_slot,
                far_type,
                par_far,
                par_type,
                op_lo_rows,
                op_hi_rows,
            )
        )
    )
    mine, theirs = pl.pallas_call(
        functools.partial(parent_kernel, lo_lines),
        out_shape=(jax.ShapeDtypeStruct((hi_lines, LANE), F32),) * 2,
        in_specs=[VMEM_SPEC] * 2,
        out_specs=(VMEM_SPEC,) * 2,
        scratch_shapes=[pltpu.VMEM((devices * hi_lines, LANE), F32)],
        compiler_params=pltpu.CompilerParams(vmem_limit_bytes=8 * MIB),
        cost_estimate=pl.CostEstimate(flops=10**8, bytes_accessed=MIB, transcendentals=0),
    )(arrived, in_vmem(d_hi))
    theirs, d_lo = lax.optimization_barrier((theirs, d_lo))
    other = exchanged(theirs, both, 0)
    incoming = pl.pallas_call(
        leaf_kernel,
        out_shape=jax.ShapeDtypeStruct((2 * boxes, width_lo // LANE, LANE), F32),
        in_specs=[HBM_SPEC, VMEM_SPEC],
        out_specs=VMEM_SPEC,
        scratch_shapes=[
            pltpu.VMEM((boxes, slot_total, 2 * width_lo), BF16),
            pltpu.VMEM((devices * lo_lines, LANE), F32),
            pltpu.VMEM((slot_total, 2 * width_lo), F32),
            pltpu.SemaphoreType.DMA((boxes // 2,)),
        ],
        compiler_params=pltpu.CompilerParams(
            vmem_limit_bytes=(10 if slot_total <= 128 else 32) * MIB
        ),
        cost_estimate=pl.CostEstimate(flops=10**9, bytes_accessed=5 * MIB, transcendentals=0),
    )(in_hbm(d_lo), arrived)
    field = pl.pallas_call(
        last_kernel,
        out_shape=jax.ShapeDtypeStruct((2 * boxes, panels), F32),
        in_specs=[VMEM_SPEC] * 3 + [HBM_SPEC] * 3 + [VMEM_SPEC],
        out_specs=VMEM_SPEC,
        scratch_shapes=[
            pltpu.VMEM(receive.shape, BF16),
            pltpu.VMEM(shift_rows.shape, F32),
            pltpu.VMEM(interp_matrix.shape, BF16),
            pltpu.VMEM((group, hi_lines, LANE), F32),
            pltpu.VMEM((2 * boxes, width_hi), BF16),
            pltpu.VMEM((2 * boxes, 2 * width_lo // LANE, LANE), F32),
            pltpu.SemaphoreType.DMA((boxes // 4,)),
            pltpu.SemaphoreType.DMA((2,)),
        ],
        compiler_params=pltpu.CompilerParams(vmem_limit_bytes=12 * MIB),
        cost_estimate=pl.CostEstimate(flops=10**9, bytes_accessed=8 * MIB, transcendentals=0),
    )(
        mine,
        other,
        incoming,
        in_hbm(shift_rows),
        in_hbm(interp_matrix),
        in_hbm(receive),
        near,
    )
    return field.reshape(boxes, 2, panels)


def solution(mesh):
    both = ("box", "samp")
    return jax.shard_map(
        on_device,
        mesh=mesh,
        in_specs=(
            P(both, None, None),
            P(both, None, None),
            P(both, None, None),
            P(both, None, None, None),
            P(both, None),
            P(both, None),
            P(both, None, None),
            P(both, None),
            P(both, None),
            P(),
            P(),
            P(),
            P("box", None),
            P("box", None),
            P(),
        ),
        out_specs=P(both, None, None),
        check_vma=False,
    )
```

```python
import functools

import jax
import jax.numpy as jnp
from jax import lax
from jax.experimental import pallas as pl
from jax.experimental.pallas import tpu as pltpu
from jax.sharding import PartitionSpec as P

F32 = jnp.float32
BF16 = jnp.bfloat16
LANE = 128
VMEM_SPEC = pl.BlockSpec(memory_space=pltpu.VMEM)
SMEM_SPEC = pl.BlockSpec(memory_space=pltpu.SMEM)
ANY_SPEC = pl.BlockSpec(memory_space=pl.ANY)
HBM_SPEC = pl.BlockSpec(memory_space=pltpu.HBM)
MIB = 1 << 20


def iota(shape, dim):
    return lax.broadcasted_iota(jnp.int32, shape, dim)


def dot_nn(lhs, rhs):
    return lax.dot_general(lhs, rhs, (((1,), (0,)), ((), ())), preferred_element_type=F32)


def dot_nt(lhs, rhs):
    return lax.dot_general(lhs, rhs, (((1,), (1,)), ((), ())), preferred_element_type=F32)


def exchanged(value, axes, first):
    count = lax.axis_size(axes)
    pairs = []
    for low in range(first, count - 1, 2):
        pairs += [(low, low + 1), (low + 1, low)]
    return lax.ppermute(value, axes, pairs)


def fetch(pairs, sems, first=0):
    copies = []
    for k, (source, target) in enumerate(pairs):
        copies.append(pltpu.make_async_copy(source, target, sems.at[first + k]))
        copies[-1].start()
    return copies


def radiate_kernel(
    group,
    dens_hbm,
    radiate_ref,
    send_hbm,
    interp_hbm,
    shift_hbm,
    out_ref,
    rad,
    dens_ref,
    send_ref,
    interp_ref,
    shift_ref,
    summed,
    table,
    parent,
    sems,
    extra,
):
    boxes = rad.shape[0]
    width = rad.shape[2] // 2
    per_step = 4
    steps = boxes // per_step
    others = fetch(
        [(dens_hbm, dens_ref), (send_hbm, send_ref), (shift_hbm, shift_ref)], extra
    )
    copies = []
    for step in range(steps):
        part = pl.ds(step * per_step, per_step)
        copies.append(pltpu.make_async_copy(radiate_ref.at[part], rad.at[part], sems.at[step]))
    for copy in copies[:2]:
        copy.start()
    others[0].wait()
    dens = dens_ref[...].astype(F32)
    owner = (iota(dens.shape, 0) // 2) % per_step
    blocks = jnp.concatenate([jnp.where(owner == b, dens, 0.0) for b in range(per_step)], 1)
    for step in range(steps):
        copies[step].wait()
        if step + 2 < steps:
            copies[step + 2].start()
        if step == steps - 2:
            others += fetch([(interp_hbm, interp_ref)], extra, 3)
        rows = slice(step * 2 * per_step, (step + 1) * 2 * per_step)
        weights = rad[step * per_step : (step + 1) * per_step].reshape(per_step * LANE, 2 * width)
        summed[rows] = dot_nn(blocks[rows].astype(BF16), weights).reshape(
            2 * per_step, 2 * width // LANE, LANE
        )
    chunks = width // LANE
    re_chunks, im_chunks = [], []
    for r in range(chunks):
        first_lo = summed[pl.ds(0, boxes, stride=2), r, :]
        first_hi = summed[pl.ds(0, boxes, stride=2), chunks + r, :]
        second_lo = summed[pl.ds(1, boxes, stride=2), r, :]
        second_hi = summed[pl.ds(1, boxes, stride=2), chunks + r, :]
        re_chunks.append((first_lo - second_hi).astype(BF16))
        im_chunks.append((first_hi + second_lo).astype(BF16))
    re_part = jnp.concatenate(re_chunks, 1)
    im_part = jnp.concatenate(im_chunks, 1)
    for r in range(chunks):
        table[pl.ds(r, boxes, stride=8), :] = re_chunks[r].astype(F32)
        table[pl.ds(chunks + r, boxes, stride=8), :] = im_chunks[r].astype(F32)
    table[pl.ds(boxes * 8, 8), :] = jnp.zeros((8, LANE), F32)
    for copy in others[1:]:
        copy.wait()
    wide = dot_nn(jnp.concatenate([re_part, im_part], 0), interp_ref[...])
    hi_chunks = wide.shape[1] // LANE
    parents = boxes // 8
    share = hi_chunks // group
    for r in range(hi_chunks):
        cols = slice(r * LANE, (r + 1) * LANE)
        s_re = shift_ref[pl.ds(2 * r, 8, stride=2 * hi_chunks), :]
        s_im = shift_ref[pl.ds(2 * r + 1, 8, stride=2 * hi_chunks), :]
        for p in range(parents):
            w_re = wide[p * 8 : (p + 1) * 8, cols]
            w_im = wide[boxes + p * 8 : boxes + (p + 1) * 8, cols]
            row = ((r // share) * parents + p) * 2 * share + r % share
            parent[row : row + 1] = jnp.sum(w_re * s_re - w_im * s_im, 0, keepdims=True)
            row += share
            parent[row : row + 1] = jnp.sum(w_re * s_im + w_im * s_re, 0, keepdims=True)
    slots, devices = send_ref.shape
    hi_rows = parents * 2 * share

    def fill(d, carry):
        for k in range(slots // 2):
            pair = [
                table[pl.ds(pl.multiple_of(send_ref[2 * k + h, d] * 8, 8), 8), :] for h in range(2)
            ]
            out_ref[d, 16 * k : 16 * (k + 1)] = jnp.concatenate(pair, 0).astype(BF16)
        member = pl.multiple_of(lax.rem(d, group) * hi_rows, 8)
        out_ref[d, 8 * slots : 8 * slots + hi_rows] = parent[pl.ds(member, hi_rows)].astype(BF16)
        return carry

    lax.fori_loop(0, devices, fill, 0, unroll=4)


def tally(index, source_row, type_row, sources, types):
    source = index[pl.ds(source_row, 1), :]
    kind = index[pl.ds(type_row, 1), :]
    faces = index.shape[1]
    by_source = jnp.where(iota((sources, faces), 0) == source, 1.0, 0.0).astype(BF16)
    by_type = jnp.where(iota((types, faces), 0) == kind, 1.0, 0.0).astype(BF16)
    return dot_nt(by_source, by_type).astype(BF16)


def index_kernel(
    types,
    group,
    slot_hbm,
    type_hbm,
    par_far_hbm,
    par_type_hbm,
    op_lo_hbm,
    op_hi_hbm,
    d_lo_hbm,
    d_ref,
    slot_ref,
    type_ref,
    par_far_ref,
    par_type_ref,
    op_lo_ref,
    op_hi_ref,
    index,
    wide_lo,
    wide_hi,
    op_lo,
    op_hi,
    counts_hi,
    d_lo,
    sems,
    extra,
):
    others = fetch(
        [
            (op_lo_hbm, op_lo_ref),
            (slot_hbm, slot_ref),
            (type_hbm, type_ref),
            (par_far_hbm, par_far_ref),
            (par_type_hbm, par_type_ref),
            (op_hi_hbm, op_hi_ref),
        ],
        extra,
    )
    boxes = slot_ref.shape[0]
    rows, far = par_far_ref.shape
    parents, sources, _ = d_ref.shape
    slot_total = d_lo.shape[1]
    type_pad = op_hi.shape[0]
    chunks = op_lo.shape[1] // (2 * LANE)
    lines = op_hi_ref.shape[0] // types
    share = lines // (2 * group)
    samp = lax.axis_index("samp")
    member = lax.rem(samp, group)
    first_parent = 2 * boxes + (samp - member) * (parents // group)
    place = member * (2 * share)
    base = place // 16 * 16
    index[...] = jnp.full(index.shape, -1, jnp.int32)
    tail = (type_pad - types) * 2 * chunks
    wide_lo[types * 2 * chunks : type_pad * 2 * chunks] = jnp.zeros((tail, LANE), F32)
    wide_hi[types * 16 : type_pad * 16] = jnp.zeros(((type_pad - types) * 16, LANE), F32)
    for copy in others[:5]:
        copy.wait()

    index[0:boxes, 0:far] = slot_ref[...]
    index[boxes : 2 * boxes, 0:far] = type_ref[...]
    index[2 * boxes : 2 * boxes + rows, 0:far] = par_far_ref[...]
    index[2 * boxes + rows : 2 * boxes + 2 * rows, 0:far] = par_type_ref[...]
    batch = 4
    share_parents = parents * batch // boxes

    wide_lo[0 : types * 2 * chunks] = op_lo_ref[...].astype(F32)
    for c in range(2):
        for r in range(chunks):
            col = (c * chunks + r) * LANE
            op_lo[:, col : col + LANE] = wide_lo[
                pl.ds(2 * r + c, type_pad, stride=2 * chunks), :
            ].astype(BF16)

    def lo_copy(step):
        part = pl.ds(step * batch, batch)
        return pltpu.make_async_copy(d_lo.at[part], d_lo_hbm.at[part], sems.at[step])

    def step_lists(step, carry):
        counts = []
        for k in range(batch):
            g = step * batch + k
            counts.append(tally(index, g, boxes + g, slot_total, type_pad))
        counts = jnp.concatenate(counts, 0)
        part = 2 * chunks * LANE // batch
        for k in range(batch):
            cols = slice(k * part, (k + 1) * part)
            d_lo[pl.ds(step * batch, batch), :, cols] = (
                dot_nn(counts, op_lo[:, cols]).astype(BF16).reshape(batch, slot_total, part)
            )
            if k < share_parents:
                p = step * share_parents + k
                at = pl.ds(pl.multiple_of(p * sources, sources), sources)
                row = first_parent + p
                counts_hi[at] = tally(index, row, rows + row, sources, type_pad)
        lo_copy(step).start()
        return carry

    lax.fori_loop(0, boxes // batch, step_lists, 0)
    others[5].wait()

    def widen(t, carry):
        source = pl.ds(pl.multiple_of(t * lines + base, 16), 16)
        wide_hi[pl.ds(pl.multiple_of(t * 16, 16), 16)] = op_hi_ref[source].astype(F32)
        return carry

    lax.fori_loop(0, types, widen, 0, unroll=4)
    for c in range(2):
        for k in range(share):
            col = (c * share + k) * LANE
            start = place - base + 2 * k + c
            op_hi[:, col : col + LANE] = wide_hi[pl.ds(start, type_pad, stride=16), :].astype(BF16)

    for first in range(0, 2 * share * LANE, 2 * LANE):
        cols = slice(first, first + 2 * LANE)
        d_ref[:, :, cols] = (
            dot_nn(counts_hi[...], op_hi[:, cols]).astype(BF16).reshape(parents, sources, 2 * LANE)
        )
    for step in range(boxes // batch):
        lo_copy(step).wait()


def parent_kernel(lo_lines, arrived_ref, d_ref, mine_ref, theirs_ref, wide):
    parents, sources, width = d_ref.shape
    share = width // (2 * LANE)
    own = parents // 2
    member = lax.rem(lax.axis_index("samp"), 2)
    wide[...] = arrived_ref[:, lo_lines:, :].astype(F32).reshape(wide.shape)
    for k in range(share):
        first = wide[pl.ds(k, sources, stride=2 * share), :]
        second = wide[pl.ds(share + k, sources, stride=2 * share), :]
        for out_ref, start in ((theirs_ref, (1 - member) * own), (mine_ref, member * own)):
            for q in range(own):
                o_re = d_ref[start + q, :, k * LANE : (k + 1) * LANE].astype(F32)
                o_im = d_ref[start + q, :, (share + k) * LANE : (share + k + 1) * LANE].astype(F32)
                row = q * 2 * share + k
                out_ref[row : row + 1] = jnp.sum(o_re * first - o_im * second, 0, keepdims=True)
                row += share
                out_ref[row : row + 1] = jnp.sum(o_re * second + o_im * first, 0, keepdims=True)


def near_kernel(
    box_total,
    even_ref,
    dens_hbm,
    odd_ref,
    near_src_hbm,
    near_tile_hbm,
    tiles_hbm,
    near_ref,
    tiles,
    halo,
    near_src_ref,
    near_tile_ref,
    dens3,
    left,
    right,
    acc,
    code,
    sems,
    extra,
):
    boxes, near = near_src_ref.shape
    tile_count = tiles.shape[0]
    steps = sems.shape[0]
    per_step = tile_count // steps
    samp = lax.axis_index("samp")
    position = lax.axis_index("box") * lax.axis_size("samp") + samp
    odd = lax.rem(samp, 2)
    others = fetch(
        [
            (near_src_hbm, near_src_ref),
            (near_tile_hbm, near_tile_ref),
            (even_ref, halo.at[2 - 2 * odd]),
            (dens_hbm, halo.at[1]),
            (odd_ref, halo.at[2 * odd]),
        ],
        extra,
    )

    def tile_copy(step):
        part = pl.ds(step * per_step, per_step)
        return pltpu.make_async_copy(tiles_hbm.at[part], tiles.at[part], sems.at[step])

    ahead = min(3, steps)
    for step in range(ahead):
        tile_copy(step).start()
    acc[...] = jnp.zeros(acc.shape, F32)
    left[...] = jnp.zeros(left.shape, F32)
    right[...] = jnp.zeros(right.shape, F32)
    for copy in others:
        copy.wait()
    for k in range(3):
        dens3[pl.ds(2 * boxes * k, 2 * boxes), :] = halo[k].astype(F32)
    first = dens3[pl.ds(0, 3 * boxes, stride=2), :]
    second = dens3[pl.ds(1, 3 * boxes, stride=2), :]
    left[pl.ds(0, 3 * boxes, stride=8), :] = first
    left[pl.ds(1, 3 * boxes, stride=8), :] = second
    right[pl.ds(0, 3 * boxes, stride=8), :] = -second
    right[pl.ds(1, 3 * boxes, stride=8), :] = first


    def locate(g, carry):
        for n in range(near):
            source = near_src_ref[g, n]
            live = source < box_total
            tile = jnp.where(live, near_tile_ref[g, n] - position * tile_count, tile_count)
            code[tile] = g * 64 + source - (position - 1) * boxes
        return carry

    lax.fori_loop(0, boxes, locate, 0)

    def multiply_pair(tile):
        both = tiles[pl.ds(tile, 2)]
        weights = jnp.concatenate(
            [both[:, 0].reshape(2 * LANE, LANE), both[:, 1].reshape(2 * LANE, LANE)], 1
        )
        owners, lefts, rights = [], [], []
        for h in range(2):
            entry = code[tile + h]
            row = pl.ds(pl.multiple_of((entry & 63) * 8, 8), 8)
            owners.append(entry >> 6)
            lefts.append(left[row])
            rights.append(right[row])
        lhs = jnp.concatenate([jnp.concatenate(lefts, 0), jnp.concatenate(rights, 0)], 1)
        product = dot_nt(lhs.astype(BF16), weights)
        for h in range(2):
            acc[owners[h]] = (
                acc[owners[h]] + product[8 * h : 8 * (h + 1), h * LANE : (h + 1) * LANE]
            )


    def step_tiles(step, carry):
        tile_copy(step).wait()

        @pl.when(step + ahead < steps)
        def _():
            tile_copy(step + ahead).start()

        for pair in range(per_step // 2):
            multiply_pair(step * per_step + 2 * pair)
        return carry

    lax.fori_loop(0, steps, step_tiles, 0)
    for g in range(boxes):
        row = 2 * g
        near_ref[row : row + 2] = acc[g, 0:2] + 0.5 * dens3[pl.ds(2 * boxes + row, 2), :]


def leaf_kernel(d_lo_hbm, arrived_ref, incoming_ref, d_lo, slots, received, sems):
    boxes, slot_total, width = d_lo.shape
    chunks = width // (2 * LANE)
    steps = sems.shape[0]
    per_boxes = boxes // steps
    copies = []
    for step in range(steps):
        part = pl.ds(step * per_boxes, per_boxes)
        copies.append(pltpu.make_async_copy(d_lo_hbm.at[part], d_lo.at[part], sems.at[step]))
    for copy in copies[:3]:
        copy.start()
    lo_lines = slots.shape[0] // arrived_ref.shape[0]
    slots[...] = arrived_ref[:, :lo_lines, :].astype(F32).reshape(slots.shape)
    for r in range(2 * chunks):
        received[:, r * LANE : (r + 1) * LANE] = slots[pl.ds(r, slot_total, stride=2 * chunks), :]

    def multiply_slots(r, g):
        first = received[:, r * LANE : (r + 1) * LANE]
        second = received[:, (chunks + r) * LANE : (chunks + r + 1) * LANE]
        o_re = d_lo[g, :, r * LANE : (r + 1) * LANE].astype(F32)
        o_im = d_lo[g, :, (chunks + r) * LANE : (chunks + r + 1) * LANE].astype(F32)
        incoming_ref[g, r : r + 1] = jnp.sum(
            o_re * first - o_im * second, 0, keepdims=True
        )
        incoming_ref[boxes + g, r : r + 1] = jnp.sum(
            o_re * second + o_im * first, 0, keepdims=True
        )

    for step in range(steps):
        copies[step].wait()
        if step + 3 < steps:
            copies[step + 3].start()
        for r in range(chunks):
            for k in range(per_boxes):
                multiply_slots(r, step * per_boxes + k)


def last_kernel(
    mine_ref,
    other_ref,
    incoming_ref,
    shift_hbm,
    interp_hbm,
    receive_ref,
    near_ref,
    out_ref,
    receive,
    shift_ref,
    interp_ref,
    parent_ref,
    down,
    blend,
    sems,
    extra,
):
    boxes = receive.shape[0]
    per_step = 4
    steps = boxes // per_step
    others = fetch([(shift_hbm, shift_ref), (interp_hbm, interp_ref)], extra)
    copies = []
    for step in range(steps):
        part = pl.ds(step * per_step, per_step)
        copies.append(pltpu.make_async_copy(receive_ref.at[part], receive.at[part], sems.at[step]))
    member = lax.rem(lax.axis_index("samp"), 2)
    parent_ref[member] = mine_ref[...]
    parent_ref[1 - member] = other_ref[...]
    own_parents = boxes // 8
    hi_chunks = down.shape[1] // LANE
    chunks = incoming_ref.shape[1]
    share = hi_chunks // parent_ref.shape[0]
    others[0].wait()
    for r in range(hi_chunks):
        s_re = shift_ref[pl.ds(2 * r, 8, stride=2 * hi_chunks), :]
        s_im = shift_ref[pl.ds(2 * r + 1, 8, stride=2 * hi_chunks), :]
        re_rows, im_rows = [], []
        for p in range(own_parents):
            row = p * 2 * share + r % share
            t_re = parent_ref[r // share, row : row + 1]
            t_im = parent_ref[r // share, row + share : row + share + 1]
            re_rows.append(s_re * t_re + s_im * t_im)
            im_rows.append(s_re * t_im - s_im * t_re)
        cols = slice(r * LANE, (r + 1) * LANE)
        down[:, cols] = jnp.concatenate(re_rows + im_rows, 0).astype(BF16)
    others[1].wait()
    for copy in copies:
        copy.start()
    total = jnp.concatenate([incoming_ref[:, r, :] for r in range(chunks)], 1)
    total = total + dot_nt(down[...], interp_ref[...])
    total = total.astype(BF16).astype(F32)
    for r in range(chunks):
        re_part = total[:boxes, r * LANE : (r + 1) * LANE]
        im_part = total[boxes:, r * LANE : (r + 1) * LANE]
        blend[pl.ds(0, boxes, stride=2), r, :] = re_part
        blend[pl.ds(1, boxes, stride=2), r, :] = im_part
        blend[pl.ds(0, boxes, stride=2), chunks + r, :] = -im_part
        blend[pl.ds(1, boxes, stride=2), chunks + r, :] = re_part
    owner = (iota((2 * per_step, LANE), 0) // 2) % per_step
    for step in range(steps):
        rows = slice(step * 2 * per_step, (step + 1) * 2 * per_step)
        lhs = jnp.concatenate([blend[rows, r, :] for r in range(2 * chunks)], 1).astype(BF16)
        copies[step].wait()
        weights = receive[step * per_step : (step + 1) * per_step]
        product = dot_nt(lhs, weights.reshape(per_step * LANE, 2 * chunks * LANE))
        total = near_ref[rows]
        for b in range(per_step):
            total = total + jnp.where(owner == b, product[:, b * LANE : (b + 1) * LANE], 0.0)
        out_ref[rows] = total


def in_hbm(array):
    return pltpu.with_memory_space_constraint(array, pltpu.HBM)


def in_vmem(array):
    return pltpu.with_memory_space_constraint(array, pltpu.VMEM)


def tiled_rows(array):
    count, parts, width = array.shape
    cut = array.reshape(count, parts, width // LANE, LANE)
    return cut.transpose(0, 2, 1, 3).reshape(-1, LANE)


def on_device(
    density,
    radiate,
    receive,
    near_tiles,
    near_src,
    near_tile,
    send_box,
    distant_pattern_slot,
    far_type,
    trans_lo,
    interp_matrix,
    shifts,
    par_far,
    par_type,
    trans_hi,
):
    boxes, _, panels = density.shape
    devices = lax.axis_size("box") * lax.axis_size("samp")
    slots = send_box.shape[2]
    types, _, width_lo = trans_lo.shape
    width_hi = trans_hi.shape[2]
    parents = boxes // 8
    slot_total = devices * slots
    par_total = devices * parents
    type_pad = -(-types // 8) * 8
    group = 2
    share = width_hi // LANE // group
    lo_lines = slots * 2 * width_lo // LANE
    hi_lines = parents * 2 * share
    lines = lo_lines + hi_lines
    rows = density.reshape(boxes * 2, panels)
    shift_rows = tiled_rows(shifts)
    send = send_box[0].T
    outgoing = pl.pallas_call(
        functools.partial(radiate_kernel, group),
        out_shape=jax.ShapeDtypeStruct((devices, lines, LANE), BF16),
        in_specs=[HBM_SPEC] * 5,
        out_specs=VMEM_SPEC,
        scratch_shapes=[
            pltpu.VMEM(radiate.shape, BF16),
            pltpu.VMEM(rows.shape, BF16),
            pltpu.SMEM(send.shape, jnp.int32),
            pltpu.VMEM(interp_matrix.shape, BF16),
            pltpu.VMEM(shift_rows.shape, F32),
            pltpu.VMEM((2 * boxes, 2 * width_lo // LANE, LANE), F32),
            pltpu.VMEM((boxes * 8 + 8, LANE), F32),
            pltpu.VMEM((parents * 2 * width_hi // LANE, LANE), F32),
            pltpu.SemaphoreType.DMA((boxes // 4,)),
            pltpu.SemaphoreType.DMA((4,)),
        ],
        compiler_params=pltpu.CompilerParams(vmem_limit_bytes=12 * MIB),
        cost_estimate=pl.CostEstimate(flops=10**9, bytes_accessed=8 * MIB, transcendentals=0),
    )(*(in_hbm(x) for x in (rows, radiate, send, interp_matrix, shift_rows)))
    both = ("box", "samp")
    even = exchanged(rows, both, 0)
    odd = exchanged(rows, both, 1)
    outgoing, even, odd = lax.optimization_barrier((outgoing, even, odd))
    arrived = lax.all_to_all(outgoing, ("box", "samp"), split_axis=0, concat_axis=0, tiled=True)
    tile_count = near_tiles.shape[0]
    far = far_type.shape
    op_hi_rows = tiled_rows(trans_hi)
    op_lo_rows = tiled_rows(trans_lo)
    steps = 8
    near = pl.pallas_call(
        functools.partial(near_kernel, boxes * devices),
        out_shape=jax.ShapeDtypeStruct((2 * boxes, panels), F32),
        in_specs=[ANY_SPEC, HBM_SPEC, ANY_SPEC] + [HBM_SPEC] * 3,
        out_specs=VMEM_SPEC,
        scratch_shapes=[
            pltpu.VMEM(near_tiles.shape, BF16),
            pltpu.VMEM((3, 2 * boxes, panels), BF16),
            pltpu.SMEM(near_src.shape, jnp.int32),
            pltpu.SMEM(near_src.shape, jnp.int32),
            pltpu.VMEM((6 * boxes, panels), F32),
            pltpu.VMEM((3 * boxes * 8, LANE), F32),
            pltpu.VMEM((3 * boxes * 8, LANE), F32),
            pltpu.VMEM((boxes, 8, LANE), F32),
            pltpu.SMEM((tile_count + 8,), jnp.int32),
            pltpu.SemaphoreType.DMA((steps,)),
            pltpu.SemaphoreType.DMA((5,)),
        ],
        compiler_params=pltpu.CompilerParams(vmem_limit_bytes=20 * MIB),
        cost_estimate=pl.CostEstimate(flops=10**10, bytes_accessed=16 * MIB, transcendentals=0),
    )(even, in_hbm(rows), odd, in_hbm(near_src), in_hbm(near_tile), in_hbm(near_tiles))
    near, far_type = lax.optimization_barrier((near, far_type))
    d_lo, d_hi = pl.pallas_call(
        functools.partial(index_kernel, types, group),
        out_shape=(
            pltpu.HBM((boxes, slot_total, 2 * width_lo), BF16),
            pltpu.VMEM((parents * group, par_total, 2 * share * LANE), BF16),
        ),
        in_specs=[HBM_SPEC] * 6,
        out_specs=(HBM_SPEC, VMEM_SPEC),
        scratch_shapes=[
            pltpu.VMEM(far, jnp.int32),
            pltpu.VMEM(far, jnp.int32),
            pltpu.VMEM(par_far.shape, jnp.int32),
            pltpu.VMEM(par_far.shape, jnp.int32),
            pltpu.VMEM(op_lo_rows.shape, BF16),
            pltpu.VMEM(op_hi_rows.shape, BF16),
            pltpu.VMEM((2 * boxes + 2 * par_far.shape[0], 2 * LANE), jnp.int32),
            pltpu.VMEM((type_pad * 2 * width_lo // LANE, LANE), F32),
            pltpu.VMEM((type_pad * 16, LANE), F32),
            pltpu.VMEM((type_pad, 2 * width_lo), BF16),
            pltpu.VMEM((type_pad, 2 * share * LANE), BF16),
            pltpu.VMEM((parents * group * par_total, type_pad), BF16),
            pltpu.VMEM((boxes, slot_total, 2 * width_lo), BF16),
            pltpu.SemaphoreType.DMA((boxes // 4,)),
            pltpu.SemaphoreType.DMA((6,)),
        ],
        compiler_params=pltpu.CompilerParams(
            vmem_limit_bytes=(20 if slot_total <= 128 else 46) * MIB
        ),
        cost_estimate=pl.CostEstimate(flops=10**9, bytes_accessed=16 * MIB, transcendentals=0),
    )(
        *(
            in_hbm(x)
            for x in (
                distant_pattern_slot,
                far_type,
                par_far,
                par_type,
                op_lo_rows,
                op_hi_rows,
            )
        )
    )
    mine, theirs = pl.pallas_call(
        functools.partial(parent_kernel, lo_lines),
        out_shape=(jax.ShapeDtypeStruct((hi_lines, LANE), F32),) * 2,
        in_specs=[VMEM_SPEC] * 2,
        out_specs=(VMEM_SPEC,) * 2,
        scratch_shapes=[pltpu.VMEM((devices * hi_lines, LANE), F32)],
        compiler_params=pltpu.CompilerParams(vmem_limit_bytes=8 * MIB),
        cost_estimate=pl.CostEstimate(flops=10**8, bytes_accessed=MIB, transcendentals=0),
    )(arrived, in_vmem(d_hi))
    theirs, d_lo = lax.optimization_barrier((theirs, d_lo))
    other = exchanged(theirs, both, 0)
    incoming = pl.pallas_call(
        leaf_kernel,
        out_shape=jax.ShapeDtypeStruct((2 * boxes, width_lo // LANE, LANE), F32),
        in_specs=[HBM_SPEC, VMEM_SPEC],
        out_specs=VMEM_SPEC,
        scratch_shapes=[
            pltpu.VMEM((boxes, slot_total, 2 * width_lo), BF16),
            pltpu.VMEM((devices * lo_lines, LANE), F32),
            pltpu.VMEM((slot_total, 2 * width_lo), F32),
            pltpu.SemaphoreType.DMA((boxes // 2,)),
        ],
        compiler_params=pltpu.CompilerParams(
            vmem_limit_bytes=(10 if slot_total <= 128 else 32) * MIB
        ),
        cost_estimate=pl.CostEstimate(flops=10**9, bytes_accessed=5 * MIB, transcendentals=0),
    )(in_hbm(d_lo), arrived)
    field = pl.pallas_call(
        last_kernel,
        out_shape=jax.ShapeDtypeStruct((2 * boxes, panels), F32),
        in_specs=[VMEM_SPEC] * 3 + [HBM_SPEC] * 3 + [VMEM_SPEC],
        out_specs=VMEM_SPEC,
        scratch_shapes=[
            pltpu.VMEM(receive.shape, BF16),
            pltpu.VMEM(shift_rows.shape, F32),
            pltpu.VMEM(interp_matrix.shape, BF16),
            pltpu.VMEM((group, hi_lines, LANE), F32),
            pltpu.VMEM((2 * boxes, width_hi), BF16),
            pltpu.VMEM((2 * boxes, 2 * width_lo // LANE, LANE), F32),
            pltpu.SemaphoreType.DMA((boxes // 4,)),
            pltpu.SemaphoreType.DMA((2,)),
        ],
        compiler_params=pltpu.CompilerParams(vmem_limit_bytes=12 * MIB),
        cost_estimate=pl.CostEstimate(flops=10**9, bytes_accessed=8 * MIB, transcendentals=0),
    )(
        mine,
        other,
        incoming,
        in_hbm(shift_rows),
        in_hbm(interp_matrix),
        in_hbm(receive),
        near,
    )
    return field.reshape(boxes, 2, panels)


def solution(mesh):
    both = ("box", "samp")
    return jax.shard_map(
        on_device,
        mesh=mesh,
        in_specs=(
            P(both, None, None),
            P(both, None, None),
            P(both, None, None),
            P(both, None, None, None),
            P(both, None),
            P(both, None),
            P(both, None, None),
            P(both, None),
            P(both, None),
            P(),
            P(),
            P(),
            P("box", None),
            P("box", None),
            P(),
        ),
        out_specs=P(both, None, None),
        check_vma=False,
    )
```

```python
import functools

import jax
import jax.numpy as jnp
from jax import lax
from jax.experimental import pallas as pl
from jax.experimental.pallas import tpu as pltpu
from jax.sharding import PartitionSpec as P

F32 = jnp.float32
BF16 = jnp.bfloat16
LANE = 128
VMEM_SPEC = pl.BlockSpec(memory_space=pltpu.VMEM)
SMEM_SPEC = pl.BlockSpec(memory_space=pltpu.SMEM)
ANY_SPEC = pl.BlockSpec(memory_space=pl.ANY)
HBM_SPEC = pl.BlockSpec(memory_space=pltpu.HBM)
MIB = 1 << 20


def iota(shape, dim):
    return lax.broadcasted_iota(jnp.int32, shape, dim)


def dot_nn(lhs, rhs):
    return lax.dot_general(lhs, rhs, (((1,), (0,)), ((), ())), preferred_element_type=F32)


def dot_nt(lhs, rhs):
    return lax.dot_general(lhs, rhs, (((1,), (1,)), ((), ())), preferred_element_type=F32)


def exchanged(value, axes, first):
    count = lax.axis_size(axes)
    pairs = []
    for low in range(first, count - 1, 2):
        pairs += [(low, low + 1), (low + 1, low)]
    return lax.ppermute(value, axes, pairs)


def fetch(pairs, sems, first=0):
    copies = []
    for k, (source, target) in enumerate(pairs):
        copies.append(pltpu.make_async_copy(source, target, sems.at[first + k]))
        copies[-1].start()
    return copies


def pieces(source, target, count):
    rows = source.shape[0] // count
    parts = [pl.ds(k * rows, rows) for k in range(count)]
    return [(source.at[part], target.at[part]) for part in parts]


def radiate_kernel(
    group,
    dens_hbm,
    radiate_ref,
    send_hbm,
    interp_hbm,
    shift_hbm,
    out_ref,
    rad,
    dens_ref,
    send_ref,
    interp_ref,
    shift_ref,
    summed,
    table,
    parent,
    sems,
    extra,
):
    boxes = rad.shape[0]
    width = rad.shape[2] // 2
    per_step = 4
    steps = boxes // per_step
    others = fetch(
        [(dens_hbm, dens_ref), (send_hbm, send_ref), (shift_hbm, shift_ref)], extra
    )
    copies = fetch(pieces(radiate_ref, rad, boxes), sems)
    others += fetch(pieces(interp_hbm, interp_ref, 4), extra, 3)
    others[0].wait()
    dens = dens_ref[...].astype(F32)
    owner = (iota(dens.shape, 0) // 2) % per_step
    blocks = jnp.concatenate([jnp.where(owner == b, dens, 0.0) for b in range(per_step)], 1)
    for step in range(steps):
        for copy in copies[step * per_step : (step + 1) * per_step]:
            copy.wait()
        rows = slice(step * 2 * per_step, (step + 1) * 2 * per_step)
        weights = rad[step * per_step : (step + 1) * per_step].reshape(per_step * LANE, 2 * width)
        summed[rows] = dot_nn(blocks[rows].astype(BF16), weights).reshape(
            2 * per_step, 2 * width // LANE, LANE
        )
    chunks = width // LANE
    re_chunks, im_chunks = [], []
    for r in range(chunks):
        first_lo = summed[pl.ds(0, boxes, stride=2), r, :]
        first_hi = summed[pl.ds(0, boxes, stride=2), chunks + r, :]
        second_lo = summed[pl.ds(1, boxes, stride=2), r, :]
        second_hi = summed[pl.ds(1, boxes, stride=2), chunks + r, :]
        re_chunks.append((first_lo - second_hi).astype(BF16))
        im_chunks.append((first_hi + second_lo).astype(BF16))
    re_part = jnp.concatenate(re_chunks, 1)
    im_part = jnp.concatenate(im_chunks, 1)
    for r in range(chunks):
        table[pl.ds(r, boxes, stride=8), :] = re_chunks[r].astype(F32)
        table[pl.ds(chunks + r, boxes, stride=8), :] = im_chunks[r].astype(F32)
    table[pl.ds(boxes * 8, 8), :] = jnp.zeros((8, LANE), F32)
    for copy in others[1:]:
        copy.wait()
    wide = dot_nn(jnp.concatenate([re_part, im_part], 0), interp_ref[...])
    hi_chunks = wide.shape[1] // LANE
    parents = boxes // 8
    share = hi_chunks // group
    for r in range(hi_chunks):
        cols = slice(r * LANE, (r + 1) * LANE)
        s_re = shift_ref[pl.ds(2 * r, 8, stride=2 * hi_chunks), :]
        s_im = shift_ref[pl.ds(2 * r + 1, 8, stride=2 * hi_chunks), :]
        for p in range(parents):
            w_re = wide[p * 8 : (p + 1) * 8, cols]
            w_im = wide[boxes + p * 8 : boxes + (p + 1) * 8, cols]
            row = ((r // share) * parents + p) * 2 * share + r % share
            parent[row : row + 1] = jnp.sum(w_re * s_re - w_im * s_im, 0, keepdims=True)
            row += share
            parent[row : row + 1] = jnp.sum(w_re * s_im + w_im * s_re, 0, keepdims=True)
    slots, devices = send_ref.shape
    hi_rows = parents * 2 * share

    def fill(d, carry):
        for k in range(slots // 2):
            pair = [
                table[pl.ds(pl.multiple_of(send_ref[2 * k + h, d] * 8, 8), 8), :] for h in range(2)
            ]
            out_ref[d, 16 * k : 16 * (k + 1)] = jnp.concatenate(pair, 0).astype(BF16)
        member = pl.multiple_of(lax.rem(d, group) * hi_rows, 8)
        out_ref[d, 8 * slots : 8 * slots + hi_rows] = parent[pl.ds(member, hi_rows)].astype(BF16)
        return carry

    lax.fori_loop(0, devices, fill, 0, unroll=4)


def tally(index, source_row, type_row, sources, types):
    source = index[pl.ds(source_row, 1), :]
    kind = index[pl.ds(type_row, 1), :]
    faces = index.shape[1]
    by_source = jnp.where(iota((sources, faces), 0) == source, 1.0, 0.0).astype(BF16)
    by_type = jnp.where(iota((types, faces), 0) == kind, 1.0, 0.0).astype(BF16)
    return dot_nt(by_source, by_type).astype(BF16)


def index_kernel(
    types,
    group,
    slot_hbm,
    type_hbm,
    par_far_hbm,
    par_type_hbm,
    op_lo_hbm,
    op_hi_hbm,
    d_lo_hbm,
    d_ref,
    slot_ref,
    type_ref,
    par_far_ref,
    par_type_ref,
    op_lo_ref,
    op_hi_ref,
    index,
    wide_lo,
    wide_hi,
    op_lo,
    op_hi,
    counts_hi,
    d_lo,
    sems,
    extra,
):
    others = fetch(
        [
            (op_lo_hbm, op_lo_ref),
            (slot_hbm, slot_ref),
            (type_hbm, type_ref),
            (par_far_hbm, par_far_ref),
            (par_type_hbm, par_type_ref),
            *pieces(op_hi_hbm, op_hi_ref, 4),
        ],
        extra,
    )
    boxes = slot_ref.shape[0]
    rows, far = par_far_ref.shape
    parents, sources, _ = d_ref.shape
    slot_total = d_lo.shape[1]
    type_pad = op_hi.shape[0]
    chunks = op_lo.shape[1] // (2 * LANE)
    lines = op_hi_ref.shape[0] // types
    share = lines // (2 * group)
    samp = lax.axis_index("samp")
    member = lax.rem(samp, group)
    first_parent = 2 * boxes + (samp - member) * (parents // group)
    place = member * (2 * share)
    base = place // 16 * 16
    index[...] = jnp.full(index.shape, -1, jnp.int32)
    tail = (type_pad - types) * 2 * chunks
    wide_lo[types * 2 * chunks : type_pad * 2 * chunks] = jnp.zeros((tail, LANE), F32)
    wide_hi[types * 16 : type_pad * 16] = jnp.zeros(((type_pad - types) * 16, LANE), F32)
    for copy in others[:5]:
        copy.wait()

    index[0:boxes, 0:far] = slot_ref[...]
    index[boxes : 2 * boxes, 0:far] = type_ref[...]
    index[2 * boxes : 2 * boxes + rows, 0:far] = par_far_ref[...]
    index[2 * boxes + rows : 2 * boxes + 2 * rows, 0:far] = par_type_ref[...]
    batch = 4
    share_parents = parents * batch // boxes

    wide_lo[0 : types * 2 * chunks] = op_lo_ref[...].astype(F32)
    for c in range(2):
        for r in range(chunks):
            col = (c * chunks + r) * LANE
            op_lo[:, col : col + LANE] = wide_lo[
                pl.ds(2 * r + c, type_pad, stride=2 * chunks), :
            ].astype(BF16)

    def lo_copy(step):
        part = pl.ds(step * batch, batch)
        return pltpu.make_async_copy(d_lo.at[part], d_lo_hbm.at[part], sems.at[step])

    def step_lists(step, carry):
        counts = []
        for k in range(batch):
            g = step * batch + k
            counts.append(tally(index, g, boxes + g, slot_total, type_pad))
        counts = jnp.concatenate(counts, 0)
        part = 2 * chunks * LANE // batch
        for k in range(batch):
            cols = slice(k * part, (k + 1) * part)
            d_lo[pl.ds(step * batch, batch), :, cols] = (
                dot_nn(counts, op_lo[:, cols]).astype(BF16).reshape(batch, slot_total, part)
            )
            if k < share_parents:
                p = step * share_parents + k
                at = pl.ds(pl.multiple_of(p * sources, sources), sources)
                row = first_parent + p
                counts_hi[at] = tally(index, row, rows + row, sources, type_pad)
        lo_copy(step).start()
        return carry

    lax.fori_loop(0, boxes // batch, step_lists, 0)
    for copy in others[5:]:
        copy.wait()

    def widen(t, carry):
        source = pl.ds(pl.multiple_of(t * lines + base, 16), 16)
        wide_hi[pl.ds(pl.multiple_of(t * 16, 16), 16)] = op_hi_ref[source].astype(F32)
        return carry

    lax.fori_loop(0, types, widen, 0, unroll=4)
    for c in range(2):
        for k in range(share):
            col = (c * share + k) * LANE
            start = place - base + 2 * k + c
            op_hi[:, col : col + LANE] = wide_hi[pl.ds(start, type_pad, stride=16), :].astype(BF16)

    for first in range(0, 2 * share * LANE, 2 * LANE):
        cols = slice(first, first + 2 * LANE)
        d_ref[:, :, cols] = (
            dot_nn(counts_hi[...], op_hi[:, cols]).astype(BF16).reshape(parents, sources, 2 * LANE)
        )
    for step in range(boxes // batch):
        lo_copy(step).wait()


def parent_kernel(lo_lines, arrived_ref, d_ref, mine_ref, theirs_ref, wide):
    parents, sources, width = d_ref.shape
    share = width // (2 * LANE)
    own = parents // 2
    member = lax.rem(lax.axis_index("samp"), 2)
    wide[...] = arrived_ref[:, lo_lines:, :].astype(F32).reshape(wide.shape)
    for k in range(share):
        first = wide[pl.ds(k, sources, stride=2 * share), :]
        second = wide[pl.ds(share + k, sources, stride=2 * share), :]
        for out_ref, start in ((theirs_ref, (1 - member) * own), (mine_ref, member * own)):
            for q in range(own):
                o_re = d_ref[start + q, :, k * LANE : (k + 1) * LANE].astype(F32)
                o_im = d_ref[start + q, :, (share + k) * LANE : (share + k + 1) * LANE].astype(F32)
                row = q * 2 * share + k
                out_ref[row : row + 1] = jnp.sum(o_re * first - o_im * second, 0, keepdims=True)
                row += share
                out_ref[row : row + 1] = jnp.sum(o_re * second + o_im * first, 0, keepdims=True)


def near_kernel(
    box_total,
    even_ref,
    dens_hbm,
    odd_ref,
    near_src_hbm,
    near_tile_hbm,
    tiles_hbm,
    near_ref,
    tiles,
    halo,
    near_src_ref,
    near_tile_ref,
    dens3,
    left,
    right,
    acc,
    code,
    sems,
    extra,
):
    boxes, near = near_src_ref.shape
    tile_count = tiles.shape[0]
    split = 4
    steps = sems.shape[0] // split
    per_step = tile_count // steps
    samp = lax.axis_index("samp")
    position = lax.axis_index("box") * lax.axis_size("samp") + samp
    odd = lax.rem(samp, 2)
    others = fetch(
        [
            (near_src_hbm, near_src_ref),
            (near_tile_hbm, near_tile_ref),
            (even_ref, halo.at[2 - 2 * odd]),
            (dens_hbm, halo.at[1]),
            (odd_ref, halo.at[2 * odd]),
        ],
        extra,
    )

    def tile_copy(piece):
        part = pl.ds(piece * (per_step // split), per_step // split)
        return pltpu.make_async_copy(tiles_hbm.at[part], tiles.at[part], sems.at[piece])

    for piece in range(steps * split):
        tile_copy(piece).start()
    acc[...] = jnp.zeros(acc.shape, F32)
    left[...] = jnp.zeros(left.shape, F32)
    right[...] = jnp.zeros(right.shape, F32)
    for copy in others:
        copy.wait()
    for k in range(3):
        dens3[pl.ds(2 * boxes * k, 2 * boxes), :] = halo[k].astype(F32)
    first = dens3[pl.ds(0, 3 * boxes, stride=2), :]
    second = dens3[pl.ds(1, 3 * boxes, stride=2), :]
    left[pl.ds(0, 3 * boxes, stride=8), :] = first
    left[pl.ds(1, 3 * boxes, stride=8), :] = second
    right[pl.ds(0, 3 * boxes, stride=8), :] = -second
    right[pl.ds(1, 3 * boxes, stride=8), :] = first


    def locate(g, carry):
        for n in range(near):
            source = near_src_ref[g, n]
            live = source < box_total
            tile = jnp.where(live, near_tile_ref[g, n] - position * tile_count, tile_count)
            code[tile] = g * 64 + source - (position - 1) * boxes
        return carry

    lax.fori_loop(0, boxes, locate, 0)

    def multiply_pair(tile):
        both = tiles[pl.ds(tile, 2)]
        weights = jnp.concatenate(
            [both[:, 0].reshape(2 * LANE, LANE), both[:, 1].reshape(2 * LANE, LANE)], 1
        )
        owners, lefts, rights = [], [], []
        for h in range(2):
            entry = code[tile + h]
            row = pl.ds(pl.multiple_of((entry & 63) * 8, 8), 8)
            owners.append(entry >> 6)
            lefts.append(left[row])
            rights.append(right[row])
        lhs = jnp.concatenate([jnp.concatenate(lefts, 0), jnp.concatenate(rights, 0)], 1)
        product = dot_nt(lhs.astype(BF16), weights)
        for h in range(2):
            acc[owners[h]] = (
                acc[owners[h]] + product[8 * h : 8 * (h + 1), h * LANE : (h + 1) * LANE]
            )


    def step_tiles(step, carry):
        for piece in range(split):
            tile_copy(step * split + piece).wait()
        for pair in range(per_step // 2):
            multiply_pair(step * per_step + 2 * pair)
        return carry

    lax.fori_loop(0, steps, step_tiles, 0)
    for g in range(boxes):
        row = 2 * g
        near_ref[row : row + 2] = acc[g, 0:2] + 0.5 * dens3[pl.ds(2 * boxes + row, 2), :]


def leaf_kernel(d_lo_hbm, arrived_ref, incoming_ref, d_lo, slots, received, sems):
    boxes, slot_total, width = d_lo.shape
    chunks = width // (2 * LANE)
    steps = sems.shape[0]
    per_boxes = boxes // steps
    copies = []
    for step in range(steps):
        part = pl.ds(step * per_boxes, per_boxes)
        copies.append(pltpu.make_async_copy(d_lo_hbm.at[part], d_lo.at[part], sems.at[step]))
        copies[-1].start()
    lo_lines = slots.shape[0] // arrived_ref.shape[0]
    slots[...] = arrived_ref[:, :lo_lines, :].astype(F32).reshape(slots.shape)
    for r in range(2 * chunks):
        received[:, r * LANE : (r + 1) * LANE] = slots[pl.ds(r, slot_total, stride=2 * chunks), :]

    def multiply_slots(r, g):
        first = received[:, r * LANE : (r + 1) * LANE]
        second = received[:, (chunks + r) * LANE : (chunks + r + 1) * LANE]
        o_re = d_lo[g, :, r * LANE : (r + 1) * LANE].astype(F32)
        o_im = d_lo[g, :, (chunks + r) * LANE : (chunks + r + 1) * LANE].astype(F32)
        incoming_ref[g, r : r + 1] = jnp.sum(
            o_re * first - o_im * second, 0, keepdims=True
        )
        incoming_ref[boxes + g, r : r + 1] = jnp.sum(
            o_re * second + o_im * first, 0, keepdims=True
        )

    for step in range(steps):
        copies[step].wait()
        for r in range(chunks):
            for k in range(per_boxes):
                multiply_slots(r, step * per_boxes + k)


def last_kernel(
    mine_ref,
    other_ref,
    incoming_ref,
    shift_hbm,
    interp_hbm,
    receive_ref,
    near_ref,
    out_ref,
    receive,
    shift_ref,
    interp_ref,
    parent_ref,
    down,
    blend,
    sems,
    extra,
):
    boxes = receive.shape[0]
    per_step = 4
    steps = boxes // per_step
    others = fetch([(shift_hbm, shift_ref), *pieces(interp_hbm, interp_ref, 4)], extra)
    copies = fetch(pieces(receive_ref, receive, boxes), sems)
    member = lax.rem(lax.axis_index("samp"), 2)
    parent_ref[member] = mine_ref[...]
    parent_ref[1 - member] = other_ref[...]
    own_parents = boxes // 8
    hi_chunks = down.shape[1] // LANE
    chunks = incoming_ref.shape[1]
    share = hi_chunks // parent_ref.shape[0]
    others[0].wait()
    for r in range(hi_chunks):
        s_re = shift_ref[pl.ds(2 * r, 8, stride=2 * hi_chunks), :]
        s_im = shift_ref[pl.ds(2 * r + 1, 8, stride=2 * hi_chunks), :]
        re_rows, im_rows = [], []
        for p in range(own_parents):
            row = p * 2 * share + r % share
            t_re = parent_ref[r // share, row : row + 1]
            t_im = parent_ref[r // share, row + share : row + share + 1]
            re_rows.append(s_re * t_re + s_im * t_im)
            im_rows.append(s_re * t_im - s_im * t_re)
        cols = slice(r * LANE, (r + 1) * LANE)
        down[:, cols] = jnp.concatenate(re_rows + im_rows, 0).astype(BF16)
    for copy in others[1:]:
        copy.wait()
    total = jnp.concatenate([incoming_ref[:, r, :] for r in range(chunks)], 1)
    total = total + dot_nt(down[...], interp_ref[...])
    total = total.astype(BF16).astype(F32)
    for r in range(chunks):
        re_part = total[:boxes, r * LANE : (r + 1) * LANE]
        im_part = total[boxes:, r * LANE : (r + 1) * LANE]
        blend[pl.ds(0, boxes, stride=2), r, :] = re_part
        blend[pl.ds(1, boxes, stride=2), r, :] = im_part
        blend[pl.ds(0, boxes, stride=2), chunks + r, :] = -im_part
        blend[pl.ds(1, boxes, stride=2), chunks + r, :] = re_part
    owner = (iota((2 * per_step, LANE), 0) // 2) % per_step
    for step in range(steps):
        rows = slice(step * 2 * per_step, (step + 1) * 2 * per_step)
        lhs = jnp.concatenate([blend[rows, r, :] for r in range(2 * chunks)], 1).astype(BF16)
        for copy in copies[step * per_step : (step + 1) * per_step]:
            copy.wait()
        weights = receive[step * per_step : (step + 1) * per_step]
        product = dot_nt(lhs, weights.reshape(per_step * LANE, 2 * chunks * LANE))
        total = near_ref[rows]
        for b in range(per_step):
            total = total + jnp.where(owner == b, product[:, b * LANE : (b + 1) * LANE], 0.0)
        out_ref[rows] = total


def in_hbm(array):
    return pltpu.with_memory_space_constraint(array, pltpu.HBM)


def in_vmem(array):
    return pltpu.with_memory_space_constraint(array, pltpu.VMEM)


def tiled_rows(array):
    count, parts, width = array.shape
    cut = array.reshape(count, parts, width // LANE, LANE)
    return cut.transpose(0, 2, 1, 3).reshape(-1, LANE)


def on_device(
    density,
    radiate,
    receive,
    near_tiles,
    near_src,
    near_tile,
    send_box,
    distant_pattern_slot,
    far_type,
    trans_lo,
    interp_matrix,
    shifts,
    par_far,
    par_type,
    trans_hi,
):
    boxes, _, panels = density.shape
    devices = lax.axis_size("box") * lax.axis_size("samp")
    slots = send_box.shape[2]
    types, _, width_lo = trans_lo.shape
    width_hi = trans_hi.shape[2]
    parents = boxes // 8
    slot_total = devices * slots
    par_total = devices * parents
    type_pad = -(-types // 8) * 8
    group = 2
    share = width_hi // LANE // group
    lo_lines = slots * 2 * width_lo // LANE
    hi_lines = parents * 2 * share
    lines = lo_lines + hi_lines
    rows = density.reshape(boxes * 2, panels)
    shift_rows = tiled_rows(shifts)
    send = send_box[0].T
    outgoing = pl.pallas_call(
        functools.partial(radiate_kernel, group),
        out_shape=jax.ShapeDtypeStruct((devices, lines, LANE), BF16),
        in_specs=[HBM_SPEC] * 5,
        out_specs=VMEM_SPEC,
        scratch_shapes=[
            pltpu.VMEM(radiate.shape, BF16),
            pltpu.VMEM(rows.shape, BF16),
            pltpu.SMEM(send.shape, jnp.int32),
            pltpu.VMEM(interp_matrix.shape, BF16),
            pltpu.VMEM(shift_rows.shape, F32),
            pltpu.VMEM((2 * boxes, 2 * width_lo // LANE, LANE), F32),
            pltpu.VMEM((boxes * 8 + 8, LANE), F32),
            pltpu.VMEM((parents * 2 * width_hi // LANE, LANE), F32),
            pltpu.SemaphoreType.DMA((boxes,)),
            pltpu.SemaphoreType.DMA((7,)),
        ],
        compiler_params=pltpu.CompilerParams(vmem_limit_bytes=12 * MIB),
        cost_estimate=pl.CostEstimate(flops=10**9, bytes_accessed=8 * MIB, transcendentals=0),
    )(*(in_hbm(x) for x in (rows, radiate, send, interp_matrix, shift_rows)))
    both = ("box", "samp")
    even = exchanged(rows, both, 0)
    odd = exchanged(rows, both, 1)
    outgoing, even, odd = lax.optimization_barrier((outgoing, even, odd))
    arrived = lax.all_to_all(outgoing, ("box", "samp"), split_axis=0, concat_axis=0, tiled=True)
    tile_count = near_tiles.shape[0]
    far = far_type.shape
    op_hi_rows = tiled_rows(trans_hi)
    op_lo_rows = tiled_rows(trans_lo)
    steps = 8
    near = pl.pallas_call(
        functools.partial(near_kernel, boxes * devices),
        out_shape=jax.ShapeDtypeStruct((2 * boxes, panels), F32),
        in_specs=[ANY_SPEC, HBM_SPEC, ANY_SPEC] + [HBM_SPEC] * 3,
        out_specs=VMEM_SPEC,
        scratch_shapes=[
            pltpu.VMEM(near_tiles.shape, BF16),
            pltpu.VMEM((3, 2 * boxes, panels), BF16),
            pltpu.SMEM(near_src.shape, jnp.int32),
            pltpu.SMEM(near_src.shape, jnp.int32),
            pltpu.VMEM((6 * boxes, panels), F32),
            pltpu.VMEM((3 * boxes * 8, LANE), F32),
            pltpu.VMEM((3 * boxes * 8, LANE), F32),
            pltpu.VMEM((boxes, 8, LANE), F32),
            pltpu.SMEM((tile_count + 8,), jnp.int32),
            pltpu.SemaphoreType.DMA((steps * 4,)),
            pltpu.SemaphoreType.DMA((5,)),
        ],
        compiler_params=pltpu.CompilerParams(vmem_limit_bytes=20 * MIB),
        cost_estimate=pl.CostEstimate(flops=10**10, bytes_accessed=16 * MIB, transcendentals=0),
    )(even, in_hbm(rows), odd, in_hbm(near_src), in_hbm(near_tile), in_hbm(near_tiles))
    near, far_type = lax.optimization_barrier((near, far_type))
    d_lo, d_hi = pl.pallas_call(
        functools.partial(index_kernel, types, group),
        out_shape=(
            pltpu.HBM((boxes, slot_total, 2 * width_lo), BF16),
            pltpu.VMEM((parents * group, par_total, 2 * share * LANE), BF16),
        ),
        in_specs=[HBM_SPEC] * 6,
        out_specs=(HBM_SPEC, VMEM_SPEC),
        scratch_shapes=[
            pltpu.VMEM(far, jnp.int32),
            pltpu.VMEM(far, jnp.int32),
            pltpu.VMEM(par_far.shape, jnp.int32),
            pltpu.VMEM(par_far.shape, jnp.int32),
            pltpu.VMEM(op_lo_rows.shape, BF16),
            pltpu.VMEM(op_hi_rows.shape, BF16),
            pltpu.VMEM((2 * boxes + 2 * par_far.shape[0], 2 * LANE), jnp.int32),
            pltpu.VMEM((type_pad * 2 * width_lo // LANE, LANE), F32),
            pltpu.VMEM((type_pad * 16, LANE), F32),
            pltpu.VMEM((type_pad, 2 * width_lo), BF16),
            pltpu.VMEM((type_pad, 2 * share * LANE), BF16),
            pltpu.VMEM((parents * group * par_total, type_pad), BF16),
            pltpu.VMEM((boxes, slot_total, 2 * width_lo), BF16),
            pltpu.SemaphoreType.DMA((boxes // 4,)),
            pltpu.SemaphoreType.DMA((9,)),
        ],
        compiler_params=pltpu.CompilerParams(
            vmem_limit_bytes=(20 if slot_total <= 128 else 46) * MIB
        ),
        cost_estimate=pl.CostEstimate(flops=10**9, bytes_accessed=16 * MIB, transcendentals=0),
    )(
        *(
            in_hbm(x)
            for x in (
                distant_pattern_slot,
                far_type,
                par_far,
                par_type,
                op_lo_rows,
                op_hi_rows,
            )
        )
    )
    mine, theirs = pl.pallas_call(
        functools.partial(parent_kernel, lo_lines),
        out_shape=(jax.ShapeDtypeStruct((hi_lines, LANE), F32),) * 2,
        in_specs=[VMEM_SPEC] * 2,
        out_specs=(VMEM_SPEC,) * 2,
        scratch_shapes=[pltpu.VMEM((devices * hi_lines, LANE), F32)],
        compiler_params=pltpu.CompilerParams(vmem_limit_bytes=8 * MIB),
        cost_estimate=pl.CostEstimate(flops=10**8, bytes_accessed=MIB, transcendentals=0),
    )(arrived, in_vmem(d_hi))
    theirs, d_lo = lax.optimization_barrier((theirs, d_lo))
    other = exchanged(theirs, both, 0)
    incoming = pl.pallas_call(
        leaf_kernel,
        out_shape=jax.ShapeDtypeStruct((2 * boxes, width_lo // LANE, LANE), F32),
        in_specs=[HBM_SPEC, VMEM_SPEC],
        out_specs=VMEM_SPEC,
        scratch_shapes=[
            pltpu.VMEM((boxes, slot_total, 2 * width_lo), BF16),
            pltpu.VMEM((devices * lo_lines, LANE), F32),
            pltpu.VMEM((slot_total, 2 * width_lo), F32),
            pltpu.SemaphoreType.DMA((boxes,)),
        ],
        compiler_params=pltpu.CompilerParams(
            vmem_limit_bytes=(10 if slot_total <= 128 else 32) * MIB
        ),
        cost_estimate=pl.CostEstimate(flops=10**9, bytes_accessed=5 * MIB, transcendentals=0),
    )(in_hbm(d_lo), arrived)
    field = pl.pallas_call(
        last_kernel,
        out_shape=jax.ShapeDtypeStruct((2 * boxes, panels), F32),
        in_specs=[VMEM_SPEC] * 3 + [HBM_SPEC] * 3 + [VMEM_SPEC],
        out_specs=VMEM_SPEC,
        scratch_shapes=[
            pltpu.VMEM(receive.shape, BF16),
            pltpu.VMEM(shift_rows.shape, F32),
            pltpu.VMEM(interp_matrix.shape, BF16),
            pltpu.VMEM((group, hi_lines, LANE), F32),
            pltpu.VMEM((2 * boxes, width_hi), BF16),
            pltpu.VMEM((2 * boxes, 2 * width_lo // LANE, LANE), F32),
            pltpu.SemaphoreType.DMA((boxes,)),
            pltpu.SemaphoreType.DMA((5,)),
        ],
        compiler_params=pltpu.CompilerParams(vmem_limit_bytes=12 * MIB),
        cost_estimate=pl.CostEstimate(flops=10**9, bytes_accessed=8 * MIB, transcendentals=0),
    )(
        mine,
        other,
        incoming,
        in_hbm(shift_rows),
        in_hbm(interp_matrix),
        in_hbm(receive),
        near,
    )
    return field.reshape(boxes, 2, panels)


def solution(mesh):
    both = ("box", "samp")
    return jax.shard_map(
        on_device,
        mesh=mesh,
        in_specs=(
            P(both, None, None),
            P(both, None, None),
            P(both, None, None),
            P(both, None, None, None),
            P(both, None),
            P(both, None),
            P(both, None, None),
            P(both, None),
            P(both, None),
            P(),
            P(),
            P(),
            P("box", None),
            P("box", None),
            P(),
        ),
        out_specs=P(both, None, None),
        check_vma=False,
    )
```

```python
import functools

import jax
import jax.numpy as jnp
from jax import lax
from jax.experimental import pallas as pl
from jax.experimental.pallas import tpu as pltpu
from jax.sharding import PartitionSpec as P

F32 = jnp.float32
BF16 = jnp.bfloat16
LANE = 128
VMEM_SPEC = pl.BlockSpec(memory_space=pltpu.VMEM)
SMEM_SPEC = pl.BlockSpec(memory_space=pltpu.SMEM)
ANY_SPEC = pl.BlockSpec(memory_space=pl.ANY)
HBM_SPEC = pl.BlockSpec(memory_space=pltpu.HBM)
MIB = 1 << 20


def iota(shape, dim):
    return lax.broadcasted_iota(jnp.int32, shape, dim)


def dot_nn(lhs, rhs):
    return lax.dot_general(lhs, rhs, (((1,), (0,)), ((), ())), preferred_element_type=F32)


def dot_nt(lhs, rhs):
    return lax.dot_general(lhs, rhs, (((1,), (1,)), ((), ())), preferred_element_type=F32)


def exchanged(value, axes, first):
    count = lax.axis_size(axes)
    pairs = []
    for low in range(first, count - 1, 2):
        pairs += [(low, low + 1), (low + 1, low)]
    return lax.ppermute(value, axes, pairs)


def fetch(pairs, sems, first=0):
    copies = []
    for k, (source, target) in enumerate(pairs):
        copies.append(pltpu.make_async_copy(source, target, sems.at[first + k]))
        copies[-1].start()
    return copies


def radiate_kernel(
    group,
    dens_hbm,
    radiate_ref,
    send_hbm,
    interp_hbm,
    shift_hbm,
    out_ref,
    rad,
    dens_ref,
    send_ref,
    interp_ref,
    shift_ref,
    summed,
    table,
    parent,
    sems,
    extra,
):
    boxes = rad.shape[0]
    width = rad.shape[2] // 2
    per_step = 4
    steps = boxes // per_step
    others = fetch(
        [(dens_hbm, dens_ref), (send_hbm, send_ref), (shift_hbm, shift_ref)], extra
    )
    copies = []
    for step in range(steps):
        part = pl.ds(step * per_step, per_step)
        copies.append(pltpu.make_async_copy(radiate_ref.at[part], rad.at[part], sems.at[step]))
        copies[-1].start()
    others += fetch([(interp_hbm, interp_ref)], extra, 3)
    others[0].wait()
    dens = dens_ref[...].astype(F32)
    owner = (iota(dens.shape, 0) // 2) % per_step
    blocks = jnp.concatenate([jnp.where(owner == b, dens, 0.0) for b in range(per_step)], 1)
    for step in range(steps):
        copies[step].wait()
        rows = slice(step * 2 * per_step, (step + 1) * 2 * per_step)
        weights = rad[step * per_step : (step + 1) * per_step].reshape(per_step * LANE, 2 * width)
        summed[rows] = dot_nn(blocks[rows].astype(BF16), weights).reshape(
            2 * per_step, 2 * width // LANE, LANE
        )
    chunks = width // LANE
    re_chunks, im_chunks = [], []
    for r in range(chunks):
        first_lo = summed[pl.ds(0, boxes, stride=2), r, :]
        first_hi = summed[pl.ds(0, boxes, stride=2), chunks + r, :]
        second_lo = summed[pl.ds(1, boxes, stride=2), r, :]
        second_hi = summed[pl.ds(1, boxes, stride=2), chunks + r, :]
        re_chunks.append((first_lo - second_hi).astype(BF16))
        im_chunks.append((first_hi + second_lo).astype(BF16))
    re_part = jnp.concatenate(re_chunks, 1)
    im_part = jnp.concatenate(im_chunks, 1)
    for r in range(chunks):
        table[pl.ds(r, boxes, stride=8), :] = re_chunks[r].astype(F32)
        table[pl.ds(chunks + r, boxes, stride=8), :] = im_chunks[r].astype(F32)
    table[pl.ds(boxes * 8, 8), :] = jnp.zeros((8, LANE), F32)
    for copy in others[1:]:
        copy.wait()
    wide = dot_nn(jnp.concatenate([re_part, im_part], 0), interp_ref[...])
    hi_chunks = wide.shape[1] // LANE
    parents = boxes // 8
    share = hi_chunks // group
    for r in range(hi_chunks):
        cols = slice(r * LANE, (r + 1) * LANE)
        s_re = shift_ref[pl.ds(2 * r, 8, stride=2 * hi_chunks), :]
        s_im = shift_ref[pl.ds(2 * r + 1, 8, stride=2 * hi_chunks), :]
        for p in range(parents):
            w_re = wide[p * 8 : (p + 1) * 8, cols]
            w_im = wide[boxes + p * 8 : boxes + (p + 1) * 8, cols]
            row = ((r // share) * parents + p) * 2 * share + r % share
            parent[row : row + 1] = jnp.sum(w_re * s_re - w_im * s_im, 0, keepdims=True)
            row += share
            parent[row : row + 1] = jnp.sum(w_re * s_im + w_im * s_re, 0, keepdims=True)
    slots, devices = send_ref.shape
    hi_rows = parents * 2 * share

    def fill(d, carry):
        for k in range(slots // 2):
            pair = [
                table[pl.ds(pl.multiple_of(send_ref[2 * k + h, d] * 8, 8), 8), :] for h in range(2)
            ]
            out_ref[d, 16 * k : 16 * (k + 1)] = jnp.concatenate(pair, 0).astype(BF16)
        member = pl.multiple_of(lax.rem(d, group) * hi_rows, 8)
        out_ref[d, 8 * slots : 8 * slots + hi_rows] = parent[pl.ds(member, hi_rows)].astype(BF16)
        return carry

    lax.fori_loop(0, devices, fill, 0, unroll=4)


def tally(index, source_row, type_row, sources, types):
    source = index[pl.ds(source_row, 1), :]
    kind = index[pl.ds(type_row, 1), :]
    faces = index.shape[1]
    by_source = jnp.where(iota((sources, faces), 0) == source, 1.0, 0.0).astype(BF16)
    by_type = jnp.where(iota((types, faces), 0) == kind, 1.0, 0.0).astype(BF16)
    return dot_nt(by_source, by_type).astype(BF16)


def index_kernel(
    types,
    group,
    slot_hbm,
    type_hbm,
    par_far_hbm,
    par_type_hbm,
    op_lo_hbm,
    op_hi_hbm,
    d_lo_hbm,
    d_ref,
    slot_ref,
    type_ref,
    par_far_ref,
    par_type_ref,
    op_lo_ref,
    op_hi_ref,
    index,
    wide_lo,
    wide_hi,
    op_lo,
    op_hi,
    counts_hi,
    d_lo,
    sems,
    extra,
):
    others = fetch(
        [
            (op_lo_hbm, op_lo_ref),
            (slot_hbm, slot_ref),
            (type_hbm, type_ref),
            (par_far_hbm, par_far_ref),
            (par_type_hbm, par_type_ref),
            (op_hi_hbm, op_hi_ref),
        ],
        extra,
    )
    boxes = slot_ref.shape[0]
    rows, far = par_far_ref.shape
    parents, sources, _ = d_ref.shape
    slot_total = d_lo.shape[1]
    type_pad = op_hi.shape[0]
    chunks = op_lo.shape[1] // (2 * LANE)
    lines = op_hi_ref.shape[0] // types
    share = lines // (2 * group)
    samp = lax.axis_index("samp")
    member = lax.rem(samp, group)
    first_parent = 2 * boxes + (samp - member) * (parents // group)
    place = member * (2 * share)
    base = place // 16 * 16
    index[...] = jnp.full(index.shape, -1, jnp.int32)
    tail = (type_pad - types) * 2 * chunks
    wide_lo[types * 2 * chunks : type_pad * 2 * chunks] = jnp.zeros((tail, LANE), F32)
    wide_hi[types * 16 : type_pad * 16] = jnp.zeros(((type_pad - types) * 16, LANE), F32)
    for copy in others[:5]:
        copy.wait()

    index[0:boxes, 0:far] = slot_ref[...]
    index[boxes : 2 * boxes, 0:far] = type_ref[...]
    index[2 * boxes : 2 * boxes + rows, 0:far] = par_far_ref[...]
    index[2 * boxes + rows : 2 * boxes + 2 * rows, 0:far] = par_type_ref[...]
    batch = 4
    share_parents = parents * batch // boxes

    wide_lo[0 : types * 2 * chunks] = op_lo_ref[...].astype(F32)
    for c in range(2):
        for r in range(chunks):
            col = (c * chunks + r) * LANE
            op_lo[:, col : col + LANE] = wide_lo[
                pl.ds(2 * r + c, type_pad, stride=2 * chunks), :
            ].astype(BF16)

    def lo_copy(step):
        part = pl.ds(step * batch, batch)
        return pltpu.make_async_copy(d_lo.at[part], d_lo_hbm.at[part], sems.at[step])

    def step_lists(step, carry):
        counts = []
        for k in range(batch):
            g = step * batch + k
            counts.append(tally(index, g, boxes + g, slot_total, type_pad))
        counts = jnp.concatenate(counts, 0)
        part = 2 * chunks * LANE // batch
        for k in range(batch):
            cols = slice(k * part, (k + 1) * part)
            d_lo[pl.ds(step * batch, batch), :, cols] = (
                dot_nn(counts, op_lo[:, cols]).astype(BF16).reshape(batch, slot_total, part)
            )
            if k < share_parents:
                p = step * share_parents + k
                at = pl.ds(pl.multiple_of(p * sources, sources), sources)
                row = first_parent + p
                counts_hi[at] = tally(index, row, rows + row, sources, type_pad)
        lo_copy(step).start()
        return carry

    lax.fori_loop(0, boxes // batch, step_lists, 0)
    others[5].wait()

    def widen(t, carry):
        source = pl.ds(pl.multiple_of(t * lines + base, 16), 16)
        wide_hi[pl.ds(pl.multiple_of(t * 16, 16), 16)] = op_hi_ref[source].astype(F32)
        return carry

    lax.fori_loop(0, types, widen, 0, unroll=4)
    for c in range(2):
        for k in range(share):
            col = (c * share + k) * LANE
            start = place - base + 2 * k + c
            op_hi[:, col : col + LANE] = wide_hi[pl.ds(start, type_pad, stride=16), :].astype(BF16)

    for first in range(0, 2 * share * LANE, 2 * LANE):
        cols = slice(first, first + 2 * LANE)
        d_ref[:, :, cols] = (
            dot_nn(counts_hi[...], op_hi[:, cols]).astype(BF16).reshape(parents, sources, 2 * LANE)
        )
    for step in range(boxes // batch):
        lo_copy(step).wait()


def parent_kernel(lo_lines, arrived_ref, d_ref, mine_ref, theirs_ref, wide):
    parents, sources, width = d_ref.shape
    share = width // (2 * LANE)
    own = parents // 2
    member = lax.rem(lax.axis_index("samp"), 2)
    wide[...] = arrived_ref[:, lo_lines:, :].astype(F32).reshape(wide.shape)
    for k in range(share):
        first = wide[pl.ds(k, sources, stride=2 * share), :]
        second = wide[pl.ds(share + k, sources, stride=2 * share), :]
        for out_ref, start in ((theirs_ref, (1 - member) * own), (mine_ref, member * own)):
            for q in range(own):
                o_re = d_ref[start + q, :, k * LANE : (k + 1) * LANE].astype(F32)
                o_im = d_ref[start + q, :, (share + k) * LANE : (share + k + 1) * LANE].astype(F32)
                row = q * 2 * share + k
                out_ref[row : row + 1] = jnp.sum(o_re * first - o_im * second, 0, keepdims=True)
                row += share
                out_ref[row : row + 1] = jnp.sum(o_re * second + o_im * first, 0, keepdims=True)


def near_kernel(
    box_total,
    even_ref,
    dens_hbm,
    odd_ref,
    near_src_hbm,
    near_tile_hbm,
    tiles_hbm,
    near_ref,
    tiles,
    halo,
    near_src_ref,
    near_tile_ref,
    dens3,
    left,
    right,
    acc,
    code,
    sems,
    extra,
):
    boxes, near = near_src_ref.shape
    tile_count = tiles.shape[0]
    steps = sems.shape[0]
    per_step = tile_count // steps
    samp = lax.axis_index("samp")
    position = lax.axis_index("box") * lax.axis_size("samp") + samp
    odd = lax.rem(samp, 2)
    others = fetch(
        [
            (near_src_hbm, near_src_ref),
            (near_tile_hbm, near_tile_ref),
            (even_ref, halo.at[2 - 2 * odd]),
            (dens_hbm, halo.at[1]),
            (odd_ref, halo.at[2 * odd]),
        ],
        extra,
    )

    def tile_copy(step):
        part = pl.ds(step * per_step, per_step)
        return pltpu.make_async_copy(tiles_hbm.at[part], tiles.at[part], sems.at[step])

    for step in range(steps):
        tile_copy(step).start()
    acc[...] = jnp.zeros(acc.shape, F32)
    left[...] = jnp.zeros(left.shape, F32)
    right[...] = jnp.zeros(right.shape, F32)
    for copy in others:
        copy.wait()
    for k in range(3):
        dens3[pl.ds(2 * boxes * k, 2 * boxes), :] = halo[k].astype(F32)
    first = dens3[pl.ds(0, 3 * boxes, stride=2), :]
    second = dens3[pl.ds(1, 3 * boxes, stride=2), :]
    left[pl.ds(0, 3 * boxes, stride=8), :] = first
    left[pl.ds(1, 3 * boxes, stride=8), :] = second
    right[pl.ds(0, 3 * boxes, stride=8), :] = -second
    right[pl.ds(1, 3 * boxes, stride=8), :] = first


    def locate(g, carry):
        for n in range(near):
            source = near_src_ref[g, n]
            live = source < box_total
            tile = jnp.where(live, near_tile_ref[g, n] - position * tile_count, tile_count)
            code[tile] = g * 64 + source - (position - 1) * boxes
        return carry

    lax.fori_loop(0, boxes, locate, 0)

    def multiply_pair(tile):
        both = tiles[pl.ds(tile, 2)]
        weights = jnp.concatenate(
            [both[:, 0].reshape(2 * LANE, LANE), both[:, 1].reshape(2 * LANE, LANE)], 1
        )
        owners, lefts, rights = [], [], []
        for h in range(2):
            entry = code[tile + h]
            row = pl.ds(pl.multiple_of((entry & 63) * 8, 8), 8)
            owners.append(entry >> 6)
            lefts.append(left[row])
            rights.append(right[row])
        lhs = jnp.concatenate([jnp.concatenate(lefts, 0), jnp.concatenate(rights, 0)], 1)
        product = dot_nt(lhs.astype(BF16), weights)
        for h in range(2):
            acc[owners[h]] = (
                acc[owners[h]] + product[8 * h : 8 * (h + 1), h * LANE : (h + 1) * LANE]
            )


    def step_tiles(step, carry):
        tile_copy(step).wait()
        for pair in range(per_step // 2):
            multiply_pair(step * per_step + 2 * pair)
        return carry

    lax.fori_loop(0, steps, step_tiles, 0)
    for g in range(boxes):
        row = 2 * g
        near_ref[row : row + 2] = acc[g, 0:2] + 0.5 * dens3[pl.ds(2 * boxes + row, 2), :]


def leaf_kernel(d_lo_hbm, arrived_ref, incoming_ref, d_lo, slots, received, sems):
    boxes, slot_total, width = d_lo.shape
    chunks = width // (2 * LANE)
    steps = sems.shape[0]
    per_boxes = boxes // steps
    copies = []
    for step in range(steps):
        part = pl.ds(step * per_boxes, per_boxes)
        copies.append(pltpu.make_async_copy(d_lo_hbm.at[part], d_lo.at[part], sems.at[step]))
        copies[-1].start()
    lo_lines = slots.shape[0] // arrived_ref.shape[0]
    slots[...] = arrived_ref[:, :lo_lines, :].astype(F32).reshape(slots.shape)
    for r in range(2 * chunks):
        received[:, r * LANE : (r + 1) * LANE] = slots[pl.ds(r, slot_total, stride=2 * chunks), :]

    def multiply_slots(r, g):
        first = received[:, r * LANE : (r + 1) * LANE]
        second = received[:, (chunks + r) * LANE : (chunks + r + 1) * LANE]
        o_re = d_lo[g, :, r * LANE : (r + 1) * LANE].astype(F32)
        o_im = d_lo[g, :, (chunks + r) * LANE : (chunks + r + 1) * LANE].astype(F32)
        incoming_ref[g, r : r + 1] = jnp.sum(
            o_re * first - o_im * second, 0, keepdims=True
        )
        incoming_ref[boxes + g, r : r + 1] = jnp.sum(
            o_re * second + o_im * first, 0, keepdims=True
        )

    for step in range(steps):
        copies[step].wait()
        for r in range(chunks):
            for k in range(per_boxes):
                multiply_slots(r, step * per_boxes + k)


def last_kernel(
    mine_ref,
    other_ref,
    incoming_ref,
    shift_hbm,
    interp_hbm,
    receive_ref,
    near_ref,
    out_ref,
    receive,
    shift_ref,
    interp_ref,
    parent_ref,
    down,
    blend,
    sems,
    extra,
):
    boxes = receive.shape[0]
    per_step = 4
    steps = boxes // per_step
    others = fetch([(shift_hbm, shift_ref), (interp_hbm, interp_ref)], extra)
    copies = []
    for step in range(steps):
        part = pl.ds(step * per_step, per_step)
        copies.append(pltpu.make_async_copy(receive_ref.at[part], receive.at[part], sems.at[step]))
        copies[-1].start()
    member = lax.rem(lax.axis_index("samp"), 2)
    parent_ref[member] = mine_ref[...]
    parent_ref[1 - member] = other_ref[...]
    own_parents = boxes // 8
    hi_chunks = down.shape[1] // LANE
    chunks = incoming_ref.shape[1]
    share = hi_chunks // parent_ref.shape[0]
    others[0].wait()
    for r in range(hi_chunks):
        s_re = shift_ref[pl.ds(2 * r, 8, stride=2 * hi_chunks), :]
        s_im = shift_ref[pl.ds(2 * r + 1, 8, stride=2 * hi_chunks), :]
        re_rows, im_rows = [], []
        for p in range(own_parents):
            row = p * 2 * share + r % share
            t_re = parent_ref[r // share, row : row + 1]
            t_im = parent_ref[r // share, row + share : row + share + 1]
            re_rows.append(s_re * t_re + s_im * t_im)
            im_rows.append(s_re * t_im - s_im * t_re)
        cols = slice(r * LANE, (r + 1) * LANE)
        down[:, cols] = jnp.concatenate(re_rows + im_rows, 0).astype(BF16)
    others[1].wait()
    total = jnp.concatenate([incoming_ref[:, r, :] for r in range(chunks)], 1)
    total = total + dot_nt(down[...], interp_ref[...])
    total = total.astype(BF16).astype(F32)
    for r in range(chunks):
        re_part = total[:boxes, r * LANE : (r + 1) * LANE]
        im_part = total[boxes:, r * LANE : (r + 1) * LANE]
        blend[pl.ds(0, boxes, stride=2), r, :] = re_part
        blend[pl.ds(1, boxes, stride=2), r, :] = im_part
        blend[pl.ds(0, boxes, stride=2), chunks + r, :] = -im_part
        blend[pl.ds(1, boxes, stride=2), chunks + r, :] = re_part
    owner = (iota((2 * per_step, LANE), 0) // 2) % per_step
    for step in range(steps):
        rows = slice(step * 2 * per_step, (step + 1) * 2 * per_step)
        lhs = jnp.concatenate([blend[rows, r, :] for r in range(2 * chunks)], 1).astype(BF16)
        copies[step].wait()
        weights = receive[step * per_step : (step + 1) * per_step]
        product = dot_nt(lhs, weights.reshape(per_step * LANE, 2 * chunks * LANE))
        total = near_ref[rows]
        for b in range(per_step):
            total = total + jnp.where(owner == b, product[:, b * LANE : (b + 1) * LANE], 0.0)
        out_ref[rows] = total


def in_hbm(array):
    return pltpu.with_memory_space_constraint(array, pltpu.HBM)


def in_vmem(array):
    return pltpu.with_memory_space_constraint(array, pltpu.VMEM)


def tiled_rows(array):
    count, parts, width = array.shape
    cut = array.reshape(count, parts, width // LANE, LANE)
    return cut.transpose(0, 2, 1, 3).reshape(-1, LANE)


def on_device(
    density,
    radiate,
    receive,
    near_tiles,
    near_src,
    near_tile,
    send_box,
    distant_pattern_slot,
    far_type,
    trans_lo,
    interp_matrix,
    shifts,
    par_far,
    par_type,
    trans_hi,
):
    boxes, _, panels = density.shape
    devices = lax.axis_size("box") * lax.axis_size("samp")
    slots = send_box.shape[2]
    types, _, width_lo = trans_lo.shape
    width_hi = trans_hi.shape[2]
    parents = boxes // 8
    slot_total = devices * slots
    par_total = devices * parents
    type_pad = -(-types // 8) * 8
    group = 2
    share = width_hi // LANE // group
    lo_lines = slots * 2 * width_lo // LANE
    hi_lines = parents * 2 * share
    lines = lo_lines + hi_lines
    rows = density.reshape(boxes * 2, panels)
    shift_rows = tiled_rows(shifts)
    send = send_box[0].T
    outgoing = pl.pallas_call(
        functools.partial(radiate_kernel, group),
        out_shape=jax.ShapeDtypeStruct((devices, lines, LANE), BF16),
        in_specs=[HBM_SPEC] * 5,
        out_specs=VMEM_SPEC,
        scratch_shapes=[
            pltpu.VMEM(radiate.shape, BF16),
            pltpu.VMEM(rows.shape, BF16),
            pltpu.SMEM(send.shape, jnp.int32),
            pltpu.VMEM(interp_matrix.shape, BF16),
            pltpu.VMEM(shift_rows.shape, F32),
            pltpu.VMEM((2 * boxes, 2 * width_lo // LANE, LANE), F32),
            pltpu.VMEM((boxes * 8 + 8, LANE), F32),
            pltpu.VMEM((parents * 2 * width_hi // LANE, LANE), F32),
            pltpu.SemaphoreType.DMA((boxes // 4,)),
            pltpu.SemaphoreType.DMA((4,)),
        ],
        compiler_params=pltpu.CompilerParams(vmem_limit_bytes=12 * MIB),
        cost_estimate=pl.CostEstimate(flops=10**9, bytes_accessed=8 * MIB, transcendentals=0),
    )(*(in_hbm(x) for x in (rows, radiate, send, interp_matrix, shift_rows)))
    both = ("box", "samp")
    even = exchanged(rows, both, 0)
    odd = exchanged(rows, both, 1)
    outgoing, even, odd = lax.optimization_barrier((outgoing, even, odd))
    arrived = lax.all_to_all(outgoing, ("box", "samp"), split_axis=0, concat_axis=0, tiled=True)
    tile_count = near_tiles.shape[0]
    far = far_type.shape
    op_hi_rows = tiled_rows(trans_hi)
    op_lo_rows = tiled_rows(trans_lo)
    steps = 8
    near = pl.pallas_call(
        functools.partial(near_kernel, boxes * devices),
        out_shape=jax.ShapeDtypeStruct((2 * boxes, panels), F32),
        in_specs=[ANY_SPEC, HBM_SPEC, ANY_SPEC] + [HBM_SPEC] * 3,
        out_specs=VMEM_SPEC,
        scratch_shapes=[
            pltpu.VMEM(near_tiles.shape, BF16),
            pltpu.VMEM((3, 2 * boxes, panels), BF16),
            pltpu.SMEM(near_src.shape, jnp.int32),
            pltpu.SMEM(near_src.shape, jnp.int32),
            pltpu.VMEM((6 * boxes, panels), F32),
            pltpu.VMEM((3 * boxes * 8, LANE), F32),
            pltpu.VMEM((3 * boxes * 8, LANE), F32),
            pltpu.VMEM((boxes, 8, LANE), F32),
            pltpu.SMEM((tile_count + 8,), jnp.int32),
            pltpu.SemaphoreType.DMA((steps,)),
            pltpu.SemaphoreType.DMA((5,)),
        ],
        compiler_params=pltpu.CompilerParams(vmem_limit_bytes=20 * MIB),
        cost_estimate=pl.CostEstimate(flops=10**10, bytes_accessed=16 * MIB, transcendentals=0),
    )(even, in_hbm(rows), odd, in_hbm(near_src), in_hbm(near_tile), in_hbm(near_tiles))
    near, far_type = lax.optimization_barrier((near, far_type))
    d_lo, d_hi = pl.pallas_call(
        functools.partial(index_kernel, types, group),
        out_shape=(
            pltpu.HBM((boxes, slot_total, 2 * width_lo), BF16),
            pltpu.VMEM((parents * group, par_total, 2 * share * LANE), BF16),
        ),
        in_specs=[HBM_SPEC] * 6,
        out_specs=(HBM_SPEC, VMEM_SPEC),
        scratch_shapes=[
            pltpu.VMEM(far, jnp.int32),
            pltpu.VMEM(far, jnp.int32),
            pltpu.VMEM(par_far.shape, jnp.int32),
            pltpu.VMEM(par_far.shape, jnp.int32),
            pltpu.VMEM(op_lo_rows.shape, BF16),
            pltpu.VMEM(op_hi_rows.shape, BF16),
            pltpu.VMEM((2 * boxes + 2 * par_far.shape[0], 2 * LANE), jnp.int32),
            pltpu.VMEM((type_pad * 2 * width_lo // LANE, LANE), F32),
            pltpu.VMEM((type_pad * 16, LANE), F32),
            pltpu.VMEM((type_pad, 2 * width_lo), BF16),
            pltpu.VMEM((type_pad, 2 * share * LANE), BF16),
            pltpu.VMEM((parents * group * par_total, type_pad), BF16),
            pltpu.VMEM((boxes, slot_total, 2 * width_lo), BF16),
            pltpu.SemaphoreType.DMA((boxes // 4,)),
            pltpu.SemaphoreType.DMA((6,)),
        ],
        compiler_params=pltpu.CompilerParams(
            vmem_limit_bytes=(20 if slot_total <= 128 else 46) * MIB
        ),
        cost_estimate=pl.CostEstimate(flops=10**9, bytes_accessed=16 * MIB, transcendentals=0),
    )(
        *(
            in_hbm(x)
            for x in (
                distant_pattern_slot,
                far_type,
                par_far,
                par_type,
                op_lo_rows,
                op_hi_rows,
            )
        )
    )
    mine, theirs = pl.pallas_call(
        functools.partial(parent_kernel, lo_lines),
        out_shape=(jax.ShapeDtypeStruct((hi_lines, LANE), F32),) * 2,
        in_specs=[VMEM_SPEC] * 2,
        out_specs=(VMEM_SPEC,) * 2,
        scratch_shapes=[pltpu.VMEM((devices * hi_lines, LANE), F32)],
        compiler_params=pltpu.CompilerParams(vmem_limit_bytes=8 * MIB),
        cost_estimate=pl.CostEstimate(flops=10**8, bytes_accessed=MIB, transcendentals=0),
    )(arrived, in_vmem(d_hi))
    theirs, d_lo = lax.optimization_barrier((theirs, d_lo))
    other = exchanged(theirs, both, 0)
    incoming = pl.pallas_call(
        leaf_kernel,
        out_shape=jax.ShapeDtypeStruct((2 * boxes, width_lo // LANE, LANE), F32),
        in_specs=[HBM_SPEC, VMEM_SPEC],
        out_specs=VMEM_SPEC,
        scratch_shapes=[
            pltpu.VMEM((boxes, slot_total, 2 * width_lo), BF16),
            pltpu.VMEM((devices * lo_lines, LANE), F32),
            pltpu.VMEM((slot_total, 2 * width_lo), F32),
            pltpu.SemaphoreType.DMA((boxes // 2,)),
        ],
        compiler_params=pltpu.CompilerParams(
            vmem_limit_bytes=(10 if slot_total <= 128 else 32) * MIB
        ),
        cost_estimate=pl.CostEstimate(flops=10**9, bytes_accessed=5 * MIB, transcendentals=0),
    )(in_hbm(d_lo), arrived)
    field = pl.pallas_call(
        last_kernel,
        out_shape=jax.ShapeDtypeStruct((2 * boxes, panels), F32),
        in_specs=[VMEM_SPEC] * 3 + [HBM_SPEC] * 3 + [VMEM_SPEC],
        out_specs=VMEM_SPEC,
        scratch_shapes=[
            pltpu.VMEM(receive.shape, BF16),
            pltpu.VMEM(shift_rows.shape, F32),
            pltpu.VMEM(interp_matrix.shape, BF16),
            pltpu.VMEM((group, hi_lines, LANE), F32),
            pltpu.VMEM((2 * boxes, width_hi), BF16),
            pltpu.VMEM((2 * boxes, 2 * width_lo // LANE, LANE), F32),
            pltpu.SemaphoreType.DMA((boxes // 4,)),
            pltpu.SemaphoreType.DMA((2,)),
        ],
        compiler_params=pltpu.CompilerParams(vmem_limit_bytes=12 * MIB),
        cost_estimate=pl.CostEstimate(flops=10**9, bytes_accessed=8 * MIB, transcendentals=0),
    )(
        mine,
        other,
        incoming,
        shift_rows,
        interp_matrix,
        in_hbm(receive),
        near,
    )
    return field.reshape(boxes, 2, panels)


def solution(mesh):
    both = ("box", "samp")
    return jax.shard_map(
        on_device,
        mesh=mesh,
        in_specs=(
            P(both, None, None),
            P(both, None, None),
            P(both, None, None),
            P(both, None, None, None),
            P(both, None),
            P(both, None),
            P(both, None, None),
            P(both, None),
            P(both, None),
            P(),
            P(),
            P(),
            P("box", None),
            P("box", None),
            P(),
        ),
        out_specs=P(both, None, None),
        check_vma=False,
    )
```

```python
import functools

import jax
import jax.numpy as jnp
from jax import lax
from jax.experimental import pallas as pl
from jax.experimental.pallas import tpu as pltpu
from jax.sharding import PartitionSpec as P

F32 = jnp.float32
BF16 = jnp.bfloat16
LANE = 128
VMEM_SPEC = pl.BlockSpec(memory_space=pltpu.VMEM)
SMEM_SPEC = pl.BlockSpec(memory_space=pltpu.SMEM)
ANY_SPEC = pl.BlockSpec(memory_space=pl.ANY)
HBM_SPEC = pl.BlockSpec(memory_space=pltpu.HBM)
MIB = 1 << 20


def iota(shape, dim):
    return lax.broadcasted_iota(jnp.int32, shape, dim)


def dot_nn(lhs, rhs):
    return lax.dot_general(lhs, rhs, (((1,), (0,)), ((), ())), preferred_element_type=F32)


def dot_nt(lhs, rhs):
    return lax.dot_general(lhs, rhs, (((1,), (1,)), ((), ())), preferred_element_type=F32)


def exchanged(value, axes, first):
    count = lax.axis_size(axes)
    pairs = []
    for low in range(first, count - 1, 2):
        pairs += [(low, low + 1), (low + 1, low)]
    return lax.ppermute(value, axes, pairs)


def fetch(pairs, sems, first=0):
    copies = []
    for k, (source, target) in enumerate(pairs):
        copies.append(pltpu.make_async_copy(source, target, sems.at[first + k]))
        copies[-1].start()
    return copies


def radiate_kernel(
    group,
    dens_hbm,
    radiate_ref,
    send_hbm,
    interp_hbm,
    shift_hbm,
    out_ref,
    rad,
    dens_ref,
    send_ref,
    interp_ref,
    shift_ref,
    summed,
    table,
    parent,
    sems,
    extra,
):
    boxes = rad.shape[0]
    width = rad.shape[2] // 2
    per_step = 4
    steps = boxes // per_step
    others = fetch(
        [(dens_hbm, dens_ref), (send_hbm, send_ref), (shift_hbm, shift_ref)], extra
    )
    copies = []
    for step in range(steps):
        part = pl.ds(step * per_step, per_step)
        copies.append(pltpu.make_async_copy(radiate_ref.at[part], rad.at[part], sems.at[step]))
        copies[-1].start()
    others += fetch([(interp_hbm, interp_ref)], extra, 3)
    others[0].wait()
    dens = dens_ref[...].astype(F32)
    owner = (iota(dens.shape, 0) // 2) % per_step
    blocks = jnp.concatenate([jnp.where(owner == b, dens, 0.0) for b in range(per_step)], 1)
    for step in range(steps):
        copies[step].wait()
        rows = slice(step * 2 * per_step, (step + 1) * 2 * per_step)
        weights = rad[step * per_step : (step + 1) * per_step].reshape(per_step * LANE, 2 * width)
        summed[rows] = dot_nn(blocks[rows].astype(BF16), weights).reshape(
            2 * per_step, 2 * width // LANE, LANE
        )
    chunks = width // LANE
    re_chunks, im_chunks = [], []
    for r in range(chunks):
        first_lo = summed[pl.ds(0, boxes, stride=2), r, :]
        first_hi = summed[pl.ds(0, boxes, stride=2), chunks + r, :]
        second_lo = summed[pl.ds(1, boxes, stride=2), r, :]
        second_hi = summed[pl.ds(1, boxes, stride=2), chunks + r, :]
        re_chunks.append((first_lo - second_hi).astype(BF16))
        im_chunks.append((first_hi + second_lo).astype(BF16))
    re_part = jnp.concatenate(re_chunks, 1)
    im_part = jnp.concatenate(im_chunks, 1)
    for r in range(chunks):
        table[pl.ds(r, boxes, stride=8), :] = re_chunks[r].astype(F32)
        table[pl.ds(chunks + r, boxes, stride=8), :] = im_chunks[r].astype(F32)
    table[pl.ds(boxes * 8, 8), :] = jnp.zeros((8, LANE), F32)
    for copy in others[1:]:
        copy.wait()
    wide = dot_nn(jnp.concatenate([re_part, im_part], 0), interp_ref[...])
    hi_chunks = wide.shape[1] // LANE
    parents = boxes // 8
    share = hi_chunks // group
    for r in range(hi_chunks):
        cols = slice(r * LANE, (r + 1) * LANE)
        s_re = shift_ref[pl.ds(2 * r, 8, stride=2 * hi_chunks), :]
        s_im = shift_ref[pl.ds(2 * r + 1, 8, stride=2 * hi_chunks), :]
        for p in range(parents):
            w_re = wide[p * 8 : (p + 1) * 8, cols]
            w_im = wide[boxes + p * 8 : boxes + (p + 1) * 8, cols]
            row = ((r // share) * parents + p) * 2 * share + r % share
            parent[row : row + 1] = jnp.sum(w_re * s_re - w_im * s_im, 0, keepdims=True)
            row += share
            parent[row : row + 1] = jnp.sum(w_re * s_im + w_im * s_re, 0, keepdims=True)
    slots, devices = send_ref.shape
    hi_rows = parents * 2 * share

    def fill(d, carry):
        for k in range(slots // 2):
            pair = [
                table[pl.ds(pl.multiple_of(send_ref[2 * k + h, d] * 8, 8), 8), :] for h in range(2)
            ]
            out_ref[d, 16 * k : 16 * (k + 1)] = jnp.concatenate(pair, 0).astype(BF16)
        member = pl.multiple_of(lax.rem(d, group) * hi_rows, 8)
        out_ref[d, 8 * slots : 8 * slots + hi_rows] = parent[pl.ds(member, hi_rows)].astype(BF16)
        return carry

    lax.fori_loop(0, devices, fill, 0, unroll=4)


def tally(index, source_row, type_row, sources, types):
    source = index[pl.ds(source_row, 1), :]
    kind = index[pl.ds(type_row, 1), :]
    faces = index.shape[1]
    by_source = jnp.where(iota((sources, faces), 0) == source, 1.0, 0.0).astype(BF16)
    by_type = jnp.where(iota((types, faces), 0) == kind, 1.0, 0.0).astype(BF16)
    return dot_nt(by_source, by_type).astype(BF16)


def index_kernel(
    types,
    group,
    slot_hbm,
    type_hbm,
    par_far_hbm,
    par_type_hbm,
    op_lo_hbm,
    op_hi_hbm,
    d_lo_hbm,
    d_ref,
    slot_ref,
    type_ref,
    par_far_ref,
    par_type_ref,
    op_lo_ref,
    op_hi_ref,
    index,
    wide_lo,
    wide_hi,
    op_lo,
    op_hi,
    counts_hi,
    d_lo,
    sems,
    extra,
):
    others = fetch(
        [
            (op_lo_hbm, op_lo_ref),
            (slot_hbm, slot_ref),
            (type_hbm, type_ref),
            (par_far_hbm, par_far_ref),
            (par_type_hbm, par_type_ref),
            (op_hi_hbm, op_hi_ref),
        ],
        extra,
    )
    boxes = slot_ref.shape[0]
    rows, far = par_far_ref.shape
    parents, sources, _ = d_ref.shape
    slot_total = d_lo.shape[1]
    type_pad = op_hi.shape[0]
    chunks = op_lo.shape[1] // (2 * LANE)
    lines = op_hi_ref.shape[0] // types
    share = lines // (2 * group)
    samp = lax.axis_index("samp")
    member = lax.rem(samp, group)
    first_parent = 2 * boxes + (samp - member) * (parents // group)
    place = member * (2 * share)
    base = place // 16 * 16
    index[...] = jnp.full(index.shape, -1, jnp.int32)
    tail = (type_pad - types) * 2 * chunks
    wide_lo[types * 2 * chunks : type_pad * 2 * chunks] = jnp.zeros((tail, LANE), F32)
    wide_hi[types * 16 : type_pad * 16] = jnp.zeros(((type_pad - types) * 16, LANE), F32)
    for copy in others[:5]:
        copy.wait()

    index[0:boxes, 0:far] = slot_ref[...]
    index[boxes : 2 * boxes, 0:far] = type_ref[...]
    index[2 * boxes : 2 * boxes + rows, 0:far] = par_far_ref[...]
    index[2 * boxes + rows : 2 * boxes + 2 * rows, 0:far] = par_type_ref[...]
    batch = 4
    share_parents = parents * batch // boxes

    wide_lo[0 : types * 2 * chunks] = op_lo_ref[...].astype(F32)
    for c in range(2):
        for r in range(chunks):
            col = (c * chunks + r) * LANE
            op_lo[:, col : col + LANE] = wide_lo[
                pl.ds(2 * r + c, type_pad, stride=2 * chunks), :
            ].astype(BF16)

    def lo_copy(step):
        part = pl.ds(step * batch, batch)
        return pltpu.make_async_copy(d_lo.at[part], d_lo_hbm.at[part], sems.at[step])

    def step_lists(step, carry):
        counts = []
        for k in range(batch):
            g = step * batch + k
            counts.append(tally(index, g, boxes + g, slot_total, type_pad))
        counts = jnp.concatenate(counts, 0)
        part = 2 * chunks * LANE // batch
        for k in range(batch):
            cols = slice(k * part, (k + 1) * part)
            d_lo[pl.ds(step * batch, batch), :, cols] = (
                dot_nn(counts, op_lo[:, cols]).astype(BF16).reshape(batch, slot_total, part)
            )
            if k < share_parents:
                p = step * share_parents + k
                at = pl.ds(pl.multiple_of(p * sources, sources), sources)
                row = first_parent + p
                counts_hi[at] = tally(index, row, rows + row, sources, type_pad)
        lo_copy(step).start()
        return carry

    lax.fori_loop(0, boxes // batch, step_lists, 0)
    others[5].wait()

    def widen(t, carry):
        source = pl.ds(pl.multiple_of(t * lines + base, 16), 16)
        wide_hi[pl.ds(pl.multiple_of(t * 16, 16), 16)] = op_hi_ref[source].astype(F32)
        return carry

    lax.fori_loop(0, types, widen, 0, unroll=4)
    for c in range(2):
        for k in range(share):
            col = (c * share + k) * LANE
            start = place - base + 2 * k + c
            op_hi[:, col : col + LANE] = wide_hi[pl.ds(start, type_pad, stride=16), :].astype(BF16)

    for first in range(0, 2 * share * LANE, 2 * LANE):
        cols = slice(first, first + 2 * LANE)
        d_ref[:, :, cols] = (
            dot_nn(counts_hi[...], op_hi[:, cols]).astype(BF16).reshape(parents, sources, 2 * LANE)
        )
    for step in range(boxes // batch):
        lo_copy(step).wait()


def parent_kernel(lo_lines, arrived_ref, d_ref, mine_ref, theirs_ref, wide):
    parents, sources, width = d_ref.shape
    share = width // (2 * LANE)
    own = parents // 2
    member = lax.rem(lax.axis_index("samp"), 2)
    wide[...] = arrived_ref[:, lo_lines:, :].astype(F32).reshape(wide.shape)
    for k in range(share):
        first = wide[pl.ds(k, sources, stride=2 * share), :]
        second = wide[pl.ds(share + k, sources, stride=2 * share), :]
        for out_ref, start in ((theirs_ref, (1 - member) * own), (mine_ref, member * own)):
            for q in range(own):
                o_re = d_ref[start + q, :, k * LANE : (k + 1) * LANE].astype(F32)
                o_im = d_ref[start + q, :, (share + k) * LANE : (share + k + 1) * LANE].astype(F32)
                row = q * 2 * share + k
                out_ref[row : row + 1] = jnp.sum(o_re * first - o_im * second, 0, keepdims=True)
                row += share
                out_ref[row : row + 1] = jnp.sum(o_re * second + o_im * first, 0, keepdims=True)


def near_kernel(
    box_total,
    even_ref,
    dens_hbm,
    odd_ref,
    near_src_hbm,
    near_tile_hbm,
    tiles_hbm,
    near_ref,
    tiles,
    halo,
    near_src_ref,
    near_tile_ref,
    dens3,
    left,
    right,
    acc,
    code,
    sems,
    extra,
):
    boxes, near = near_src_ref.shape
    tile_count = tiles.shape[0]
    steps = sems.shape[0]
    per_step = tile_count // steps
    samp = lax.axis_index("samp")
    position = lax.axis_index("box") * lax.axis_size("samp") + samp
    odd = lax.rem(samp, 2)
    others = fetch(
        [
            (near_src_hbm, near_src_ref),
            (near_tile_hbm, near_tile_ref),
            (even_ref, halo.at[2 - 2 * odd]),
            (dens_hbm, halo.at[1]),
            (odd_ref, halo.at[2 * odd]),
        ],
        extra,
    )

    def tile_copy(step):
        part = pl.ds(step * per_step, per_step)
        return pltpu.make_async_copy(tiles_hbm.at[part], tiles.at[part], sems.at[step])

    for step in range(steps):
        tile_copy(step).start()
    acc[...] = jnp.zeros(acc.shape, F32)
    left[...] = jnp.zeros(left.shape, F32)
    right[...] = jnp.zeros(right.shape, F32)
    for copy in others:
        copy.wait()
    for k in range(3):
        dens3[pl.ds(2 * boxes * k, 2 * boxes), :] = halo[k].astype(F32)
    first = dens3[pl.ds(0, 3 * boxes, stride=2), :]
    second = dens3[pl.ds(1, 3 * boxes, stride=2), :]
    left[pl.ds(0, 3 * boxes, stride=8), :] = first
    left[pl.ds(1, 3 * boxes, stride=8), :] = second
    right[pl.ds(0, 3 * boxes, stride=8), :] = -second
    right[pl.ds(1, 3 * boxes, stride=8), :] = first


    def locate(g, carry):
        for n in range(near):
            source = near_src_ref[g, n]
            live = source < box_total
            tile = jnp.where(live, near_tile_ref[g, n] - position * tile_count, tile_count)
            code[tile] = g * 64 + source - (position - 1) * boxes
        return carry

    lax.fori_loop(0, boxes, locate, 0)

    def multiply_pair(tile):
        both = tiles[pl.ds(tile, 2)]
        weights = jnp.concatenate(
            [both[:, 0].reshape(2 * LANE, LANE), both[:, 1].reshape(2 * LANE, LANE)], 1
        )
        owners, lefts, rights = [], [], []
        for h in range(2):
            entry = code[tile + h]
            row = pl.ds(pl.multiple_of((entry & 63) * 8, 8), 8)
            owners.append(entry >> 6)
            lefts.append(left[row])
            rights.append(right[row])
        lhs = jnp.concatenate([jnp.concatenate(lefts, 0), jnp.concatenate(rights, 0)], 1)
        product = dot_nt(lhs.astype(BF16), weights)
        for h in range(2):
            acc[owners[h]] = (
                acc[owners[h]] + product[8 * h : 8 * (h + 1), h * LANE : (h + 1) * LANE]
            )


    def step_tiles(step, carry):
        tile_copy(step).wait()
        for pair in range(per_step // 2):
            multiply_pair(step * per_step + 2 * pair)
        return carry

    lax.fori_loop(0, steps, step_tiles, 0)
    for g in range(boxes):
        row = 2 * g
        near_ref[row : row + 2] = acc[g, 0:2] + 0.5 * dens3[pl.ds(2 * boxes + row, 2), :]


def leaf_kernel(d_lo_hbm, arrived_ref, incoming_ref, d_lo, slots, received, sems):
    boxes, slot_total, width = d_lo.shape
    chunks = width // (2 * LANE)
    steps = sems.shape[0]
    per_boxes = boxes // steps
    copies = []
    for step in range(steps):
        part = pl.ds(step * per_boxes, per_boxes)
        copies.append(pltpu.make_async_copy(d_lo_hbm.at[part], d_lo.at[part], sems.at[step]))
        copies[-1].start()
    lo_lines = slots.shape[0] // arrived_ref.shape[0]
    slots[...] = arrived_ref[:, :lo_lines, :].astype(F32).reshape(slots.shape)
    for r in range(2 * chunks):
        received[:, r * LANE : (r + 1) * LANE] = slots[pl.ds(r, slot_total, stride=2 * chunks), :]

    def multiply_slots(r, g):
        first = received[:, r * LANE : (r + 1) * LANE]
        second = received[:, (chunks + r) * LANE : (chunks + r + 1) * LANE]
        o_re = d_lo[g, :, r * LANE : (r + 1) * LANE].astype(F32)
        o_im = d_lo[g, :, (chunks + r) * LANE : (chunks + r + 1) * LANE].astype(F32)
        incoming_ref[g, r : r + 1] = jnp.sum(
            o_re * first - o_im * second, 0, keepdims=True
        )
        incoming_ref[boxes + g, r : r + 1] = jnp.sum(
            o_re * second + o_im * first, 0, keepdims=True
        )

    for step in range(steps):
        copies[step].wait()
        for r in range(chunks):
            for k in range(per_boxes):
                multiply_slots(r, step * per_boxes + k)


def last_kernel(
    mine_ref,
    other_ref,
    incoming_ref,
    shift_hbm,
    interp_hbm,
    receive_ref,
    near_ref,
    out_ref,
    receive,
    shift_ref,
    interp_ref,
    parent_ref,
    down,
    blend,
    sems,
    extra,
):
    boxes = receive.shape[0]
    per_step = 4
    steps = boxes // per_step
    others = fetch([(shift_hbm, shift_ref), (interp_hbm, interp_ref)], extra)
    copies = []
    for step in range(steps):
        part = pl.ds(step * per_step, per_step)
        copies.append(pltpu.make_async_copy(receive_ref.at[part], receive.at[part], sems.at[step]))
        copies[-1].start()
    member = lax.rem(lax.axis_index("samp"), 2)
    parent_ref[member] = mine_ref[...]
    parent_ref[1 - member] = other_ref[...]
    own_parents = boxes // 8
    hi_chunks = down.shape[1] // LANE
    chunks = incoming_ref.shape[1]
    share = hi_chunks // parent_ref.shape[0]
    others[0].wait()
    for r in range(hi_chunks):
        s_re = shift_ref[pl.ds(2 * r, 8, stride=2 * hi_chunks), :]
        s_im = shift_ref[pl.ds(2 * r + 1, 8, stride=2 * hi_chunks), :]
        re_rows, im_rows = [], []
        for p in range(own_parents):
            row = p * 2 * share + r % share
            t_re = parent_ref[r // share, row : row + 1]
            t_im = parent_ref[r // share, row + share : row + share + 1]
            re_rows.append(s_re * t_re + s_im * t_im)
            im_rows.append(s_re * t_im - s_im * t_re)
        cols = slice(r * LANE, (r + 1) * LANE)
        down[:, cols] = jnp.concatenate(re_rows + im_rows, 0).astype(BF16)
    others[1].wait()
    total = jnp.concatenate([incoming_ref[:, r, :] for r in range(chunks)], 1)
    total = total + dot_nt(down[...], interp_ref[...])
    total = total.astype(BF16).astype(F32)
    for r in range(chunks):
        re_part = total[:boxes, r * LANE : (r + 1) * LANE]
        im_part = total[boxes:, r * LANE : (r + 1) * LANE]
        blend[pl.ds(0, boxes, stride=2), r, :] = re_part
        blend[pl.ds(1, boxes, stride=2), r, :] = im_part
        blend[pl.ds(0, boxes, stride=2), chunks + r, :] = -im_part
        blend[pl.ds(1, boxes, stride=2), chunks + r, :] = re_part
    owner = (iota((2 * per_step, LANE), 0) // 2) % per_step
    for step in range(steps):
        rows = slice(step * 2 * per_step, (step + 1) * 2 * per_step)
        lhs = jnp.concatenate([blend[rows, r, :] for r in range(2 * chunks)], 1).astype(BF16)
        copies[step].wait()
        weights = receive[step * per_step : (step + 1) * per_step]
        product = dot_nt(lhs, weights.reshape(per_step * LANE, 2 * chunks * LANE))
        total = near_ref[rows]
        for b in range(per_step):
            total = total + jnp.where(owner == b, product[:, b * LANE : (b + 1) * LANE], 0.0)
        out_ref[rows] = total


def in_hbm(array):
    return pltpu.with_memory_space_constraint(array, pltpu.HBM)


def in_vmem(array):
    return pltpu.with_memory_space_constraint(array, pltpu.VMEM)


def tiled_rows(array):
    count, parts, width = array.shape
    cut = array.reshape(count, parts, width // LANE, LANE)
    return cut.transpose(0, 2, 1, 3).reshape(-1, LANE)


def on_device(
    density,
    radiate,
    receive,
    near_tiles,
    near_src,
    near_tile,
    send_box,
    distant_pattern_slot,
    far_type,
    trans_lo,
    interp_matrix,
    shifts,
    par_far,
    par_type,
    trans_hi,
):
    boxes, _, panels = density.shape
    devices = lax.axis_size("box") * lax.axis_size("samp")
    slots = send_box.shape[2]
    types, _, width_lo = trans_lo.shape
    width_hi = trans_hi.shape[2]
    parents = boxes // 8
    slot_total = devices * slots
    par_total = devices * parents
    type_pad = -(-types // 8) * 8
    group = 2
    share = width_hi // LANE // group
    lo_lines = slots * 2 * width_lo // LANE
    hi_lines = parents * 2 * share
    lines = lo_lines + hi_lines
    rows = density.reshape(boxes * 2, panels)
    shift_rows = tiled_rows(shifts)
    send = send_box[0].T
    outgoing = pl.pallas_call(
        functools.partial(radiate_kernel, group),
        out_shape=jax.ShapeDtypeStruct((devices, lines, LANE), BF16),
        in_specs=[HBM_SPEC] * 5,
        out_specs=VMEM_SPEC,
        scratch_shapes=[
            pltpu.VMEM(radiate.shape, BF16),
            pltpu.VMEM(rows.shape, BF16),
            pltpu.SMEM(send.shape, jnp.int32),
            pltpu.VMEM(interp_matrix.shape, BF16),
            pltpu.VMEM(shift_rows.shape, F32),
            pltpu.VMEM((2 * boxes, 2 * width_lo // LANE, LANE), F32),
            pltpu.VMEM((boxes * 8 + 8, LANE), F32),
            pltpu.VMEM((parents * 2 * width_hi // LANE, LANE), F32),
            pltpu.SemaphoreType.DMA((boxes // 4,)),
            pltpu.SemaphoreType.DMA((4,)),
        ],
        compiler_params=pltpu.CompilerParams(vmem_limit_bytes=12 * MIB),
        cost_estimate=pl.CostEstimate(flops=10**9, bytes_accessed=8 * MIB, transcendentals=0),
    )(*(in_hbm(x) for x in (rows, radiate, send, interp_matrix, shift_rows)))
    both = ("box", "samp")
    even = exchanged(rows, both, 0)
    odd = exchanged(rows, both, 1)
    outgoing, even, odd = lax.optimization_barrier((outgoing, even, odd))
    arrived = lax.all_to_all(outgoing, ("box", "samp"), split_axis=0, concat_axis=0, tiled=True)
    tile_count = near_tiles.shape[0]
    far = far_type.shape
    op_hi_rows = tiled_rows(trans_hi)
    op_lo_rows = tiled_rows(trans_lo)
    steps = 8
    near = pl.pallas_call(
        functools.partial(near_kernel, boxes * devices),
        out_shape=jax.ShapeDtypeStruct((2 * boxes, panels), F32),
        in_specs=[ANY_SPEC, HBM_SPEC, ANY_SPEC] + [HBM_SPEC] * 3,
        out_specs=VMEM_SPEC,
        scratch_shapes=[
            pltpu.VMEM(near_tiles.shape, BF16),
            pltpu.VMEM((3, 2 * boxes, panels), BF16),
            pltpu.SMEM(near_src.shape, jnp.int32),
            pltpu.SMEM(near_src.shape, jnp.int32),
            pltpu.VMEM((6 * boxes, panels), F32),
            pltpu.VMEM((3 * boxes * 8, LANE), F32),
            pltpu.VMEM((3 * boxes * 8, LANE), F32),
            pltpu.VMEM((boxes, 8, LANE), F32),
            pltpu.SMEM((tile_count + 8,), jnp.int32),
            pltpu.SemaphoreType.DMA((steps,)),
            pltpu.SemaphoreType.DMA((5,)),
        ],
        compiler_params=pltpu.CompilerParams(vmem_limit_bytes=20 * MIB),
        cost_estimate=pl.CostEstimate(flops=10**10, bytes_accessed=16 * MIB, transcendentals=0),
    )(even, in_hbm(rows), odd, in_hbm(near_src), in_hbm(near_tile), in_hbm(near_tiles))
    near, far_type = lax.optimization_barrier((near, far_type))
    d_lo, d_hi = pl.pallas_call(
        functools.partial(index_kernel, types, group),
        out_shape=(
            pltpu.HBM((boxes, slot_total, 2 * width_lo), BF16),
            pltpu.VMEM((parents * group, par_total, 2 * share * LANE), BF16),
        ),
        in_specs=[HBM_SPEC] * 6,
        out_specs=(HBM_SPEC, VMEM_SPEC),
        scratch_shapes=[
            pltpu.VMEM(far, jnp.int32),
            pltpu.VMEM(far, jnp.int32),
            pltpu.VMEM(par_far.shape, jnp.int32),
            pltpu.VMEM(par_far.shape, jnp.int32),
            pltpu.VMEM(op_lo_rows.shape, BF16),
            pltpu.VMEM(op_hi_rows.shape, BF16),
            pltpu.VMEM((2 * boxes + 2 * par_far.shape[0], 2 * LANE), jnp.int32),
            pltpu.VMEM((type_pad * 2 * width_lo // LANE, LANE), F32),
            pltpu.VMEM((type_pad * 16, LANE), F32),
            pltpu.VMEM((type_pad, 2 * width_lo), BF16),
            pltpu.VMEM((type_pad, 2 * share * LANE), BF16),
            pltpu.VMEM((parents * group * par_total, type_pad), BF16),
            pltpu.VMEM((boxes, slot_total, 2 * width_lo), BF16),
            pltpu.SemaphoreType.DMA((boxes // 4,)),
            pltpu.SemaphoreType.DMA((6,)),
        ],
        compiler_params=pltpu.CompilerParams(
            vmem_limit_bytes=(20 if slot_total <= 128 else 46) * MIB
        ),
        cost_estimate=pl.CostEstimate(flops=10**9, bytes_accessed=16 * MIB, transcendentals=0),
    )(
        *(
            in_hbm(x)
            for x in (
                distant_pattern_slot,
                far_type,
                par_far,
                par_type,
                op_lo_rows,
                op_hi_rows,
            )
        )
    )
    mine, theirs = pl.pallas_call(
        functools.partial(parent_kernel, lo_lines),
        out_shape=(jax.ShapeDtypeStruct((hi_lines, LANE), F32),) * 2,
        in_specs=[VMEM_SPEC] * 2,
        out_specs=(VMEM_SPEC,) * 2,
        scratch_shapes=[pltpu.VMEM((devices * hi_lines, LANE), F32)],
        compiler_params=pltpu.CompilerParams(vmem_limit_bytes=8 * MIB),
        cost_estimate=pl.CostEstimate(flops=10**8, bytes_accessed=MIB, transcendentals=0),
    )(arrived, in_vmem(d_hi))
    theirs, d_lo, late_interp, late_shift = lax.optimization_barrier(
        (theirs, d_lo, interp_matrix, shift_rows)
    )
    other = exchanged(theirs, both, 0)
    incoming = pl.pallas_call(
        leaf_kernel,
        out_shape=jax.ShapeDtypeStruct((2 * boxes, width_lo // LANE, LANE), F32),
        in_specs=[HBM_SPEC, VMEM_SPEC],
        out_specs=VMEM_SPEC,
        scratch_shapes=[
            pltpu.VMEM((boxes, slot_total, 2 * width_lo), BF16),
            pltpu.VMEM((devices * lo_lines, LANE), F32),
            pltpu.VMEM((slot_total, 2 * width_lo), F32),
            pltpu.SemaphoreType.DMA((boxes // 2,)),
        ],
        compiler_params=pltpu.CompilerParams(
            vmem_limit_bytes=(10 if slot_total <= 128 else 32) * MIB
        ),
        cost_estimate=pl.CostEstimate(flops=10**9, bytes_accessed=5 * MIB, transcendentals=0),
    )(in_hbm(d_lo), arrived)
    field = pl.pallas_call(
        last_kernel,
        out_shape=jax.ShapeDtypeStruct((2 * boxes, panels), F32),
        in_specs=[VMEM_SPEC] * 3 + [HBM_SPEC] * 3 + [VMEM_SPEC],
        out_specs=VMEM_SPEC,
        scratch_shapes=[
            pltpu.VMEM(receive.shape, BF16),
            pltpu.VMEM(shift_rows.shape, F32),
            pltpu.VMEM(interp_matrix.shape, BF16),
            pltpu.VMEM((group, hi_lines, LANE), F32),
            pltpu.VMEM((2 * boxes, width_hi), BF16),
            pltpu.VMEM((2 * boxes, 2 * width_lo // LANE, LANE), F32),
            pltpu.SemaphoreType.DMA((boxes // 4,)),
            pltpu.SemaphoreType.DMA((2,)),
        ],
        compiler_params=pltpu.CompilerParams(vmem_limit_bytes=12 * MIB),
        cost_estimate=pl.CostEstimate(flops=10**9, bytes_accessed=8 * MIB, transcendentals=0),
    )(
        mine,
        other,
        incoming,
        late_shift,
        late_interp,
        in_hbm(receive),
        near,
    )
    return field.reshape(boxes, 2, panels)


def solution(mesh):
    both = ("box", "samp")
    return jax.shard_map(
        on_device,
        mesh=mesh,
        in_specs=(
            P(both, None, None),
            P(both, None, None),
            P(both, None, None),
            P(both, None, None, None),
            P(both, None),
            P(both, None),
            P(both, None, None),
            P(both, None),
            P(both, None),
            P(),
            P(),
            P(),
            P("box", None),
            P("box", None),
            P(),
        ),
        out_specs=P(both, None, None),
        check_vma=False,
    )
```
